256 devices in a mesh: dp: 2 (over core), row: 8 (over z_lo, x), col: 16 (over z_hi, y).
Axes of the slice: x: 4, y: 4, z: 8 (z_hi: 4, z_lo: 2; z = z_hi * 2 + z_lo), core: 2. Of those that a mesh axis runs over, the one named last changes fastest.
Arguments:
- stream: bfloat16 [2048, 8192], P(('dp', 'row'), 'col'), may hold values from -96 to 96
- hidden: bfloat16 [2048, 29568], P(('dp', 'col'), 'row'), may hold values from -4 to 4
- w_down: bfloat16 [29568, 8192], P('row', 'col'), may hold values from -0.03125 to 0.03125
- norm_gain: float32 [8192], P('col'), may hold values from 0.5 to 1.5
- value_head: float32 [8192], P('col'), may hold values from -0.00048828125 to 0.00048828125
- value_bias: float32 [1], replicated, may hold values from -1 to 1
- rewards: float32 [2, 1024], P('dp', 'row'), may hold values from -16 to 16
- segments: int32 [2, 1024], P('dp', 'row'), may hold values from 0 to 5, never falling along the last dimension, each value on 1 to 512 neighbouring positions
Outputs:
- weight_grad: bfloat16 [29568, 8192], P('row', 'col')
- hidden_grad: bfloat16 [2048, 29568], P(('dp', 'col'), 'row')
- stream_grad: bfloat16 [2048, 8192], P(('dp', 'row'), 'col')
The draws below stay inside these ranges and needn't reach their ends.
All inputs are finite; a program needn't handle non-finite values.
Results may differ from the reference program's by a relative error of at most 0.02.
Values may be sent and summed in bfloat16 or wider, within the bound.
No kernel may reach another device: no remote copies, remote signals or barrier semaphores. Data moves between devices by JAX's collectives and lax.ppermute only.
A program may use at most 128 MiB of HBM per device.

```python
import math
import jax
import jax.numpy as jnp
import numpy as np
from jax import lax

D = 8192
FF = 29568
SEQS = 6
TOK_REP = 1024
TOKENS = 2048
N_DP = 2
N_COL = 16


def common_direction(key):
    return jax.random.uniform(key, (D,), jnp.float32, -1.0, 1.0)


def draw_value_head(key, part):
    direction = common_direction(key)
    return 4.0 * direction / D


def draw_stream(key, part):
    direction = common_direction(key)
    key = jax.random.fold_in(key, 11)
    keys = jax.random.split(key, 6)
    row_scale = jnp.exp(jax.random.uniform(keys[0], (TOKENS, 1), jnp.float32, 0.0, math.log(10.0)))
    col_scale = jnp.exp(jax.random.uniform(keys[1], (1, D), jnp.float32, math.log(0.5), math.log(2.0)))
    sign = jnp.where(jax.random.bernoulli(keys[4], 0.5, (TOKENS, 1)), 1.0, -1.0)
    strength = sign * jax.random.uniform(keys[5], (TOKENS, 1), jnp.float32, 0.6, 1.4)
    aligned = 0.6 * strength * direction[None, :]
    base = jax.random.truncated_normal(keys[2], -4.0, 4.0, (TOKENS, D), jnp.float32)
    return ((base * col_scale + aligned) * row_scale).astype(jnp.bfloat16)


def draw_rewards(key, part):
    key = jax.random.fold_in(key, 23)
    place = jnp.arange(TOK_REP, dtype=jnp.float32)[None, :] / TOK_REP
    base = jax.random.truncated_normal(key, -4.0, 4.0, (N_DP, TOK_REP), jnp.float32)
    return base * (1.0 + 2.0 * place)


def levels(own_key, dims, cuts, smallest, largest):
    def one(dim, parts):
        draws = jax.random.uniform(jax.random.fold_in(jax.random.fold_in(own_key, 6), dim), (parts,), jnp.float32, smallest / len(cuts), largest / len(cuts))
        return jnp.repeat(jnp.exp(draws), dims[dim] // parts).reshape((-1,) + (1,) * (len(dims) - dim - 1))

    loudness = one(*cuts[0])
    for cut in cuts[1:]:
        loudness = loudness * one(*cut)
    return loudness


def length_profile(count, total, bound, lean):
    portions = [(1 << 20) // math.isqrt(standing ** lean) + 1 for standing in range(2, count + 1)]
    spare, holding = total - bound - (count - 1), [1] * (count - 1)
    while spare > 0:
        movable = [i for i in range(count - 1) if holding[i] < bound]
        pool, left = sum([portions[i] for i in movable]), spare
        for i in movable:
            more = min(bound - holding[i], max(1, left * portions[i] // pool), spare)
            holding[i] = holding[i] + more
            spare = spare - more
    return np.array([bound] + holding)


def ragged_sizes(key, amount, total, most, skew):
    if amount == 2:
        one = jax.random.randint(key, (), max(1, total - most), min(most, total - 1) + 1)
        return jnp.stack([one, total - one])
    sizes = jnp.asarray(length_profile(amount, total, most, skew), jnp.int32)
    pairs = (amount - 1) // 2
    giver, taker = sizes[1:1 + 2 * pairs:2], sizes[2:2 + 2 * pairs:2]
    margin = jnp.minimum(giver - 1, most - taker)
    passed = jax.random.randint(jax.random.fold_in(key, 1), (pairs,), 0, 1 << 20) % (margin + 1)
    sizes = sizes.at[1:1 + 2 * pairs:2].set(giver - passed).at[2:2 + 2 * pairs:2].set(taker + passed)
    return sizes[jax.random.permutation(jax.random.fold_in(key, 2), amount)]


def normal_values(own_key, dims, deviation, most, pieces=(), held_as=jnp.bfloat16):
    level = levels(own_key, dims, pieces, -0.22, 0.18) if pieces else 1.0
    drawn = jax.random.normal(own_key, dims, jnp.float32) * deviation * level
    return jnp.minimum(jnp.maximum(drawn, -most), most).astype(held_as)


def setup_inputs(seed: int = 0) -> dict:
    arg_keys = jax.random.split(jax.random.key(seed), 9)
    return {
        "stream": draw_stream(jax.random.fold_in(arg_keys[8], 71), 0),
        "hidden": normal_values(arg_keys[1], (TOKENS, FF), 0.3, 4.0, ((0, 32), (1, 8))),
        "w_down": normal_values(arg_keys[2], (FF, D), FF ** -0.5, 0.03125, ((0, 8), (1, 16))),
        "norm_gain": jnp.clip(1.0 + 0.1 * jax.random.normal(arg_keys[3], (D,), jnp.float32), 0.5, 1.5),
        "value_head": draw_value_head(jax.random.fold_in(arg_keys[8], 71), 0),
        "value_bias": jnp.clip(jax.random.uniform(arg_keys[5], (1,), jnp.float32, -1.0, 1.0), -1.0, 1.0),
        "rewards": draw_rewards(jax.random.fold_in(arg_keys[8], 71), 0),
        "segments": jax.vmap(lambda own: jnp.searchsorted(jnp.cumsum(ragged_sizes(own, SEQS, TOK_REP, TOK_REP // 2, 0)), jnp.arange(TOK_REP), side="right"))(jax.random.split(arg_keys[7], N_DP)).reshape((N_DP, TOK_REP)).astype(jnp.int32),
    }


loss_scale = 2097152.0

def replica_returns(rows):
    reward_row, segment_row = rows
    place = jnp.arange(TOK_REP, dtype=jnp.int32)
    owed = (segment_row[None, :] == segment_row[:, None]) & (place[None, :] >= place[:, None])
    return jnp.dot(owed.astype(jnp.float32), reward_row, precision=lax.Precision.HIGHEST)

def reference(stream, hidden, w_down, norm_gain, value_head, value_bias, rewards, segments):
    y = stream.astype(jnp.float32)
    gw = norm_gain * value_head
    sq = lax.optimization_barrier(jnp.sum(y * y, axis=1))
    lin = lax.optimization_barrier(jnp.sum(y * gw[None, :], axis=1))
    rms = jnp.sqrt(sq / D + 1e-05)
    value = lin / rms + value_bias[0]
    returns = lax.map(replica_returns, (rewards, segments)).reshape(TOKENS)
    mean = jnp.sum(returns) / TOKENS
    spread = jnp.sum((returns - mean) ** 2) / TOKENS
    target = (returns - mean) / jnp.sqrt(spread + 1e-05)
    dvalue = loss_scale * (value - target) / TOKENS
    grad_full = (dvalue / rms)[:, None] * (gw[None, :] - y / rms[:, None] * ((value - value_bias[0]) / D)[:, None])
    stream_grad = grad_full.astype(jnp.bfloat16)
    weight_grad = jnp.dot(hidden.T, stream_grad, preferred_element_type=jnp.float32).astype(jnp.bfloat16)
    width = D // N_COL

    def add_block(total, index):
        start = (index * width).astype(jnp.int32)
        grad_block = lax.dynamic_slice_in_dim(stream_grad, start, width, 1)
        weight_block = lax.dynamic_slice_in_dim(w_down, start, width, 1)
        term = jnp.dot(grad_block, weight_block.T, preferred_element_type=jnp.float32).astype(jnp.bfloat16)
        return (total + term.astype(jnp.float32), None)
    summed, unused = lax.scan(add_block, jnp.zeros((TOKENS, FF), jnp.float32), jnp.arange(N_COL, dtype=jnp.int32))
    return (weight_grad, summed.astype(jnp.bfloat16), stream_grad)
```

```python
import jax
import jax.numpy as jnp
from jax import lax
from jax.experimental import pallas as pl
from jax.experimental.pallas import tpu as pltpu
from jax.sharding import PartitionSpec as P

loss_scale = 2097152.0
bf16, f32 = jnp.bfloat16, jnp.float32

PAIR = [(c, c ^ 1) for c in range(16)]
MATE = [(c, c ^ 3) for c in range(16)]
ZUP = [(c, (c + 4) % 16) for c in range(16)]
ZDOWN = [(c, (c + 12) % 16) for c in range(16)]
ZONE = [(c, c ^ 4) for c in range(16)]
ZTHREE = [(c, c ^ 12) for c in range(16)]
ZLO = [(r, r ^ 4) for r in range(8)]
CORE = [(0, 1), (1, 0)]


def x_shift(k):
    return [(r, 4 * (r // 4) + (r + k) % 4) for r in range(8)]


def col(a, perm):
    return lax.ppermute(a, "col", perm)


def row(a, perm):
    return lax.ppermute(a, "row", perm)


def core(a):
    return lax.ppermute(a, "dp", CORE)


def returns_kernel(reward_ref, segment_ref, out_ref):
    value = reward_ref[...]
    segment = segment_ref[...]
    shape = value.shape
    line = lax.broadcasted_iota(jnp.int32, shape, 0) % 8
    lane = lax.broadcasted_iota(jnp.int32, shape, 1)

    def ahead(a, step):
        if step >= 128:
            return pltpu.roll(a, shape[0] - step // 128, 0)
        here = pltpu.roll(a, 128 - step, 1)
        below = pltpu.roll(here, shape[0] - 1, 0)
        return jnp.where(lane + step < 128, here, below)

    step = 1
    while step < 1024:
        inside = line * 128 + lane + step < 1024
        same = inside & (ahead(segment, step) == segment)
        value = value + jnp.where(same, ahead(value, step), 0.0)
        step *= 2
    count = shape[0] * shape[1]
    mean = jnp.sum(value) / count
    off = value - mean
    spread = jnp.sum(off * off) / count
    out_ref[...] = off / jnp.sqrt(jnp.broadcast_to(spread, shape) + 1e-05)


def targets(reward, segment):
    return pl.pallas_call(
        returns_kernel, out_shape=jax.ShapeDtypeStruct(reward.shape, f32)
    )(reward, segment)


def by_x(place, own, one_back, one_on, two_on):
    rel = jnp.stack([own, one_on, two_on, one_back, own, one_on, two_on])
    return lax.dynamic_slice_in_dim(rel, (4 - place) % 4, 4, 0)


def per_device(stream, hidden, w_down, norm_gain, value_head, value_bias, rewards, segments):
    p, r, c = lax.axis_index("dp"), lax.axis_index("row"), lax.axis_index("col")
    x, y, zhi = r % 4, c % 4, c // 4
    half = y // 2
    odd = y % 2
    width = 8192.0
    count = 2048.0
    gw = norm_gain * value_head

    stream_mate = col(stream, MATE)

    ha, hb = hidden[:32], hidden[32:]
    h3y = col(hidden, PAIR)
    down_a = col(ha, ZUP)
    up_b = col(hb, ZDOWN)
    h1 = jnp.concatenate([up_b, down_a], 0)

    ys = stream.astype(f32)
    part = jnp.stack(
        [jnp.sum(ys * ys, 1), jnp.sum(ys * gw[None], 1), rewards[0], segments[0].astype(f32)]
    )
    part_other = row(part, ZLO)
    zlo = r // 4
    pair2 = jnp.where(zlo == 0, jnp.stack([part, part_other]), jnp.stack([part_other, part]))
    all8 = by_x(
        x, pair2, row(pair2, x_shift(1)), row(pair2, x_shift(-1)), row(pair2, x_shift(2))
    )
    all8 = jnp.transpose(all8, (2, 1, 0, 3)).reshape(4, 8, 128)
    sums = all8[:2]
    owed = all8[2:]
    sums = sums + col(sums, PAIR)
    sums = sums + col(sums, MATE)
    sums = sums + col(sums, ZONE)
    sums = sums + col(sums, ZTHREE)
    owed_other = core(owed)
    both = jnp.where(p == 0, jnp.concatenate([owed, owed_other], 1), jnp.concatenate([owed_other, owed], 1))
    target = targets(both[0], both[1].astype(jnp.int32))

    rms = jnp.sqrt(sums[0] / width + 1e-05)
    head = sums[1] / rms
    value = head + value_bias[0]
    mine = lax.dynamic_slice_in_dim(target, p * 8, 8, 0)
    dvalue = loss_scale * (value - mine) / count
    scale = dvalue / rms
    lean = head / width / rms

    def gradient(block, gains, scales, leans):
        return (scales[:, None] * (gains[None] - block.astype(f32) * leans[:, None])).astype(bf16)

    own_scale = lax.dynamic_slice_in_dim(scale, r, 1, 0)[0]
    own_lean = lax.dynamic_slice_in_dim(lean, r, 1, 0)[0]
    stream_grad = gradient(stream, gw, own_scale, own_lean)

    block = jnp.concatenate([stream, stream_mate], 1)
    block_other = row(block, ZLO)
    two = jnp.where(zlo == 0, jnp.stack([block, block_other]), jnp.stack([block_other, block]))
    back, on, far = row(two, x_shift(1)), row(two, x_shift(-1)), row(two, x_shift(2))
    is_source = (x % 2) == half
    first = (x // 2) == 0
    low = jnp.where(is_source, jnp.where(x == half, two, far), jnp.where(x == half + 1, back, on))
    high = jnp.where(is_source, jnp.where(x == half, far, two), jnp.where(x == half + 1, on, back))
    blocks = jnp.stack([low, high], 1).reshape(4, 2, 64, 1024)
    gw_mate = col(gw, MATE)
    gains = jnp.concatenate([gw, gw_mate])

    def of_half(a):
        return lax.dynamic_index_in_dim(a.reshape(4, 2, 128), half, 1, False).reshape(4, 2, 64)

    scale4, lean4 = of_half(scale), of_half(lean)
    grads = (
        scale4[..., None] * (gains - blocks.astype(f32) * lean4[..., None])
    ).astype(bf16)

    def at(step, parity):
        z = (zhi + step) % 4
        return lax.dynamic_slice(grads, (z, parity, 0, 0), (1, 1, 64, 1024)).reshape(64, 1024)

    def pieces(parity):
        far, up, down, here = at(2, parity), at(1, parity), at(3, parity), at(0, parity)
        return jnp.concatenate([far, up[32:], down[:32], up[:32], down[32:], here], 0)

    g_other = pieces(1 - odd)
    g_own = pieces(odd)

    w_rows = w_down.shape[0] // 2
    w_half = lax.dynamic_slice_in_dim(w_down, p * w_rows, w_rows, 0)
    w_got = col(w_half, MATE)
    w_got_other = core(w_got)
    w_mate = jnp.where(
        p == 0, jnp.concatenate([w_got, w_got_other]), jnp.concatenate([w_got_other, w_got])
    )
    w_all = jnp.concatenate([w_down, w_mate], 1)

    h1y = col(h1, PAIR)
    far_a = col(down_a, ZUP)
    far_b = col(up_b, ZDOWN)
    h0 = jnp.concatenate([far_a, far_b], 0)
    up_a = col(ha, ZDOWN)
    down_b = col(hb, ZUP)
    h2 = jnp.concatenate([up_a, down_b], 0)
    h0y = col(h0, PAIR)
    h2y = col(h2, PAIR)
    h_own = jnp.concatenate([h0, h1, h2, hidden], 0)
    h_own_other = core(h_own)
    h_y = jnp.concatenate([h0y, h1y, h2y, h3y], 0)
    h_y_other = core(h_y)
    h_all = jnp.concatenate([h_own, h_y, h_own_other, h_y_other], 0)

    g_rep = jnp.concatenate([g_own, g_other], 0)
    q = 1 - p
    give = jnp.concatenate(
        [
            lax.dynamic_slice_in_dim(g_rep, q * 256, 256, 1),
            lax.dynamic_slice_in_dim(g_rep, 512 + q * 256, 256, 1),
        ],
        1,
    )
    got = core(give)
    keep_own = lax.dynamic_slice_in_dim(g_rep, p * 256, 256, 1)
    keep_mate = lax.dynamic_slice_in_dim(g_rep, 512 + p * 256, 256, 1)
    g_all_own = jnp.concatenate([keep_own, got[:, :256]], 0)
    g_all_mate = jnp.concatenate([keep_mate, got[:, 256:]], 0)

    def outer(a, b):
        return lax.dot_general(a, b, (((0,), (0,)), ((), ())), preferred_element_type=f32)

    def inner(a, b):
        return lax.dot_general(a, b, (((1,), (1,)), ((), ())), preferred_element_type=f32)

    w_send = outer(h_all, g_all_mate).astype(bf16)
    w_recv = col(w_send, MATE)

    s = [inner(g_other[64 * i : 64 * i + 64], w_all).astype(bf16) for i in range(4)]
    t = [col(a, PAIR) for a in s]
    own = inner(g_own, w_all)

    w_own = outer(h_all, g_all_own)

    def total(i, *more):
        a = own[64 * i : 64 * i + 64] + t[i].astype(f32)
        for m in more:
            a = a + m.astype(f32)
        return a.astype(bf16)

    q0 = total(0)
    from_down_a = col(q0[:32], ZUP)
    from_up_b = col(q0[32:], ZDOWN)
    q1 = total(1)
    pure_b = col(q1[:32], ZUP)
    pure_a = col(q1[32:], ZDOWN)
    q2 = total(2, jnp.concatenate([from_down_a, from_up_b], 0))
    mixed_a = col(q2[:32], ZUP)
    mixed_b = col(q2[32:], ZDOWN)
    hidden_grad = total(
        3,
        jnp.concatenate([pure_a, pure_b], 0),
        jnp.concatenate([mixed_a, mixed_b], 0),
    )

    w_sum = (w_own + w_recv.astype(f32)).astype(bf16)
    w_sum_other = core(w_sum)
    weight_grad = jnp.where(
        p == 0,
        jnp.concatenate([w_sum, w_sum_other], 1),
        jnp.concatenate([w_sum_other, w_sum], 1),
    )
    return weight_grad, hidden_grad, stream_grad


def solution(mesh):
    in_specs = (
        P(("dp", "row"), "col"),
        P(("dp", "col"), "row"),
        P("row", "col"),
        P("col"),
        P("col"),
        P(),
        P("dp", "row"),
        P("dp", "row"),
    )
    out_specs = (P("row", "col"), P(("dp", "col"), "row"), P(("dp", "row"), "col"))
    return jax.shard_map(
        per_device, mesh=mesh, in_specs=in_specs, out_specs=out_specs, check_vma=False
    )
```

```python
import functools

import jax
import jax.numpy as jnp
from jax import lax
from jax.experimental import pallas as pl
from jax.experimental.pallas import tpu as pltpu
from jax.sharding import PartitionSpec as P

loss_scale = 2097152.0
bf16, f32 = jnp.bfloat16, jnp.float32
WIDTH, COUNT = 8192.0, 2048.0

PAIR = [(c, c ^ 1) for c in range(16)]
MATE = [(c, c ^ 3) for c in range(16)]
ZUP = [(c, (c + 4) % 16) for c in range(16)]
ZDOWN = [(c, (c + 12) % 16) for c in range(16)]
ZONE = [(c, c ^ 4) for c in range(16)]
ZTHREE = [(c, c ^ 12) for c in range(16)]
ZLO = [(r, r ^ 4) for r in range(8)]
CORE = [(0, 1), (1, 0)]
XONE = [(r, r ^ 1) for r in range(8)]
XTHREE = [(r, r ^ 3) for r in range(8)]
VMEM_LIMIT = 48 * 1024 * 1024


def send(a, axis, perm, name):
    with jax.named_scope(name):
        return lax.ppermute(a, axis, perm)


def col(a, perm, name):
    return send(a, "col", perm, name)


def row(a, perm, name):
    return send(a, "row", perm, name)


def core(a, name):
    return send(a, "dp", CORE, name)


def after(a, *others):
    return lax.optimization_barrier((a, *others))[0]


def sds(shape, dtype):
    return jax.ShapeDtypeStruct(shape, dtype)


def call(body, out_shape, args, in_specs=None, scratch=(), flops=0, moved=0, name=None):
    extra = {} if in_specs is None else {"in_specs": in_specs}
    with jax.named_scope(name or getattr(body, "__name__", "fold")):
      return pl.pallas_call(
        body,
        out_shape=out_shape,
        scratch_shapes=list(scratch),
        compiler_params=pltpu.CompilerParams(vmem_limit_bytes=VMEM_LIMIT),
        cost_estimate=pl.CostEstimate(flops=flops, bytes_accessed=moved, transcendentals=0),
        **extra,
    )(*args)


def place():
    r, c = lax.axis_index("row"), lax.axis_index("col")
    return r % 4, r // 4, c % 4, c // 4


def prep_body(stream, gain, head, reward, segment, out, s_v, g_v, h_v, r_v, i_v, sems):
    moves = [
        pltpu.make_async_copy(src, dst, sems.at[i])
        for i, (src, dst) in enumerate(
            ((stream, s_v), (gain, g_v), (head, h_v), (reward, r_v), (segment, i_v))
        )
    ]
    for m in moves:
        m.start()
    for m in moves:
        m.wait()

    def parts(v):
        high = v.astype(bf16).astype(f32)
        mid = (v - high).astype(bf16).astype(f32)
        return high, mid, v - high - mid

    out[0:128] = s_v[...]
    rows = parts(g_v[...] * h_v[...])
    rows += (jnp.concatenate([*parts(r_v[...]), i_v[...].astype(f32)], 1),)
    line = lax.broadcasted_iota(jnp.int32, (16, 512), 0)
    extra = jnp.zeros((16, 512), f32)
    for i, a in enumerate(rows):
        extra = jnp.where(line == i, jnp.broadcast_to(a, (16, 512)), extra)
    out[128:144] = extra.astype(bf16)


def pick_body(own, other, out):
    x, _, y, _ = place()

    @pl.when(lax.rem(x, 2) == y // 2)
    def _():
        out[0:128] = own[0:128]

    @pl.when(lax.rem(x, 2) != y // 2)
    def _():
        out[0:128] = other[0:128]

    mine, theirs = own[128:144].astype(f32), other[128:144].astype(f32)
    even = lax.rem(x, 2) == 0
    line = lax.broadcasted_iota(jnp.int32, mine.shape, 0)
    first = jnp.where(even, mine, theirs)
    second = jnp.where(even, theirs, mine)
    second = jnp.broadcast_to(second[3:4], mine.shape)
    out[128:144] = jnp.where(line == 4, second, jnp.where(line == 3, first, mine)).astype(bf16)


def gains_of(block):
    extra = block[128:144].astype(f32)
    return extra[0:1] + extra[1:2] + extra[2:3]


def sums_body(near, away, sums, owed):
    x, _, _, _ = place()
    gw = gains_of(near)
    sums[...] = jnp.zeros(sums.shape, f32)

    def total(a):
        a = sum(a[:, 128 * i : 128 * i + 128] for i in range(8))
        return jnp.sum(a.T, axis=0, keepdims=True)

    for i, block in enumerate((near, away)):
        v = block[0:128].astype(f32)
        sums[2 * i : 2 * i + 1] = total(v * v)
        sums[2 * i + 1 : 2 * i + 2] = total(v * gw)
        extra = block[128:144].astype(f32)
        side = jnp.where(i == 0, x // 2, 1 - x // 2)
        for j in range(2):
            line = extra[3 + j : 4 + j]
            owed[pl.ds(2 * side + j, 1)] = line[:, 0:128] + line[:, 128:256] + line[:, 256:384]
            owed[pl.ds(4 + 2 * side + j, 1)] = line[:, 384:512]


def coefs_body(here, there, bias, out, target):
    x, zlo, y, _ = place()

    def rows(at):
        mine, theirs = here[at : at + 4], there[at : at + 4]
        return jnp.where(zlo == 0, mine, theirs), jnp.where(zlo == 0, theirs, mine)

    value = jnp.concatenate([*rows(8), *rows(16)], 0)
    segment = jnp.concatenate([*rows(12), *rows(20)], 0)
    shape = value.shape
    line = lax.broadcasted_iota(jnp.int32, shape, 0) % 8
    lane = lax.broadcasted_iota(jnp.int32, shape, 1)

    def ahead(a, step):
        if step >= 128:
            return pltpu.roll(a, shape[0] - step // 128, 0)
        here = pltpu.roll(a, 128 - step, 1)
        below = pltpu.roll(here, shape[0] - 1, 0)
        return jnp.where(lane + step < 128, here, below)

    step = 1
    while step < 1024:
        inside = line * 128 + lane + step < 1024
        same = inside & (ahead(segment, step) == segment)
        value = value + jnp.where(same, ahead(value, step), 0.0)
        step *= 2
    mean = jnp.sum(value) / COUNT
    off = value - mean
    spread = jnp.sum(off * off) / COUNT
    target[...] = (off / jnp.sqrt(jnp.broadcast_to(spread, shape) + 1e-05))[:8]
    wanted, sq, lin = [], [], []
    for i in range(4):
        zl = zlo if i < 2 else 1 - zlo
        b = x // 2 if i % 2 == 0 else 1 - x // 2
        wanted.append(target[pl.ds(4 * zl + 2 * b + y // 2, 1)])
        src = (here, there)[i // 2]
        at = 2 * (i % 2)
        sq.append(src[at : at + 1])
        lin.append(src[at + 1 : at + 2])
    wanted, sq, lin = (jnp.concatenate(a, 0) for a in (wanted, sq, lin))
    rms = jnp.sqrt(sq / WIDTH + 1e-05)
    head = lin / rms
    dvalue = loss_scale * (head + bias[0] - wanted) / COUNT
    out[0:4] = dvalue / rms
    out[4:8] = head / WIDTH / rms


def columns(coefs):
    padded = jnp.concatenate([coefs, jnp.zeros((120, 128), f32)], 0).T
    lane = lax.broadcasted_iota(jnp.int32, (128, 128), 1)

    def column(at):
        return jnp.sum(jnp.where(lane == at, padded, 0.0), axis=1, keepdims=True)

    return column


def formed(block, s, l, gains):
    return (s * (gains - block.astype(f32) * l)).astype(bf16)


def own_grad_body(stream, block, coefs, coefs_mate, grad):
    x, _, y, _ = place()
    column = columns(jnp.where(lax.rem(x, 2) == y // 2, coefs[...], coefs_mate[...]))
    grad[...] = formed(stream[...], column(0), column(4), gains_of(block)[:, :512])


def grad_body(coefs, here, there, g_own, g_other):
    x, zlo, y, zhi = place()
    odd = lax.rem(y, 2)
    column = columns(coefs[...])
    gains = gains_of(here)
    spots = {2: (0, 32), 1: (128, 64), 3: (96, 160), 0: (192, 224)}
    for k in range(4):
        z = lax.rem(zhi + k, 4)
        zl, b = z // 2, lax.rem(z, 2)
        at = jnp.where(zl == zlo, 0, 2) + jnp.where(b == x // 2, 0, 1)
        s_all, l_all = column(at), column(4 + at)
        s_all = jnp.where(odd == 0, s_all, jnp.concatenate([s_all[64:], s_all[:64]], 0))
        l_all = jnp.where(odd == 0, l_all, jnp.concatenate([l_all[64:], l_all[:64]], 0))
        start = jnp.where(b == x // 2, 0, 144)
        for same, src in ((True, here), (False, there)):

            @pl.when((zl == zlo) == same)
            def _(src=src, s_all=s_all, l_all=l_all, start=start, k=k):
                for who, out in ((0, g_own), (1, g_other)):
                    parity = odd if who == 0 else 1 - odd
                    for i in range(2):
                        first = pl.multiple_of(start + 64 * parity + 32 * i, 16)
                        rows = slice(64 * who + 32 * i, 64 * who + 32 * i + 32)
                        out[spots[k][i] : spots[k][i] + 32] = formed(
                            src[pl.ds(first, 32)], s_all[rows], l_all[rows], gains
                        )


LO = 1856
CHUNKS = ((0, 1024), (1024, 2048), (2048, 3072), (3072, 3696))
GOT = LO // 2
HIGH = 3696 - LO
SPANS = ((0, GOT), (GOT, LO), (LO, HIGH + GOT), (HIGH + GOT, 3696))
def inner_body(*refs):
    g_own, g_other, w, got0, got1, other0, other1 = refs[:7]
    sent, own, (w_v, m_v, sems) = refs[7:11], refs[11:15], refs[15:]
    p = lax.axis_index("dp")
    for i, (a, b) in enumerate(CHUNKS):
        pltpu.make_async_copy(w.at[a:b], w_v.at[a:b], sems.at[i]).start()

    def mate_copy(j, low, high):
        a, b = SPANS[j]
        src = (*low, *high)[j]
        off = (0, GOT, HIGH, HIGH + GOT)[j]
        return pltpu.make_async_copy(src.at[a - off : b - off], m_v.at[a:b], sems.at[4 + j])

    got, other = (got0, got1), (other0, other1)

    @pl.when(p == 0)
    def _():
        for j in range(4):
            mate_copy(j, got, other).start()

    @pl.when(p == 1)
    def _():
        for j in range(4):
            mate_copy(j, other, got).start()

    left = jnp.concatenate([g_other[:, :512], g_own[:, :512]], 0)
    right = jnp.concatenate([g_other[:, 512:], g_own[:, 512:]], 0)
    nt = (((1,), (1,)), ((), ()))
    waits = ((0, 1), (2,), (3,), ())
    for i, (a, b) in enumerate(CHUNKS):
        pltpu.make_async_copy(w.at[a:b], w_v.at[a:b], sems.at[i]).wait()
        for j in waits[i]:
            mate_copy(j, other, other).wait()
        for f in range(a, b, 512):
            e = min(f + 512, b)
            out = lax.dot_general(left, w_v[f:e], nt, preferred_element_type=f32)
            out = out + lax.dot_general(right, m_v[f:e], nt, preferred_element_type=f32)
            for n in range(4):
                sent[n][:, f:e] = out[64 * n : 64 * n + 64].astype(bf16)
                own[n][:, f:e] = out[256 + 64 * n : 256 + 64 * n + 64]


def outer_body(*refs, first):
    pieces, (g_own, g_other), (give, keep, h_v, g_v) = refs[:8], refs[8:10], refs[10:]
    p = lax.axis_index("dp")
    for n, piece in enumerate(pieces):
        h_v[64 * n : 64 * n + 64] = piece[...]
    for n, side in enumerate((1 - p, p)):
        start = pl.multiple_of(first + 256 * side, 256)
        g_v[:256, 256 * n : 256 * n + 256] = g_own[:, pl.ds(start, 256)]
        g_v[256:, 256 * n : 256 * n + 256] = g_other[:, pl.ds(start, 256)]
    for f in range(0, 3696, 512):
        e = min(f + 512, 3696)
        out = lax.dot_general(
            h_v[:, f:e], g_v[...], (((0,), (0,)), ((), ())), preferred_element_type=f32
        )
        give[f:e] = out[:, :256].astype(bf16)
        keep[f:e] = out[:, 256:]


def outer(pieces, g_own, g_other, first, name):
    return call(
        functools.partial(outer_body, first=first),
        [sds((3696, 256), bf16), sds((3696, 256), f32)],
        (*pieces, g_own, g_other),
        scratch=[pltpu.VMEM((512, 3696), bf16), pltpu.VMEM((512, 512), bf16)],
        flops=512 * 1024 * 3696,
        moved=8 << 20,
        name=name,
    )


def fold_body(*refs, extra, split):
    own, other = refs[:2]
    for i in range(2):
        rows = slice(32 * i, 32 * i + 32)
        total = own[rows] + other[rows].astype(f32)
        for m in refs[2 + i * extra : 2 + i * extra + extra]:
            total = total + m[...].astype(f32)
        if split:
            refs[2 + 2 * extra + i][...] = total.astype(bf16)
        else:
            refs[2 + 2 * extra][rows] = total.astype(bf16)


def fold(own, other, first=(), second=(), split=True):
    extra = len(first)
    wide = own.shape[1]
    out = [sds((32, wide), bf16)] * 2 if split else sds((64, wide), bf16)
    return call(
        functools.partial(fold_body, extra=extra, split=split),
        out,
        (own, other, *first, *second),
        moved=64 * wide * 10,
    )


def join_body(mine, other, out):
    p = lax.axis_index("dp")
    out[:, pl.ds(pl.multiple_of(256 * p, 256), 256)] = mine[...]
    out[:, pl.ds(pl.multiple_of(256 * (1 - p), 256), 256)] = other[...]


def join(mine, other):
    rows = mine.shape[0]
    tile = 1232
    return pl.pallas_call(
        join_body,
        grid=(rows // tile,),
        in_specs=[pl.BlockSpec((tile, 256), lambda i: (i, 0))] * 2,
        out_specs=pl.BlockSpec((tile, 512), lambda i: (i, 0)),
        out_shape=sds((rows, 512), bf16),
        compiler_params=pltpu.CompilerParams(vmem_limit_bytes=VMEM_LIMIT),
        cost_estimate=pl.CostEstimate(flops=0, bytes_accessed=rows * 2048, transcendentals=0),
    )(mine, other)


def per_device(stream, hidden, w_down, norm_gain, value_head, value_bias, rewards, segments):
    p = lax.axis_index("dp")
    smem = pl.BlockSpec(memory_space=pltpu.SMEM)
    vmem = pl.BlockSpec(memory_space=pltpu.VMEM)
    hbm = pl.BlockSpec(memory_space=pl.ANY)

    payload = call(
        prep_body,
        sds((144, 512), bf16),
        (stream, norm_gain[None], value_head[None], rewards, segments),
        in_specs=[hbm] * 5,
        scratch=[
            pltpu.VMEM((128, 512), bf16),
            pltpu.VMEM((1, 512), f32),
            pltpu.VMEM((1, 512), f32),
            pltpu.VMEM((1, 128), f32),
            pltpu.VMEM((1, 128), jnp.int32),
            pltpu.SemaphoreType.DMA((5,)),
        ],
    )
    payload_mate = col(payload, MATE, "payload_mate")
    ready = after(hidden, payload)
    y3 = col(ready, PAIR, "y3")
    ha, hb = ready[:32], ready[32:]
    down_a = col(ha, ZUP, "down_a")
    up_b = col(hb, ZDOWN, "up_b")

    w_half = lax.dynamic_slice_in_dim(w_down, p * HIGH, LO, 0)
    got0 = col(after(w_half[:GOT], payload_mate), MATE, "got0")
    got1 = col(after(w_half[GOT:], got0), MATE, "got1")

    block = jnp.concatenate([payload, payload_mate], 1)
    near = call(
        pick_body, sds((144, 1024), bf16), (block, row(block, XONE, "block_x1"))
    )
    near = after(near, y3, down_a, up_b)
    away = row(near, XTHREE, "block_x3")
    here = jnp.concatenate([near, away], 0)
    there = row(here, ZLO, "block_zlo")

    h1 = jnp.concatenate([up_b, down_a], 0)
    y1 = col(h1, PAIR, "y1")
    far_a = col(down_a, ZUP, "far_a")
    far_b = col(up_b, ZDOWN, "far_b")
    far_a, far_b = lax.optimization_barrier((far_a, far_b, away))[:2]
    up_a = col(after(ha, far_b), ZDOWN, "up_a")
    down_b = col(after(hb, far_a), ZUP, "down_b")
    h0 = jnp.concatenate([far_a, far_b], 0)
    h2 = jnp.concatenate([up_a, down_b], 0)
    y0 = col(after(h0, y1), PAIR, "y0")

    sums, owed = call(sums_body, (sds((8, 128), f32), sds((8, 128), f32)), (near, away))
    owed_other = core(owed, "owed_other")
    gates = ((y1, far_a, far_b), (got0,), (up_a, down_b))
    for i, perm in enumerate((PAIR, ZONE, ZTHREE)):
        sums = after(sums, *gates[i])
        sums = sums + col(sums, perm, f"sums{i}")
    y2 = col(after(h2, y0, sums), PAIR, "y2")
    got_other0 = core(got0, "got_other0")
    tiny = jnp.concatenate([sums, owed, owed_other], 0)
    coefs = call(
        coefs_body,
        sds((8, 128), f32),
        (tiny, row(tiny, ZLO, "sums_zlo"), value_bias),
        in_specs=[vmem, vmem, smem],
        scratch=[pltpu.VMEM((8, 128), f32)],
    )
    g_own, g_other = call(
        grad_body,
        (sds((256, 1024), bf16), sds((256, 1024), bf16)),
        (after(coefs, there, got1), here, there),
        moved=4 << 20,
    )
    got_other1 = core(got1, "got_other1")

    pieces = (h0, h1, h2, hidden, y0, y1, y2, y3)
    mate_give, mate_keep = outer(pieces, g_own, g_other, 512, "outer_mate")
    mate_got = core(mate_give, "mate_got")
    outs = call(
        inner_body,
        [sds((64, 3696), bf16)] * 4 + [sds((64, 3696), f32)] * 4,
        (after(g_own, mate_keep), g_other, w_down, got0, got1, got_other0, got_other1),
        in_specs=[vmem] * 2 + [hbm] * 5,
        scratch=[
            pltpu.VMEM((3696, 512), bf16),
            pltpu.VMEM((3696, 512), bf16),
            pltpu.SemaphoreType.DMA((8,)),
        ],
        flops=2 * 512 * 1024 * 3696,
        moved=13 << 20,
    )
    sent, own = outs[:4], outs[4:]
    w_send = (mate_keep + mate_got.astype(f32)).astype(bf16)
    w_recv = col(w_send, MATE, "w_recv")
    t = [col(a, PAIR, f"t{i}") for i, a in enumerate(sent)]

    give, keep = outer(pieces, after(g_own, w_send, own[0]), g_other, 0, "outer_own")
    own_got = core(give, "own_got")
    q0a, q0b = fold(own[0], after(t[0], keep))
    from_down = col(q0a, ZUP, "from_down")
    from_up = col(q0b, ZDOWN, "from_up")
    q1b, q1a = fold(own[1], t[1])
    from_down, from_up, q1a, q1b = lax.optimization_barrier((from_down, from_up, q1a, q1b))
    pure_b = col(q1b, ZUP, "pure_b")
    pure_a = col(q1a, ZDOWN, "pure_a")
    q2a, q2b = fold(own[2], after(t[2], pure_a, pure_b), (from_down,), (from_up,))
    mixed_a = col(q2a, ZUP, "mixed_a")
    mixed_b = col(q2b, ZDOWN, "mixed_b")
    hidden_grad = fold(own[3], t[3], (pure_a, mixed_a), (pure_b, mixed_b), split=False)

    coefs_mate = col(after(coefs, q0a), MATE, "coefs_mate")
    stream_grad = call(
        own_grad_body, sds((128, 512), bf16), (stream, near, coefs, coefs_mate)
    )

    keep = after(keep, hidden_grad)
    w_sum = (keep + own_got.astype(f32) + w_recv.astype(f32)).astype(bf16)
    weight_grad = join(w_sum, core(w_sum, "w_sum"))
    return weight_grad, hidden_grad, stream_grad


def solution(mesh):
    in_specs = (
        P(("dp", "row"), "col"),
        P(("dp", "col"), "row"),
        P("row", "col"),
        P("col"),
        P("col"),
        P(),
        P("dp", "row"),
        P("dp", "row"),
    )
    out_specs = (P("row", "col"), P(("dp", "col"), "row"), P(("dp", "row"), "col"))
    return jax.shard_map(
        per_device, mesh=mesh, in_specs=in_specs, out_specs=out_specs, check_vma=False
    )
```

```python
import functools

import jax
import jax.numpy as jnp
from jax import lax
from jax.experimental import pallas as pl
from jax.experimental.pallas import tpu as pltpu
from jax.sharding import PartitionSpec as P

loss_scale = 2097152.0
bf16, f32 = jnp.bfloat16, jnp.float32
WIDTH, COUNT = 8192.0, 2048.0

PAIR = [(c, c ^ 1) for c in range(16)]
MATE = [(c, c ^ 3) for c in range(16)]
ZUP = [(c, (c + 4) % 16) for c in range(16)]
ZDOWN = [(c, (c + 12) % 16) for c in range(16)]
ZONE = [(c, c ^ 4) for c in range(16)]
ZTHREE = [(c, c ^ 12) for c in range(16)]
ZLO = [(r, r ^ 4) for r in range(8)]
CORE = [(0, 1), (1, 0)]
XONE = [(r, r ^ 1) for r in range(8)]
XTHREE = [(r, r ^ 3) for r in range(8)]
VMEM_LIMIT = 56 * 1024 * 1024


def send(a, axis, perm, name):
    with jax.named_scope(name):
        return lax.ppermute(a, axis, perm)


def col(a, perm, name):
    return send(a, "col", perm, name)


def row(a, perm, name):
    return send(a, "row", perm, name)


def core(a, name):
    return send(a, "dp", CORE, name)


def after(a, *others):
    return lax.optimization_barrier((a, *others))[0]


def sds(shape, dtype):
    return jax.ShapeDtypeStruct(shape, dtype)


def call(body, out_shape, args, in_specs=None, scratch=(), flops=0, moved=0, name=None):
    extra = {} if in_specs is None else {"in_specs": in_specs}
    with jax.named_scope(name or getattr(body, "__name__", "mid")):
      return pl.pallas_call(
        body,
        out_shape=out_shape,
        scratch_shapes=list(scratch),
        compiler_params=pltpu.CompilerParams(vmem_limit_bytes=VMEM_LIMIT),
        cost_estimate=pl.CostEstimate(flops=flops, bytes_accessed=moved, transcendentals=0),
        **extra,
    )(*args)


def place():
    r, c = lax.axis_index("row"), lax.axis_index("col")
    return r % 4, r // 4, c % 4, c // 4


def prep_body(stream, gain, head, reward, segment, out, s_v, g_v, h_v, r_v, i_v, sems):
    moves = [
        pltpu.make_async_copy(src, dst, sems.at[i])
        for i, (src, dst) in enumerate(
            ((stream, s_v), (gain, g_v), (head, h_v), (reward, r_v), (segment, i_v))
        )
    ]
    for m in moves:
        m.start()
    for m in moves:
        m.wait()

    def parts(v):
        high = v.astype(bf16).astype(f32)
        mid = (v - high).astype(bf16).astype(f32)
        return high, mid, v - high - mid

    out[0:128] = s_v[...]
    rows = parts(g_v[...] * h_v[...])
    rows += (jnp.concatenate([*parts(r_v[...]), i_v[...].astype(f32)], 1),)
    line = lax.broadcasted_iota(jnp.int32, (16, 512), 0)
    extra = jnp.zeros((16, 512), f32)
    for i, a in enumerate(rows):
        extra = jnp.where(line == i, jnp.broadcast_to(a, (16, 512)), extra)
    out[128:144] = extra.astype(bf16)


def pick_body(own, other, out, sums, owed):
    x, _, y, _ = place()

    @pl.when(lax.rem(x, 2) == y // 2)
    def _():
        out[0:128] = own[0:128]

    @pl.when(lax.rem(x, 2) != y // 2)
    def _():
        out[0:128] = other[0:128]

    mine, theirs = own[128:144].astype(f32), other[128:144].astype(f32)
    even = lax.rem(x, 2) == 0
    first = jnp.where(even, mine, theirs)
    second = jnp.where(even, theirs, mine)
    for i, a in enumerate((first[3:4], second[3:4])):
        owed[i : i + 1] = a[:, 0:128] + a[:, 128:256] + a[:, 256:384]
        owed[2 + i : 3 + i] = a[:, 384:512]
    owed[4:8] = jnp.zeros((4, 128), f32)
    out[128:144] = mine.astype(bf16)
    gw = gains_of(own)

    def total(a):
        a = sum(a[:, 128 * i : 128 * i + 128] for i in range(8))
        return jnp.sum(a.T, axis=0, keepdims=True)

    v = out[0:128].astype(f32)
    sums[0:1] = total(v * v)
    sums[1:2] = total(v * gw)
    sums[2:8] = jnp.zeros((6, 128), f32)


def gains_of(block):
    extra = block[128:144].astype(f32)
    return extra[0:1] + extra[1:2] + extra[2:3]


def coefs_body(here, there, bias, out, target):
    x, zlo, y, _ = place()

    def side(src, at):
        near, away = src[at : at + 2], src[24 + at : 26 + at]
        low, high = jnp.where(x // 2 == 0, near, away), jnp.where(x // 2 == 0, away, near)
        return jnp.concatenate([low, high], 0)

    def rows(at):
        mine, theirs = side(here, at), side(there, at)
        return jnp.where(zlo == 0, mine, theirs), jnp.where(zlo == 0, theirs, mine)

    value = jnp.concatenate([*rows(8), *rows(16)], 0)
    segment = jnp.concatenate([*rows(10), *rows(18)], 0)
    shape = value.shape
    line = lax.broadcasted_iota(jnp.int32, shape, 0) % 8
    lane = lax.broadcasted_iota(jnp.int32, shape, 1)

    def ahead(a, step):
        if step >= 128:
            return pltpu.roll(a, shape[0] - step // 128, 0)
        here = pltpu.roll(a, 128 - step, 1)
        below = pltpu.roll(here, shape[0] - 1, 0)
        return jnp.where(lane + step < 128, here, below)

    step = 1
    while step < 1024:
        inside = line * 128 + lane + step < 1024
        same = inside & (ahead(segment, step) == segment)
        value = value + jnp.where(same, ahead(value, step), 0.0)
        step *= 2
    mean = jnp.sum(value) / COUNT
    off = value - mean
    spread = jnp.sum(off * off) / COUNT
    target[...] = (off / jnp.sqrt(jnp.broadcast_to(spread, shape) + 1e-05))[:8]
    wanted, sq, lin = [], [], []
    for i in range(4):
        zl = zlo if i < 2 else 1 - zlo
        b = x // 2 if i % 2 == 0 else 1 - x // 2
        wanted.append(target[pl.ds(4 * zl + 2 * b + y // 2, 1)])
        src = (here, there)[i // 2]
        at = 24 * (i % 2)
        sq.append(src[at : at + 1])
        lin.append(src[at + 1 : at + 2])
    wanted, sq, lin = (jnp.concatenate(a, 0) for a in (wanted, sq, lin))
    rms = jnp.sqrt(sq / WIDTH + 1e-05)
    head = lin / rms
    dvalue = loss_scale * (head + bias[0] - wanted) / COUNT
    out[0:4] = dvalue / rms
    out[4:8] = head / WIDTH / rms


def columns(coefs):
    padded = jnp.concatenate([coefs, jnp.zeros((120, 128), f32)], 0).T
    lane = lax.broadcasted_iota(jnp.int32, (128, 128), 1)

    def column(at):
        return jnp.sum(jnp.where(lane == at, padded, 0.0), axis=1, keepdims=True)

    return column


def formed(block, s, l, gains):
    return (s * (gains - block.astype(f32) * l)).astype(bf16)


def own_grad_body(stream, block, coefs, coefs_mate, grad):
    x, _, y, _ = place()
    column = columns(jnp.where(lax.rem(x, 2) == y // 2, coefs[...], coefs_mate[...]))
    grad[...] = formed(stream[...], column(0), column(4), gains_of(block)[:, :512])


def grad_body(coefs, here, there, g_own, g_other):
    x, zlo, y, zhi = place()
    odd = lax.rem(y, 2)
    column = columns(coefs[...])
    gains = gains_of(here)
    for spot, k in enumerate((2, 1, 3, 0)):
        z = lax.rem(zhi + k, 4)
        zl, b = z // 2, lax.rem(z, 2)
        at = jnp.where(zl == zlo, 0, 2) + jnp.where(b == x // 2, 0, 1)
        s_all, l_all = column(at), column(4 + at)
        s_all = jnp.where(odd == 0, s_all, jnp.concatenate([s_all[64:], s_all[:64]], 0))
        l_all = jnp.where(odd == 0, l_all, jnp.concatenate([l_all[64:], l_all[:64]], 0))
        start = jnp.where(b == x // 2, 0, 144)
        for same, src in ((True, here), (False, there)):

            @pl.when((zl == zlo) == same)
            def _(src=src, s_all=s_all, l_all=l_all, start=start, spot=spot):
                for who, out in ((0, g_own), (1, g_other)):
                    parity = odd if who == 0 else 1 - odd
                    first = pl.multiple_of(start + 64 * parity, 16)
                    rows = slice(64 * who, 64 * who + 64)
                    out[64 * spot : 64 * spot + 64] = formed(
                        src[pl.ds(first, 64)], s_all[rows], l_all[rows], gains
                    )


LO = 1856
CHUNKS = ((0, 1024), (1024, 2048), (2048, 3072), (3072, 3696))
HIGH = 3696 - LO
SPANS = ((0, LO), (LO, 3696))
PARTS = ((0, 64), (64, 128), (128, 192), (192, 256))
def inner_body(*refs):
    g_own, g_other, w, got, other = refs[:5]
    sent, own, (w_v, m_v, sems) = refs[5:9], refs[9:13], refs[13:]
    p = lax.axis_index("dp")
    for i, (a, b) in enumerate(CHUNKS):
        pltpu.make_async_copy(w.at[a:b], w_v.at[a:b], sems.at[i]).start()

    def mate_copy(j, low, high):
        a, b = SPANS[j]
        src, off = (low, high)[j], (0, HIGH)[j]
        return pltpu.make_async_copy(src.at[a - off : b - off], m_v.at[a:b], sems.at[4 + j])

    @pl.when(p == 0)
    def _():
        for j in range(2):
            mate_copy(j, got, other).start()

    @pl.when(p == 1)
    def _():
        for j in range(2):
            mate_copy(j, other, got).start()

    left = jnp.concatenate([g_other[:, :512], g_own[:, :512]], 0)
    right = jnp.concatenate([g_other[:, 512:], g_own[:, 512:]], 0)
    nt = (((1,), (1,)), ((), ()))
    waits = ((0,), (1,), (), ())
    for i, (a, b) in enumerate(CHUNKS):
        pltpu.make_async_copy(w.at[a:b], w_v.at[a:b], sems.at[i]).wait()
        for j in waits[i]:
            mate_copy(j, other, other).wait()
        for f in range(a, b, 512):
            e = min(f + 512, b)
            out = lax.dot_general(left, w_v[f:e], nt, preferred_element_type=f32)
            out = out + lax.dot_general(right, m_v[f:e], nt, preferred_element_type=f32)
            for n, (low, high) in enumerate(PARTS):
                sent[n][:, f:e] = out[low:high].astype(bf16)
                own[n][:, f:e] = out[256 + low : 256 + high]


def outer_body(*refs):
    pieces, (g_own, g_other) = refs[:8], refs[8:10]
    give, mate_keep, keep, h_v, g_v = refs[10:]
    p = lax.axis_index("dp")
    at = 0
    for piece in pieces:
        h_v[at : at + piece.shape[0]] = piece[...]
        at += piece.shape[0]
    for n, side in enumerate((1 - p, 3 - p, 2 + p, p)):
        start = pl.multiple_of(256 * side, 256)
        g_v[:256, 256 * n : 256 * n + 256] = g_own[:, pl.ds(start, 256)]
        g_v[256:, 256 * n : 256 * n + 256] = g_other[:, pl.ds(start, 256)]
    for f in range(0, 3696, 512):
        e = min(f + 512, 3696)
        out = lax.dot_general(
            h_v[:, f:e], g_v[...], (((0,), (0,)), ((), ())), preferred_element_type=f32
        )
        give[f:e] = out[:, :512].astype(bf16)
        mate_keep[f:e] = out[:, 512:768]
        keep[f:e] = out[:, 768:]


def outer(pieces, g_own, g_other):
    return call(
        outer_body,
        [sds((3696, 512), bf16), sds((3696, 256), f32), sds((3696, 256), f32)],
        (*pieces, g_own, g_other),
        scratch=[pltpu.VMEM((512, 3696), bf16), pltpu.VMEM((512, 1024), bf16)],
        flops=2 * 512 * 1024 * 3696,
        moved=16 << 20,
    )


def far_body(own, other, first, second):
    total = own[...] + other[...].astype(f32)
    first[...] = total[:32].astype(bf16)
    second[...] = total[32:].astype(bf16)


def mid_body(own, other, more, out, *, first):
    total = own[...] + other[...].astype(f32)
    for at in (0, 32):
        part = total[at : at + 32]
        if at == first:
            part = part + more[...].astype(f32)
        out[at : at + 32] = part.astype(bf16)


def here_body(own, other, below, above, out):
    total = own[...] + other[...].astype(f32)
    out[...] = (total + below[...].astype(f32) + above[...].astype(f32)).astype(bf16)


def join_body(mine, other, out):
    p = lax.axis_index("dp")
    out[:, pl.ds(pl.multiple_of(256 * p, 256), 256)] = mine[...]
    out[:, pl.ds(pl.multiple_of(256 * (1 - p), 256), 256)] = other[...]


def join(mine, other):
    rows = mine.shape[0]
    tile = 1232
    return pl.pallas_call(
        join_body,
        grid=(rows // tile,),
        in_specs=[pl.BlockSpec((tile, 256), lambda i: (i, 0))] * 2,
        out_specs=pl.BlockSpec((tile, 512), lambda i: (i, 0)),
        out_shape=sds((rows, 512), bf16),
        compiler_params=pltpu.CompilerParams(vmem_limit_bytes=VMEM_LIMIT),
        cost_estimate=pl.CostEstimate(flops=0, bytes_accessed=rows * 2048, transcendentals=0),
    )(mine, other)


def per_device(stream, hidden, w_down, norm_gain, value_head, value_bias, rewards, segments):
    p = lax.axis_index("dp")
    smem = pl.BlockSpec(memory_space=pltpu.SMEM)
    vmem = pl.BlockSpec(memory_space=pltpu.VMEM)
    hbm = pl.BlockSpec(memory_space=pl.ANY)

    payload = call(
        prep_body,
        sds((144, 512), bf16),
        (stream, norm_gain[None], value_head[None], rewards, segments),
        in_specs=[hbm] * 5,
        scratch=[
            pltpu.VMEM((128, 512), bf16),
            pltpu.VMEM((1, 512), f32),
            pltpu.VMEM((1, 512), f32),
            pltpu.VMEM((1, 128), f32),
            pltpu.VMEM((1, 128), jnp.int32),
            pltpu.SemaphoreType.DMA((5,)),
        ],
    )
    payload_mate = col(payload, MATE, "payload_mate")
    y3 = col(hidden, PAIR, "y3")
    down = col(hidden, ZUP, "down")
    up = col(hidden, ZDOWN, "up")

    w_half = lax.dynamic_slice_in_dim(w_down, p * HIGH, LO, 0)
    got = col(after(w_half, payload_mate), MATE, "got")

    block = jnp.concatenate([payload, payload_mate], 1)
    near, sums, owed = call(
        pick_body,
        (sds((144, 1024), bf16), sds((8, 128), f32), sds((8, 128), f32)),
        (block, row(block, XONE, "block_x1")),
    )
    away = row(near, XTHREE, "block_x3")
    here = jnp.concatenate([near, away], 0)
    there = row(here, ZLO, "block_zlo")
    owed_other = core(owed, "owed_other")

    gates = ((y3,), (down, up), (away,))
    for i, perm in enumerate((PAIR, ZONE, ZTHREE)):
        sums = after(sums, *gates[i])
        sums = sums + col(sums, perm, f"sums{i}")
        if i == 0:
            down, up = lax.optimization_barrier((down, up, sums))[:2]
            far_a = col(down[:32], ZUP, "far_a")
            far_b = col(up[32:], ZDOWN, "far_b")
            y12 = col(jnp.concatenate([up, down], 0), PAIR, "y12")
    y0 = col(after(jnp.concatenate([far_a, far_b], 0), sums), PAIR, "y0")
    tiny = jnp.concatenate([sums, owed, owed_other], 0)
    tiny = after(tiny, far_a, far_b)
    tiny = jnp.concatenate([tiny, row(tiny, XTHREE, "tiny_x3")], 0)
    tiny_zlo = row(tiny, ZLO, "tiny_zlo")
    coefs = call(
        coefs_body,
        sds((8, 128), f32),
        (after(tiny, got), tiny_zlo, value_bias),
        in_specs=[vmem, vmem, smem],
        scratch=[pltpu.VMEM((8, 128), f32)],
    )
    got_other = core(after(got, tiny_zlo), "got_other")
    coefs_mate = col(coefs, MATE, "coefs_mate")
    g_own, g_other = call(
        grad_body,
        (sds((256, 1024), bf16), sds((256, 1024), bf16)),
        (coefs, here, there),
        moved=4 << 20,
    )

    pieces = (far_a, far_b, up, down, hidden, y0, y12, y3)
    give, mate_keep, keep = outer(pieces, after(g_own, coefs_mate), g_other)
    both_got = core(give, "both_got")
    outs = call(
        inner_body,
        [sds((b - a, 3696), d) for d in (bf16, f32) for a, b in PARTS],
        (after(g_own, mate_keep), g_other, w_down, got, got_other),
        in_specs=[vmem] * 2 + [hbm] * 3,
        scratch=[
            pltpu.VMEM((3696, 512), bf16),
            pltpu.VMEM((3696, 512), bf16),
            pltpu.SemaphoreType.DMA((6,)),
        ],
        flops=2 * 512 * 1024 * 3696,
        moved=13 << 20,
    )
    sent, own = outs[:4], outs[4:]
    t = [col(a, PAIR, f"t{i}") for i, a in enumerate(sent)]

    w_send = (after(mate_keep, own[0]) + both_got[:, 256:].astype(f32)).astype(bf16)
    w_recv = col(w_send, MATE, "w_recv")

    half_rows = [sds((32, 3696), bf16)] * 2
    q_a, q_b = call(far_body, half_rows, (own[0], after(t[0], w_send)))
    from_down = col(q_a, ZUP, "from_down")
    from_up = col(q_b, ZDOWN, "from_up")
    q_up = call(
        functools.partial(mid_body, first=0), sds((64, 3696), bf16), (own[1], t[1], from_down)
    )
    below = col(q_up, ZUP, "below")
    q_down = call(
        functools.partial(mid_body, first=32), sds((64, 3696), bf16), (own[2], t[2], from_up)
    )
    above = col(q_down, ZDOWN, "above")

    stream_grad = call(
        own_grad_body, sds((128, 512), bf16), (stream, near, coefs, coefs_mate)
    )
    hidden_grad = call(here_body, sds((64, 3696), bf16), (own[3], t[3], below, above))
    keep = after(keep, hidden_grad, stream_grad)
    w_sum = (keep + both_got[:, :256].astype(f32) + w_recv.astype(f32)).astype(bf16)
    w_sum_other = core(w_sum, "w_sum")
    weight_grad = join(w_sum, w_sum_other)
    return weight_grad, hidden_grad, stream_grad


def solution(mesh):
    in_specs = (
        P(("dp", "row"), "col"),
        P(("dp", "col"), "row"),
        P("row", "col"),
        P("col"),
        P("col"),
        P(),
        P("dp", "row"),
        P("dp", "row"),
    )
    out_specs = (P("row", "col"), P(("dp", "col"), "row"), P(("dp", "row"), "col"))
    return jax.shard_map(
        per_device, mesh=mesh, in_specs=in_specs, out_specs=out_specs, check_vma=False
    )
```

```python
import functools

import jax
import jax.numpy as jnp
from jax import lax
from jax.experimental import pallas as pl
from jax.experimental.pallas import tpu as pltpu
from jax.sharding import PartitionSpec as P

loss_scale = 2097152.0
bf16, f32 = jnp.bfloat16, jnp.float32
WIDTH, COUNT = 8192.0, 2048.0

PAIR = [(c, c ^ 1) for c in range(16)]
MATE = [(c, c ^ 3) for c in range(16)]
ZUP = [(c, (c + 4) % 16) for c in range(16)]
ZDOWN = [(c, (c + 12) % 16) for c in range(16)]
ZONE = [(c, c ^ 4) for c in range(16)]
ZTHREE = [(c, c ^ 12) for c in range(16)]
ZLO = [(r, r ^ 4) for r in range(8)]
CORE = [(0, 1), (1, 0)]
XONE = [(r, r ^ 1) for r in range(8)]
XTHREE = [(r, r ^ 3) for r in range(8)]
MIB = 1024 * 1024


def send(a, axis, perm, name):
    with jax.named_scope(name):
        return lax.ppermute(a, axis, perm)


def col(a, perm, name):
    return send(a, "col", perm, name)


def row(a, perm, name):
    return send(a, "row", perm, name)


def core(a, name):
    return send(a, "dp", CORE, name)


def after(a, *others):
    return lax.optimization_barrier((a, *others))[0]


def sds(shape, dtype):
    return jax.ShapeDtypeStruct(shape, dtype)


def call(body, out_shape, args, in_specs=None, scratch=(), flops=0, moved=0, name=None, grant=16):
    extra = {} if in_specs is None else {"in_specs": in_specs}
    with jax.named_scope(name or getattr(body, "__name__", "mid")):
      return pl.pallas_call(
        body,
        out_shape=out_shape,
        scratch_shapes=list(scratch),
        compiler_params=pltpu.CompilerParams(vmem_limit_bytes=grant * MIB),
        cost_estimate=pl.CostEstimate(flops=flops, bytes_accessed=moved, transcendentals=0),
        **extra,
    )(*args)


def place():
    r, c = lax.axis_index("row"), lax.axis_index("col")
    return r % 4, r // 4, c % 4, c // 4


def prep_body(stream, gain, head, reward, segment, out, s_v, g_v, h_v, r_v, i_v, sems):
    moves = [
        pltpu.make_async_copy(src, dst, sems.at[i])
        for i, (src, dst) in enumerate(
            ((stream, s_v), (gain, g_v), (head, h_v), (reward, r_v), (segment, i_v))
        )
    ]
    for m in moves:
        m.start()
    for m in moves:
        m.wait()

    def parts(v):
        high = v.astype(bf16).astype(f32)
        mid = (v - high).astype(bf16).astype(f32)
        return high, mid, v - high - mid

    out[0:128] = s_v[...]
    rows = parts(g_v[...] * h_v[...])
    rows += (jnp.concatenate([*parts(r_v[...]), i_v[...].astype(f32)], 1),)
    line = lax.broadcasted_iota(jnp.int32, (16, 512), 0)
    extra = jnp.zeros((16, 512), f32)
    for i, a in enumerate(rows):
        extra = jnp.where(line == i, jnp.broadcast_to(a, (16, 512)), extra)
    out[128:144] = extra.astype(bf16)


def pick_body(own, other, out, sums, owed):
    x, _, y, _ = place()

    @pl.when(lax.rem(x, 2) == y // 2)
    def _():
        out[0:128] = own[0:128]

    @pl.when(lax.rem(x, 2) != y // 2)
    def _():
        out[0:128] = other[0:128]

    mine, theirs = own[128:144].astype(f32), other[128:144].astype(f32)
    even = lax.rem(x, 2) == 0
    first = jnp.where(even, mine, theirs)
    second = jnp.where(even, theirs, mine)
    for i, a in enumerate((first[3:4], second[3:4])):
        owed[i : i + 1] = a[:, 0:128] + a[:, 128:256] + a[:, 256:384]
        owed[2 + i : 3 + i] = a[:, 384:512]
    owed[4:8] = jnp.zeros((4, 128), f32)
    out[128:144] = mine.astype(bf16)
    gw = gains_of(own)

    def total(a):
        a = sum(a[:, 128 * i : 128 * i + 128] for i in range(8))
        return jnp.sum(a.T, axis=0, keepdims=True)

    v = out[0:128].astype(f32)
    sums[0:1] = total(v * v)
    sums[1:2] = total(v * gw)
    sums[2:8] = jnp.zeros((6, 128), f32)


def gains_of(block):
    extra = block[128:144].astype(f32)
    return extra[0:1] + extra[1:2] + extra[2:3]


def coefs_body(here, there, bias, out, target):
    x, zlo, y, _ = place()

    def side(src, at):
        near, away = src[at : at + 2], src[24 + at : 26 + at]
        low, high = jnp.where(x // 2 == 0, near, away), jnp.where(x // 2 == 0, away, near)
        return jnp.concatenate([low, high], 0)

    def rows(at):
        mine, theirs = side(here, at), side(there, at)
        return jnp.where(zlo == 0, mine, theirs), jnp.where(zlo == 0, theirs, mine)

    value = jnp.concatenate([*rows(8), *rows(16)], 0)
    segment = jnp.concatenate([*rows(10), *rows(18)], 0)
    shape = value.shape
    line = lax.broadcasted_iota(jnp.int32, shape, 0) % 8
    lane = lax.broadcasted_iota(jnp.int32, shape, 1)

    def ahead(a, step):
        if step >= 128:
            return pltpu.roll(a, shape[0] - step // 128, 0)
        here = pltpu.roll(a, 128 - step, 1)
        below = pltpu.roll(here, shape[0] - 1, 0)
        return jnp.where(lane + step < 128, here, below)

    step = 1
    while step < 1024:
        inside = line * 128 + lane + step < 1024
        same = inside & (ahead(segment, step) == segment)
        value = value + jnp.where(same, ahead(value, step), 0.0)
        step *= 2
    mean = jnp.sum(value) / COUNT
    off = value - mean
    spread = jnp.sum(off * off) / COUNT
    target[...] = (off / jnp.sqrt(jnp.broadcast_to(spread, shape) + 1e-05))[:8]
    wanted, sq, lin = [], [], []
    for i in range(4):
        zl = zlo if i < 2 else 1 - zlo
        b = x // 2 if i % 2 == 0 else 1 - x // 2
        wanted.append(target[pl.ds(4 * zl + 2 * b + y // 2, 1)])
        src = (here, there)[i // 2]
        at = 24 * (i % 2)
        sq.append(src[at : at + 1])
        lin.append(src[at + 1 : at + 2])
    wanted, sq, lin = (jnp.concatenate(a, 0) for a in (wanted, sq, lin))
    rms = jnp.sqrt(sq / WIDTH + 1e-05)
    head = lin / rms
    dvalue = loss_scale * (head + bias[0] - wanted) / COUNT
    out[0:4] = dvalue / rms
    out[4:8] = head / WIDTH / rms


def columns(coefs):
    padded = jnp.concatenate([coefs, jnp.zeros((120, 128), f32)], 0).T
    lane = lax.broadcasted_iota(jnp.int32, (128, 128), 1)

    def column(at):
        return jnp.sum(jnp.where(lane == at, padded, 0.0), axis=1, keepdims=True)

    return column


def formed(block, s, l, gains):
    return (s * (gains - block.astype(f32) * l)).astype(bf16)


def own_grad_body(stream, block, coefs, coefs_mate, grad):
    x, _, y, _ = place()
    column = columns(jnp.where(lax.rem(x, 2) == y // 2, coefs[...], coefs_mate[...]))
    grad[...] = formed(stream[...], column(0), column(4), gains_of(block)[:, :512])


def grad_body(coefs, here, there, g_own, g_other):
    x, zlo, y, zhi = place()
    odd = lax.rem(y, 2)
    column = columns(coefs[...])
    gains = gains_of(here)
    for k, spots in enumerate(((192, 224), (128, 64), (0, 32), (96, 160))):
        z = lax.rem(zhi + k, 4)
        zl, b = z // 2, lax.rem(z, 2)
        at = jnp.where(zl == zlo, 0, 2) + jnp.where(b == x // 2, 0, 1)
        s_all, l_all = column(at), column(4 + at)
        s_all = jnp.where(odd == 0, s_all, jnp.concatenate([s_all[64:], s_all[:64]], 0))
        l_all = jnp.where(odd == 0, l_all, jnp.concatenate([l_all[64:], l_all[:64]], 0))
        start = jnp.where(b == x // 2, 0, 144)
        for same, src in ((True, here), (False, there)):

            @pl.when((zl == zlo) == same)
            def _(src=src, s_all=s_all, l_all=l_all, start=start, spots=spots):
                for who, out in ((0, g_own), (1, g_other)):
                    parity = odd if who == 0 else 1 - odd
                    first = pl.multiple_of(start + 64 * parity, 16)
                    rows = slice(64 * who, 64 * who + 64)
                    made = formed(src[pl.ds(first, 64)], s_all[rows], l_all[rows], gains)
                    for i, spot in enumerate(spots):
                        out[spot : spot + 32] = made[32 * i : 32 * i + 32]


LO = 1856
CHUNKS = ((0, 1024), (1024, 2048), (2048, 3072), (3072, 3696))
HIGH = 3696 - LO
SPANS = ((0, LO), (LO, 3696))
PARTS = ((0, 64), (64, 128), (128, 192), (192, 256))
def inner_body(*refs):
    g_own, g_other, w, got, other = refs[:5]
    sent, own, (w_v, m_v, sems) = refs[5:9], refs[9:13], refs[13:]
    p = lax.axis_index("dp")
    for i, (a, b) in enumerate(CHUNKS):
        pltpu.make_async_copy(w.at[a:b], w_v.at[a:b], sems.at[i]).start()

    def mate_copy(j, low, high):
        a, b = SPANS[j]
        src, off = (low, high)[j], (0, HIGH)[j]
        return pltpu.make_async_copy(src.at[a - off : b - off], m_v.at[a:b], sems.at[4 + j])

    @pl.when(p == 0)
    def _():
        for j in range(2):
            mate_copy(j, got, other).start()

    @pl.when(p == 1)
    def _():
        for j in range(2):
            mate_copy(j, other, got).start()

    left = jnp.concatenate([g_other[:, :512], g_own[:, :512]], 0)
    right = jnp.concatenate([g_other[:, 512:], g_own[:, 512:]], 0)
    nt = (((1,), (1,)), ((), ()))
    waits = ((0,), (1,), (), ())
    for i, (a, b) in enumerate(CHUNKS):
        pltpu.make_async_copy(w.at[a:b], w_v.at[a:b], sems.at[i]).wait()
        for j in waits[i]:
            mate_copy(j, other, other).wait()
        for f in range(a, b, 512):
            e = min(f + 512, b)
            out = lax.dot_general(left, w_v[f:e], nt, preferred_element_type=f32)
            out = out + lax.dot_general(right, m_v[f:e], nt, preferred_element_type=f32)
            for n, (low, high) in enumerate(PARTS):
                sent[n][:, f:e] = out[low:high].astype(bf16)
                own[n][:, f:e] = out[256 + low : 256 + high]


def outer_body(*refs, first):
    pieces, (g_own, g_other), (give, keep, h_v, g_v) = refs[:8], refs[8:10], refs[10:]
    p = lax.axis_index("dp")
    far_a, far_b, up, down, here, y0, y12, y3 = pieces
    for at, src in (
        (0, far_a[...]),
        (32, far_b[...]),
        (64, up[32:64]),
        (96, down[0:32]),
        (128, up[0:32]),
        (160, down[32:64]),
        (192, here[...]),
        (256, y0[...]),
        (320, y12[32:96]),
        (384, y12[0:32]),
        (416, y12[96:128]),
        (448, y3[...]),
    ):
        h_v[at : at + src.shape[0]] = src
    for n, side in enumerate((1 - p, p)):
        start = pl.multiple_of(first + 256 * side, 256)
        g_v[:256, 256 * n : 256 * n + 256] = g_own[:, pl.ds(start, 256)]
        g_v[256:, 256 * n : 256 * n + 256] = g_other[:, pl.ds(start, 256)]
    for f in range(0, 3696, 512):
        e = min(f + 512, 3696)
        out = lax.dot_general(
            h_v[:, f:e], g_v[...], (((0,), (0,)), ((), ())), preferred_element_type=f32
        )
        give[f:e] = out[:, :256].astype(bf16)
        keep[f:e] = out[:, 256:]


def outer(pieces, g_own, g_other, first, name):
    return call(
        functools.partial(outer_body, first=first),
        [sds((3696, 256), bf16), sds((3696, 256), f32)],
        (*pieces, g_own, g_other),
        scratch=[pltpu.VMEM((512, 3696), bf16), pltpu.VMEM((512, 512), bf16)],
        flops=512 * 1024 * 3696,
        moved=8 << 20,
        name=name,
        grant=28,
    )


def fold_body(own, other, *refs):
    *more, first, second = refs
    total = own[...] + other[...].astype(f32)
    for i, out in enumerate((first, second)):
        part = total[32 * i : 32 * i + 32]
        if more:
            part = part + more[i][...].astype(f32)
        out[...] = part.astype(bf16)


def fold(own, other, *more):
    return call(fold_body, [sds((32, own.shape[1]), bf16)] * 2, (own, other, *more))


def here_body(own, other, pure_a, pure_b, mixed_a, mixed_b, out):
    total = own[...] + other[...].astype(f32)
    for at, (one, two) in ((0, (pure_a, mixed_a)), (32, (pure_b, mixed_b))):
        part = total[at : at + 32] + one[...].astype(f32) + two[...].astype(f32)
        out[at : at + 32] = part.astype(bf16)


SHARES = ((0, 3696),)


def join_body(*refs):
    p = lax.axis_index("dp")
    out = refs[-1]
    n = len(SHARES)
    for (a, b), mine, other in zip(SHARES, refs[:n], refs[n : 2 * n]):
        out[a:b, pl.ds(pl.multiple_of(256 * p, 256), 256)] = mine[...]
        out[a:b, pl.ds(pl.multiple_of(256 * (1 - p), 256), 256)] = other[...]


def join(mine, other):
    return call(join_body, sds((3696, 512), bf16), (*mine, *other))


def per_device(stream, hidden, w_down, norm_gain, value_head, value_bias, rewards, segments):
    p = lax.axis_index("dp")
    smem = pl.BlockSpec(memory_space=pltpu.SMEM)
    vmem = pl.BlockSpec(memory_space=pltpu.VMEM)
    hbm = pl.BlockSpec(memory_space=pl.ANY)

    payload = call(
        prep_body,
        sds((144, 512), bf16),
        (stream, norm_gain[None], value_head[None], rewards, segments),
        in_specs=[hbm] * 5,
        scratch=[
            pltpu.VMEM((128, 512), bf16),
            pltpu.VMEM((1, 512), f32),
            pltpu.VMEM((1, 512), f32),
            pltpu.VMEM((1, 128), f32),
            pltpu.VMEM((1, 128), jnp.int32),
            pltpu.SemaphoreType.DMA((5,)),
        ],
        grant=56,
    )
    payload_mate = col(payload, MATE, "payload_mate")
    y3 = col(hidden, PAIR, "y3")
    down = col(hidden, ZUP, "down")
    up = col(hidden, ZDOWN, "up")

    w_half = lax.dynamic_slice_in_dim(w_down, p * HIGH, LO, 0)
    got = col(after(w_half, payload_mate), MATE, "got")

    block = jnp.concatenate([payload, payload_mate], 1)
    near, sums, owed = call(
        pick_body,
        (sds((144, 1024), bf16), sds((8, 128), f32), sds((8, 128), f32)),
        (block, row(block, XONE, "block_x1")),
    )
    away = row(near, XTHREE, "block_x3")
    here = jnp.concatenate([near, away], 0)
    there = row(here, ZLO, "block_zlo")
    owed_other = core(owed, "owed_other")

    gates = ((y3,), (down, up), (away,))
    for i, perm in enumerate((PAIR, ZONE, ZTHREE)):
        sums = after(sums, *gates[i])
        sums = sums + col(sums, perm, f"sums{i}")
        if i == 0:
            down, up = lax.optimization_barrier((down, up, sums))[:2]
            far_a = col(down[:32], ZUP, "far_a")
            far_b = col(up[32:], ZDOWN, "far_b")
            y12 = col(jnp.concatenate([up, down], 0), PAIR, "y12")
    y0 = col(after(jnp.concatenate([far_a, far_b], 0), sums), PAIR, "y0")
    tiny = jnp.concatenate([sums, owed, owed_other], 0)
    tiny = after(tiny, far_a, far_b)
    tiny = jnp.concatenate([tiny, row(tiny, XTHREE, "tiny_x3")], 0)
    tiny_zlo = row(tiny, ZLO, "tiny_zlo")
    coefs = call(
        coefs_body,
        sds((8, 128), f32),
        (after(tiny, got), tiny_zlo, value_bias),
        in_specs=[vmem, vmem, smem],
        scratch=[pltpu.VMEM((8, 128), f32)],
    )
    got_other = core(after(got, tiny_zlo), "got_other")
    coefs_mate = col(coefs, MATE, "coefs_mate")
    g_own, g_other = call(
        grad_body,
        (sds((256, 1024), bf16), sds((256, 1024), bf16)),
        (coefs, here, there),
        moved=4 << 20,
    )

    pieces = (far_a, far_b, up, down, hidden, y0, y12, y3)
    mate_give, mate_keep = outer(pieces, after(g_own, coefs_mate), g_other, 512, "outer_mate")
    mate_got = core(mate_give, "mate_got")
    w_send = [(mate_keep[a:b] + mate_got[a:b].astype(f32)).astype(bf16) for a, b in SHARES]
    w_recv = col(w_send[0], MATE, "w_recv")

    outs = call(
        inner_body,
        [sds((b - a, 3696), d) for d in (bf16, f32) for a, b in PARTS],
        (after(g_own, w_send[0]), g_other, w_down, got, got_other),
        in_specs=[vmem] * 2 + [hbm] * 3,
        scratch=[
            pltpu.VMEM((3696, 512), bf16),
            pltpu.VMEM((3696, 512), bf16),
            pltpu.SemaphoreType.DMA((6,)),
        ],
        flops=2 * 512 * 1024 * 3696,
        moved=13 << 20,
        grant=28,
    )
    sent, own = outs[:4], outs[4:]
    t = [col(sent[0], PAIR, "t0")]
    t += [col(after(sent[i], mate_got), PAIR, f"t{i}") for i in (1, 2)]

    stream_grad = call(
        own_grad_body, sds((128, 512), bf16), (after(stream, own[0]), near, coefs, coefs_mate)
    )
    q0a, q0b = fold(own[0], after(t[0], w_send[0]))
    from_down = col(q0a, ZUP, "from_down")
    from_up = col(q0b, ZDOWN, "from_up")
    q1b, q1a = fold(own[1], after(t[1], from_down, from_up))
    t.append(col(after(sent[3], q1a), PAIR, "t3"))
    give, keep = outer(pieces, g_own, g_other, 0, "outer_own")
    own_got = core(give, "own_got")
    pure_b = col(q1b, ZUP, "pure_b")
    pure_a = col(q1a, ZDOWN, "pure_a")
    q2a, q2b = fold(own[2], after(t[2], w_recv, pure_a, pure_b, stream_grad), from_down, from_up)
    mixed_a = col(q2a, ZUP, "mixed_a")
    mixed_b = col(q2b, ZDOWN, "mixed_b")
    hidden_grad = call(
        here_body, sds((64, 3696), bf16), (own[3], t[3], pure_a, pure_b, mixed_a, mixed_b)
    )

    keep = after(keep, q2a)
    w_sum = [
        (keep[a:b] + own_got[a:b].astype(f32) + w.astype(f32)).astype(bf16)
        for (a, b), w in zip(SHARES, (w_recv,))
    ]
    w_sum_other = [core(w, f"w_sum{i}") for i, w in enumerate(w_sum)]
    weight_grad = join(w_sum, w_sum_other)
    return weight_grad, hidden_grad, stream_grad


def solution(mesh):
    in_specs = (
        P(("dp", "row"), "col"),
        P(("dp", "col"), "row"),
        P("row", "col"),
        P("col"),
        P("col"),
        P(),
        P("dp", "row"),
        P("dp", "row"),
    )
    out_specs = (P("row", "col"), P(("dp", "col"), "row"), P(("dp", "row"), "col"))
    return jax.shard_map(
        per_device, mesh=mesh, in_specs=in_specs, out_specs=out_specs, check_vma=False
    )
```

```python
import functools

import jax
import jax.numpy as jnp
from jax import lax
from jax.experimental import pallas as pl
from jax.experimental.pallas import tpu as pltpu
from jax.sharding import PartitionSpec as P

loss_scale = 2097152.0
bf16, f32 = jnp.bfloat16, jnp.float32
WIDTH, COUNT = 8192.0, 2048.0

PAIR = [(c, c ^ 1) for c in range(16)]
MATE = [(c, c ^ 3) for c in range(16)]
ZUP = [(c, (c + 4) % 16) for c in range(16)]
ZDOWN = [(c, (c + 12) % 16) for c in range(16)]
ZONE = [(c, c ^ 4) for c in range(16)]
ZTHREE = [(c, c ^ 12) for c in range(16)]
ZLO = [(r, r ^ 4) for r in range(8)]
CORE = [(0, 1), (1, 0)]
XONE = [(r, r ^ 1) for r in range(8)]
XTHREE = [(r, r ^ 3) for r in range(8)]
MIB = 1024 * 1024


def send(a, axis, perm, name):
    with jax.named_scope(name):
        return lax.ppermute(a, axis, perm)


def col(a, perm, name):
    return send(a, "col", perm, name)


def row(a, perm, name):
    return send(a, "row", perm, name)


def core(a, name):
    return send(a, "dp", CORE, name)


def after(a, *others):
    return lax.optimization_barrier((a, *others))[0]


def sds(shape, dtype):
    return jax.ShapeDtypeStruct(shape, dtype)


def call(body, out_shape, args, in_specs=None, scratch=(), flops=0, moved=0, name=None, grant=16):
    extra = {} if in_specs is None else {"in_specs": in_specs}
    with jax.named_scope(name or getattr(body, "__name__", "mid")):
      return pl.pallas_call(
        body,
        out_shape=out_shape,
        scratch_shapes=list(scratch),
        compiler_params=pltpu.CompilerParams(vmem_limit_bytes=grant * MIB),
        cost_estimate=pl.CostEstimate(flops=flops, bytes_accessed=moved, transcendentals=0),
        **extra,
    )(*args)


def place():
    r, c = lax.axis_index("row"), lax.axis_index("col")
    return r % 4, r // 4, c % 4, c // 4


def prep_body(stream, gain, head, reward, segment, out, s_v, g_v, h_v, r_v, i_v, sems):
    moves = [
        pltpu.make_async_copy(src, dst, sems.at[i])
        for i, (src, dst) in enumerate(
            ((stream, s_v), (gain, g_v), (head, h_v), (reward, r_v), (segment, i_v))
        )
    ]
    for m in moves:
        m.start()
    for m in moves:
        m.wait()

    def parts(v):
        high = v.astype(bf16).astype(f32)
        mid = (v - high).astype(bf16).astype(f32)
        return high, mid, v - high - mid

    out[0:128] = s_v[...]
    rows = parts(g_v[...] * h_v[...])
    rows += (jnp.concatenate([*parts(r_v[...]), i_v[...].astype(f32)], 1),)
    line = lax.broadcasted_iota(jnp.int32, (16, 512), 0)
    extra = jnp.zeros((16, 512), f32)
    for i, a in enumerate(rows):
        extra = jnp.where(line == i, jnp.broadcast_to(a, (16, 512)), extra)
    out[128:144] = extra.astype(bf16)


def pick_body(own, other, out, sums, owed):
    x, _, y, _ = place()

    @pl.when(lax.rem(x, 2) == y // 2)
    def _():
        out[0:128] = own[0:128]

    @pl.when(lax.rem(x, 2) != y // 2)
    def _():
        out[0:128] = other[0:128]

    mine, theirs = own[128:144].astype(f32), other[128:144].astype(f32)
    even = lax.rem(x, 2) == 0
    first = jnp.where(even, mine, theirs)
    second = jnp.where(even, theirs, mine)
    for i, a in enumerate((first[3:4], second[3:4])):
        owed[i : i + 1] = a[:, 0:128] + a[:, 128:256] + a[:, 256:384]
        owed[2 + i : 3 + i] = a[:, 384:512]
    owed[4:8] = jnp.zeros((4, 128), f32)
    out[128:144] = mine.astype(bf16)
    gw = gains_of(own)

    def total(a):
        a = sum(a[:, 128 * i : 128 * i + 128] for i in range(8))
        return jnp.sum(a.T, axis=0, keepdims=True)

    v = out[0:128].astype(f32)
    sums[0:1] = total(v * v)
    sums[1:2] = total(v * gw)
    sums[2:8] = jnp.zeros((6, 128), f32)


def gains_of(block):
    extra = block[128:144].astype(f32)
    return extra[0:1] + extra[1:2] + extra[2:3]


def coefs_body(here, there, bias, out, target):
    x, zlo, y, _ = place()

    def side(src, at):
        near, away = src[at : at + 2], src[24 + at : 26 + at]
        low, high = jnp.where(x // 2 == 0, near, away), jnp.where(x // 2 == 0, away, near)
        return jnp.concatenate([low, high], 0)

    def rows(at):
        mine, theirs = side(here, at), side(there, at)
        return jnp.where(zlo == 0, mine, theirs), jnp.where(zlo == 0, theirs, mine)

    value = jnp.concatenate([*rows(8), *rows(16)], 0)
    segment = jnp.concatenate([*rows(10), *rows(18)], 0)
    shape = value.shape
    line = lax.broadcasted_iota(jnp.int32, shape, 0) % 8
    lane = lax.broadcasted_iota(jnp.int32, shape, 1)

    def ahead(a, step):
        if step >= 128:
            return pltpu.roll(a, shape[0] - step // 128, 0)
        here = pltpu.roll(a, 128 - step, 1)
        below = pltpu.roll(here, shape[0] - 1, 0)
        return jnp.where(lane + step < 128, here, below)

    step = 1
    while step < 1024:
        inside = line * 128 + lane + step < 1024
        same = inside & (ahead(segment, step) == segment)
        value = value + jnp.where(same, ahead(value, step), 0.0)
        step *= 2
    mean = jnp.sum(value) / COUNT
    off = value - mean
    spread = jnp.sum(off * off) / COUNT
    target[...] = (off / jnp.sqrt(jnp.broadcast_to(spread, shape) + 1e-05))[:8]
    wanted, sq, lin = [], [], []
    for i in range(4):
        zl = zlo if i < 2 else 1 - zlo
        b = x // 2 if i % 2 == 0 else 1 - x // 2
        wanted.append(target[pl.ds(4 * zl + 2 * b + y // 2, 1)])
        src = (here, there)[i // 2]
        at = 24 * (i % 2)
        sq.append(src[at : at + 1])
        lin.append(src[at + 1 : at + 2])
    wanted, sq, lin = (jnp.concatenate(a, 0) for a in (wanted, sq, lin))
    rms = jnp.sqrt(sq / WIDTH + 1e-05)
    head = lin / rms
    dvalue = loss_scale * (head + bias[0] - wanted) / COUNT
    out[0:4] = dvalue / rms
    out[4:8] = head / WIDTH / rms


def columns(coefs):
    padded = jnp.concatenate([coefs, jnp.zeros((120, 128), f32)], 0).T
    lane = lax.broadcasted_iota(jnp.int32, (128, 128), 1)

    def column(at):
        return jnp.sum(jnp.where(lane == at, padded, 0.0), axis=1, keepdims=True)

    return column


def formed(block, s, l, gains):
    return (s * (gains - block.astype(f32) * l)).astype(bf16)


def own_grad_body(stream, block, coefs, coefs_mate, grad):
    x, _, y, _ = place()
    column = columns(jnp.where(lax.rem(x, 2) == y // 2, coefs[...], coefs_mate[...]))
    grad[...] = formed(stream[...], column(0), column(4), gains_of(block)[:, :512])


def grad_body(coefs, here, there, g_own, g_other):
    x, zlo, y, zhi = place()
    odd = lax.rem(y, 2)
    column = columns(coefs[...])
    gains = gains_of(here)
    for k, spots in enumerate(((192, 224), (128, 64), (0, 32), (96, 160))):
        z = lax.rem(zhi + k, 4)
        zl, b = z // 2, lax.rem(z, 2)
        at = jnp.where(zl == zlo, 0, 2) + jnp.where(b == x // 2, 0, 1)
        s_all, l_all = column(at), column(4 + at)
        s_all = jnp.where(odd == 0, s_all, jnp.concatenate([s_all[64:], s_all[:64]], 0))
        l_all = jnp.where(odd == 0, l_all, jnp.concatenate([l_all[64:], l_all[:64]], 0))
        start = jnp.where(b == x // 2, 0, 144)
        for same, src in ((True, here), (False, there)):

            @pl.when((zl == zlo) == same)
            def _(src=src, s_all=s_all, l_all=l_all, start=start, spots=spots):
                for who, out in ((0, g_own), (1, g_other)):
                    parity = odd if who == 0 else 1 - odd
                    first = pl.multiple_of(start + 64 * parity, 16)
                    rows = slice(64 * who, 64 * who + 64)
                    made = formed(src[pl.ds(first, 64)], s_all[rows], l_all[rows], gains)
                    for i, spot in enumerate(spots):
                        out[spot : spot + 32] = made[32 * i : 32 * i + 32]


LO = 1856
CHUNKS = ((0, 1024), (1024, 2048), (2048, 3072), (3072, 3696))
HIGH = 3696 - LO
SPANS = ((0, LO), (LO, 3696))
PARTS = ((0, 64), (64, 128), (128, 192), (192, 256))
def inner_body(*refs):
    g_own, g_other, w, got, other = refs[:5]
    sent, own, (w_v, m_v, sems) = refs[5:9], refs[9:13], refs[13:]
    p = lax.axis_index("dp")
    for i, (a, b) in enumerate(CHUNKS):
        pltpu.make_async_copy(w.at[a:b], w_v.at[a:b], sems.at[i]).start()

    def mate_copy(j, low, high):
        a, b = SPANS[j]
        src, off = (low, high)[j], (0, HIGH)[j]
        return pltpu.make_async_copy(src.at[a - off : b - off], m_v.at[a:b], sems.at[4 + j])

    @pl.when(p == 0)
    def _():
        for j in range(2):
            mate_copy(j, got, other).start()

    @pl.when(p == 1)
    def _():
        for j in range(2):
            mate_copy(j, other, got).start()

    left = jnp.concatenate([g_other[:, :512], g_own[:, :512]], 0)
    right = jnp.concatenate([g_other[:, 512:], g_own[:, 512:]], 0)
    nt = (((1,), (1,)), ((), ()))
    waits = ((0,), (1,), (), ())
    for i, (a, b) in enumerate(CHUNKS):
        pltpu.make_async_copy(w.at[a:b], w_v.at[a:b], sems.at[i]).wait()
        for j in waits[i]:
            mate_copy(j, other, other).wait()
        for f in range(a, b, 512):
            e = min(f + 512, b)
            out = lax.dot_general(left, w_v[f:e], nt, preferred_element_type=f32)
            out = out + lax.dot_general(right, m_v[f:e], nt, preferred_element_type=f32)
            for n, (low, high) in enumerate(PARTS):
                sent[n][:, f:e] = out[low:high].astype(bf16)
                own[n][:, f:e] = out[256 + low : 256 + high]


def outer_body(*refs, first, split):
    (far_a, far_b, up, down, here, y0, y12, y3), (g_own, g_other) = refs[:8], refs[8:10]
    *outs, h_v, g_v = refs[10:]
    p = lax.axis_index("dp")
    for at, src in (
        (0, far_a[...]),
        (32, far_b[...]),
        (64, up[32:64]),
        (96, down[0:32]),
        (128, up[0:32]),
        (160, down[32:64]),
        (192, here[...]),
        (256, y0[...]),
        (320, y12[32:96]),
        (384, y12[0:32]),
        (416, y12[96:128]),
        (448, y3[...]),
    ):
        h_v[at : at + src.shape[0]] = src
    for n, side in enumerate((1 - p, p) if split else (0, 1)):
        start = pl.multiple_of(first + 256 * side, 256)
        g_v[:256, 256 * n : 256 * n + 256] = g_own[:, pl.ds(start, 256)]
        g_v[256:, 256 * n : 256 * n + 256] = g_other[:, pl.ds(start, 256)]
    for f in range(0, 3696, 512):
        e = min(f + 512, 3696)
        out = lax.dot_general(
            h_v[:, f:e], g_v[...], (((0,), (0,)), ((), ())), preferred_element_type=f32
        )
        if split:
            outs[0][f:e] = out[:, :256].astype(bf16)
            outs[1][f:e] = out[:, 256:]
        else:
            outs[0][f:e] = out


def outer(pieces, g_own, g_other, first, split, name):
    out = [sds((3696, 256), bf16), sds((3696, 256), f32)] if split else sds((3696, 512), f32)
    return call(
        functools.partial(outer_body, first=first, split=split),
        out,
        (*pieces, g_own, g_other),
        scratch=[pltpu.VMEM((512, 3696), bf16), pltpu.VMEM((512, 512), bf16)],
        flops=512 * 1024 * 3696,
        moved=8 << 20,
        name=name,
        grant=28,
    )


def fold_body(own, other, *refs):
    *more, first, second = refs
    total = own[...] + other[...].astype(f32)
    for i, out in enumerate((first, second)):
        part = total[32 * i : 32 * i + 32]
        if more:
            part = part + more[i][...].astype(f32)
        out[...] = part.astype(bf16)


def fold(own, other, *more):
    return call(fold_body, [sds((32, own.shape[1]), bf16)] * 2, (own, other, *more))


def here_body(own, other, pure_a, pure_b, mixed_a, mixed_b, out):
    total = own[...] + other[...].astype(f32)
    for at, (one, two) in ((0, (pure_a, mixed_a)), (32, (pure_b, mixed_b))):
        part = total[at : at + 32] + one[...].astype(f32) + two[...].astype(f32)
        out[at : at + 32] = part.astype(bf16)


def merge_body(partial, recv, out):
    p = lax.axis_index("dp")
    mine = pl.ds(pl.multiple_of(256 * p, 256), 256)
    rest = pl.ds(pl.multiple_of(256 * (1 - p), 256), 256)
    out[:, mine] = (partial[:, mine] + recv[...].astype(f32)).astype(bf16)
    out[:, rest] = partial[:, rest].astype(bf16)


def per_device(stream, hidden, w_down, norm_gain, value_head, value_bias, rewards, segments):
    p = lax.axis_index("dp")
    smem = pl.BlockSpec(memory_space=pltpu.SMEM)
    vmem = pl.BlockSpec(memory_space=pltpu.VMEM)
    hbm = pl.BlockSpec(memory_space=pl.ANY)

    payload = call(
        prep_body,
        sds((144, 512), bf16),
        (stream, norm_gain[None], value_head[None], rewards, segments),
        in_specs=[hbm] * 5,
        scratch=[
            pltpu.VMEM((128, 512), bf16),
            pltpu.VMEM((1, 512), f32),
            pltpu.VMEM((1, 512), f32),
            pltpu.VMEM((1, 128), f32),
            pltpu.VMEM((1, 128), jnp.int32),
            pltpu.SemaphoreType.DMA((5,)),
        ],
        grant=56,
    )
    payload_mate = col(payload, MATE, "payload_mate")
    ready = after(hidden, payload)
    y3 = col(ready, PAIR, "y3")
    down = col(ready, ZUP, "down")
    up = col(ready, ZDOWN, "up")

    w_half = lax.dynamic_slice_in_dim(w_down, p * HIGH, LO, 0)
    got = col(after(w_half, payload_mate), MATE, "got")

    block = jnp.concatenate([payload, payload_mate], 1)
    near, sums, owed = call(
        pick_body,
        (sds((144, 1024), bf16), sds((8, 128), f32), sds((8, 128), f32)),
        (block, row(block, XONE, "block_x1")),
    )
    away = row(near, XTHREE, "block_x3")
    here = jnp.concatenate([near, away], 0)
    there = row(here, ZLO, "block_zlo")
    owed_other = core(owed, "owed_other")

    gates = ((y3,), (down, up), (away,))
    for i, perm in enumerate((PAIR, ZONE, ZTHREE)):
        sums = after(sums, *gates[i])
        sums = sums + col(sums, perm, f"sums{i}")
        if i == 0:
            down, up = lax.optimization_barrier((down, up, sums))[:2]
            far_a = col(down[:32], ZUP, "far_a")
            far_b = col(up[32:], ZDOWN, "far_b")
            y12 = col(jnp.concatenate([up, down], 0), PAIR, "y12")
    y0 = col(after(jnp.concatenate([far_a, far_b], 0), sums), PAIR, "y0")
    tiny = jnp.concatenate([sums, owed, owed_other], 0)
    tiny = after(tiny, far_a, far_b)
    tiny = jnp.concatenate([tiny, row(tiny, XTHREE, "tiny_x3")], 0)
    tiny_zlo = row(tiny, ZLO, "tiny_zlo")
    coefs = call(
        coefs_body,
        sds((8, 128), f32),
        (after(tiny, got), tiny_zlo, value_bias),
        in_specs=[vmem, vmem, smem],
        scratch=[pltpu.VMEM((8, 128), f32)],
    )
    got_other = core(after(got, tiny_zlo), "got_other")
    coefs_mate = col(coefs, MATE, "coefs_mate")
    g_own, g_other = call(
        grad_body,
        (sds((256, 1024), bf16), sds((256, 1024), bf16)),
        (coefs, here, there),
        moved=4 << 20,
    )

    pieces = (far_a, far_b, up, down, hidden, y0, y12, y3)
    mate_give, mate_keep = outer(pieces, after(g_own, coefs_mate), g_other, 512, True, "outer_mate")
    mate_got = core(mate_give, "mate_got")
    outs = call(
        inner_body,
        [sds((b - a, 3696), d) for d in (bf16, f32) for a, b in PARTS],
        (after(g_own, mate_keep), g_other, w_down, got, got_other),
        in_specs=[vmem] * 2 + [hbm] * 3,
        scratch=[
            pltpu.VMEM((3696, 512), bf16),
            pltpu.VMEM((3696, 512), bf16),
            pltpu.SemaphoreType.DMA((6,)),
        ],
        flops=2 * 512 * 1024 * 3696,
        moved=13 << 20,
        grant=28,
    )
    sent, own = outs[:4], outs[4:]
    t = [col(a, PAIR, f"t{i}") for i, a in enumerate(sent)]
    w_send = (after(mate_keep, own[0]) + mate_got.astype(f32)).astype(bf16)
    w_recv = col(w_send, MATE, "w_recv")

    stream_grad = call(
        own_grad_body, sds((128, 512), bf16), (after(stream, own[0]), near, coefs, coefs_mate)
    )
    q0a, q0b = fold(own[0], after(t[0], w_send))
    from_down = col(q0a, ZUP, "from_down")
    from_up = col(q0b, ZDOWN, "from_up")
    partial = outer(pieces, after(g_own, q0a), g_other, 0, False, "outer_own")
    q1b, q1a = fold(own[1], after(t[1], partial, from_down, from_up))
    pure_b = col(q1b, ZUP, "pure_b")
    pure_a = col(q1a, ZDOWN, "pure_a")
    q2a, q2b = fold(own[2], after(t[2], w_recv, pure_a, pure_b, stream_grad), from_down, from_up)
    mixed_a = col(q2a, ZUP, "mixed_a")
    mixed_b = col(q2b, ZDOWN, "mixed_b")
    part = call(merge_body, sds((3696, 512), bf16), (after(partial, q2a), w_recv))
    part_other = core(part, "part")
    weight_grad = (part.astype(f32) + part_other.astype(f32)).astype(bf16)
    hidden_grad = call(
        here_body,
        sds((64, 3696), bf16),
        (after(own[3], weight_grad), t[3], pure_a, pure_b, mixed_a, mixed_b),
    )
    return weight_grad, hidden_grad, stream_grad


def solution(mesh):
    in_specs = (
        P(("dp", "row"), "col"),
        P(("dp", "col"), "row"),
        P("row", "col"),
        P("col"),
        P("col"),
        P(),
        P("dp", "row"),
        P("dp", "row"),
    )
    out_specs = (P("row", "col"), P(("dp", "col"), "row"), P(("dp", "row"), "col"))
    return jax.shard_map(
        per_device, mesh=mesh, in_specs=in_specs, out_specs=out_specs, check_vma=False
    )
```

```python
import functools

import jax
import jax.numpy as jnp
from jax import lax
from jax.experimental import pallas as pl
from jax.experimental.pallas import tpu as pltpu
from jax.sharding import PartitionSpec as P

loss_scale = 2097152.0
bf16, f32 = jnp.bfloat16, jnp.float32
WIDTH, COUNT = 8192.0, 2048.0

PAIR = [(c, c ^ 1) for c in range(16)]
MATE = [(c, c ^ 3) for c in range(16)]
ZUP = [(c, (c + 4) % 16) for c in range(16)]
ZDOWN = [(c, (c + 12) % 16) for c in range(16)]
ZONE = [(c, c ^ 4) for c in range(16)]
ZTHREE = [(c, c ^ 12) for c in range(16)]
ZLO = [(r, r ^ 4) for r in range(8)]
CORE = [(0, 1), (1, 0)]
XONE = [(r, r ^ 1) for r in range(8)]
XTHREE = [(r, r ^ 3) for r in range(8)]
MIB = 1024 * 1024


def send(a, axis, perm, name):
    with jax.named_scope(name):
        return lax.ppermute(a, axis, perm)


def col(a, perm, name):
    return send(a, "col", perm, name)


def row(a, perm, name):
    return send(a, "row", perm, name)


def core(a, name):
    return send(a, "dp", CORE, name)


def after(a, *others):
    return lax.optimization_barrier((a, *others))[0]


def sds(shape, dtype):
    return jax.ShapeDtypeStruct(shape, dtype)


def call(body, out_shape, args, in_specs=None, scratch=(), flops=0, moved=0, name=None, grant=16):
    extra = {} if in_specs is None else {"in_specs": in_specs}
    with jax.named_scope(name or getattr(body, "__name__", "mid")):
      return pl.pallas_call(
        body,
        out_shape=out_shape,
        scratch_shapes=list(scratch),
        compiler_params=pltpu.CompilerParams(vmem_limit_bytes=grant * MIB),
        cost_estimate=pl.CostEstimate(flops=flops, bytes_accessed=moved, transcendentals=0),
        **extra,
    )(*args)


def place():
    r, c = lax.axis_index("row"), lax.axis_index("col")
    return r % 4, r // 4, c % 4, c // 4


def prep_body(stream, gain, head, reward, segment, out, owed, s_v, g_v, h_v, r_v, i_v, sems):
    moves = [
        pltpu.make_async_copy(src, dst, sems.at[i])
        for i, (src, dst) in enumerate(
            ((stream, s_v), (gain, g_v), (head, h_v), (reward, r_v), (segment, i_v))
        )
    ]
    for m in moves:
        m.start()
    for m in moves:
        m.wait()

    def parts(v):
        high = v.astype(bf16).astype(f32)
        mid = (v - high).astype(bf16).astype(f32)
        return high, mid, v - high - mid

    out[0:128] = s_v[...]
    rows = parts(g_v[...] * h_v[...])
    rows += (jnp.concatenate([*parts(r_v[...]), i_v[...].astype(f32)], 1),)
    line = lax.broadcasted_iota(jnp.int32, (16, 512), 0)
    extra = jnp.zeros((16, 512), f32)
    for i, a in enumerate(rows):
        extra = jnp.where(line == i, jnp.broadcast_to(a, (16, 512)), extra)
    out[128:144] = extra.astype(bf16)
    owed[...] = jnp.zeros(owed.shape, f32)
    for i, a in enumerate(rows[3:]):
        for j in range(4):
            owed[4 * i + j : 4 * i + j + 1] = a[:, 128 * j : 128 * j + 128]


def wide_body(own, mate, owed, out):
    out[:, :512] = own[...]
    out[:, 512:] = mate[...]
    extra = own[128:144].astype(f32)
    theirs = jnp.concatenate([owed[i : i + 1] for i in range(4)], 1)
    line = lax.broadcasted_iota(jnp.int32, extra.shape, 0)
    extra = jnp.where(line == 4, jnp.broadcast_to(theirs, extra.shape), extra)
    out[128:144, :512] = extra.astype(bf16)


def pick_body(own, other, out, sums, owed):
    x, _, y, _ = place()

    @pl.when(lax.rem(x, 2) == y // 2)
    def _():
        out[0:128] = own[0:128]

    @pl.when(lax.rem(x, 2) != y // 2)
    def _():
        out[0:128] = other[0:128]

    mine, theirs = own[128:144].astype(f32), other[128:144].astype(f32)
    even = lax.rem(x, 2) == 0
    first = jnp.where(even, mine, theirs)
    second = jnp.where(even, theirs, mine)
    for i, a in enumerate((first[3:4], second[3:4], first[4:5], second[4:5])):
        at = (0, 1, 4, 5)[i]
        owed[at : at + 1] = a[:, 0:128] + a[:, 128:256] + a[:, 256:384]
        owed[2 + at : 3 + at] = a[:, 384:512]
    out[128:144] = mine.astype(bf16)
    gw = gains_of(own)

    def total(a):
        a = sum(a[:, 128 * i : 128 * i + 128] for i in range(8))
        return jnp.sum(a.T, axis=0, keepdims=True)

    v = out[0:128].astype(f32)
    sums[0:1] = total(v * v)
    sums[1:2] = total(v * gw)
    sums[2:8] = jnp.zeros((6, 128), f32)


def gains_of(block):
    extra = block[128:144].astype(f32)
    return extra[0:1] + extra[1:2] + extra[2:3]


def coefs_body(here, there, bias, out, target):
    x, zlo, y, _ = place()

    def side(src, at):
        near, away = src[at : at + 2], src[16 + at : 18 + at]
        low, high = jnp.where(x // 2 == 0, near, away), jnp.where(x // 2 == 0, away, near)
        return jnp.concatenate([low, high], 0)

    def rows(at):
        mine, theirs = side(here, at), side(there, at)
        return jnp.where(zlo == 0, mine, theirs), jnp.where(zlo == 0, theirs, mine)

    value = jnp.concatenate([*rows(8), *rows(12)], 0)
    segment = jnp.concatenate([*rows(10), *rows(14)], 0)
    shape = value.shape
    line = lax.broadcasted_iota(jnp.int32, shape, 0) % 8
    lane = lax.broadcasted_iota(jnp.int32, shape, 1)

    def ahead(a, step):
        if step >= 128:
            return pltpu.roll(a, shape[0] - step // 128, 0)
        here = pltpu.roll(a, 128 - step, 1)
        below = pltpu.roll(here, shape[0] - 1, 0)
        return jnp.where(lane + step < 128, here, below)

    step = 1
    while step < 1024:
        inside = line * 128 + lane + step < 1024
        same = inside & (ahead(segment, step) == segment)
        value = value + jnp.where(same, ahead(value, step), 0.0)
        step *= 2
    mean = jnp.sum(value) / COUNT
    off = value - mean
    spread = jnp.sum(off * off) / COUNT
    target[...] = (off / jnp.sqrt(jnp.broadcast_to(spread, shape) + 1e-05))[:8]
    wanted, sq, lin = [], [], []
    for i in range(4):
        zl = zlo if i < 2 else 1 - zlo
        b = x // 2 if i % 2 == 0 else 1 - x // 2
        wanted.append(target[pl.ds(4 * zl + 2 * b + y // 2, 1)])
        src = (here, there)[i // 2]
        at = 16 * (i % 2)
        sq.append(src[at : at + 1])
        lin.append(src[at + 1 : at + 2])
    wanted, sq, lin = (jnp.concatenate(a, 0) for a in (wanted, sq, lin))
    rms = jnp.sqrt(sq / WIDTH + 1e-05)
    head = lin / rms
    dvalue = loss_scale * (head + bias[0] - wanted) / COUNT
    out[0:4] = dvalue / rms
    out[4:8] = head / WIDTH / rms


def columns(coefs):
    padded = jnp.concatenate([coefs, jnp.zeros((120, 128), f32)], 0).T
    lane = lax.broadcasted_iota(jnp.int32, (128, 128), 1)

    def column(at):
        return jnp.sum(jnp.where(lane == at, padded, 0.0), axis=1, keepdims=True)

    return column


def formed(block, s, l, gains):
    return (s * (gains - block.astype(f32) * l)).astype(bf16)


def own_grad_body(stream, block, coefs, coefs_mate, grad):
    x, _, y, _ = place()
    column = columns(jnp.where(lax.rem(x, 2) == y // 2, coefs[...], coefs_mate[...]))
    grad[...] = formed(stream[...], column(0), column(4), gains_of(block)[:, :512])


def grad_body(coefs, here, there, g_own, g_other):
    x, zlo, y, zhi = place()
    odd = lax.rem(y, 2)
    column = columns(coefs[...])
    gains = gains_of(here)
    for k, spots in enumerate(((192, 224), (128, 64), (0, 32), (96, 160))):
        z = lax.rem(zhi + k, 4)
        zl, b = z // 2, lax.rem(z, 2)
        at = jnp.where(zl == zlo, 0, 2) + jnp.where(b == x // 2, 0, 1)
        s_all, l_all = column(at), column(4 + at)
        s_all = jnp.where(odd == 0, s_all, jnp.concatenate([s_all[64:], s_all[:64]], 0))
        l_all = jnp.where(odd == 0, l_all, jnp.concatenate([l_all[64:], l_all[:64]], 0))
        start = jnp.where(b == x // 2, 0, 144)
        for same, src in ((True, here), (False, there)):

            @pl.when((zl == zlo) == same)
            def _(src=src, s_all=s_all, l_all=l_all, start=start, spots=spots):
                for who, out in ((0, g_own), (1, g_other)):
                    parity = odd if who == 0 else 1 - odd
                    first = pl.multiple_of(start + 64 * parity, 16)
                    rows = slice(64 * who, 64 * who + 64)
                    made = formed(src[pl.ds(first, 64)], s_all[rows], l_all[rows], gains)
                    for i, spot in enumerate(spots):
                        out[spot : spot + 32] = made[32 * i : 32 * i + 32]


LO = 1856
CHUNKS = ((0, 1024), (1024, 2048), (2048, 3072), (3072, 3696))
HIGH = 3696 - LO
SPANS = ((0, LO), (LO, 3696))
def inner_body(g, w, got, other, *refs):
    out, (w_v, m_v, sems) = refs[:4], refs[4:]
    p = lax.axis_index("dp")
    for i, (a, b) in enumerate(CHUNKS):
        pltpu.make_async_copy(w.at[a:b], w_v.at[a:b], sems.at[i]).start()

    def mate_copy(j, low, high):
        a, b = SPANS[j]
        src, off = (low, high)[j], (0, HIGH)[j]
        return pltpu.make_async_copy(src.at[a - off : b - off], m_v.at[a:b], sems.at[4 + j])

    @pl.when(p == 0)
    def _():
        for j in range(2):
            mate_copy(j, got, other).start()

    @pl.when(p == 1)
    def _():
        for j in range(2):
            mate_copy(j, other, got).start()

    left, right = g[:, :512], g[:, 512:]
    nt = (((1,), (1,)), ((), ()))
    waits = ((0,), (1,), (), ())
    for i, (a, b) in enumerate(CHUNKS):
        pltpu.make_async_copy(w.at[a:b], w_v.at[a:b], sems.at[i]).wait()
        for j in waits[i]:
            mate_copy(j, other, other).wait()
        for f in range(a, b, 512):
            e = min(f + 512, b)
            made = lax.dot_general(left, w_v[f:e], nt, preferred_element_type=f32)
            made = made + lax.dot_general(right, m_v[f:e], nt, preferred_element_type=f32)
            for n, o in enumerate(out):
                o[:, f:e] = made[64 * n : 64 * n + 64].astype(o.dtype)


def inner(g, w, got, other, dtype, name):
    hbm = pl.BlockSpec(memory_space=pl.ANY)
    return call(
        inner_body,
        [sds((64, 3696), dtype)] * 4,
        (g, w, got, other),
        in_specs=[pl.BlockSpec(memory_space=pltpu.VMEM)] + [hbm] * 3,
        scratch=[
            pltpu.VMEM((3696, 512), bf16),
            pltpu.VMEM((3696, 512), bf16),
            pltpu.SemaphoreType.DMA((6,)),
        ],
        flops=2 * 256 * 1024 * 3696,
        moved=10 << 20,
        name=name,
        grant=24,
    )


def outer_body(*refs, first, split):
    (far_a, far_b, up, down, here, y0, y12, y3), (g_own, g_other) = refs[:8], refs[8:10]
    *outs, h_v, g_v = refs[10:]
    p = lax.axis_index("dp")
    for at, src in (
        (0, far_a[...]),
        (32, far_b[...]),
        (64, up[32:64]),
        (96, down[0:32]),
        (128, up[0:32]),
        (160, down[32:64]),
        (192, here[...]),
        (256, y0[...]),
        (320, y12[32:96]),
        (384, y12[0:32]),
        (416, y12[96:128]),
        (448, y3[...]),
    ):
        h_v[at : at + src.shape[0]] = src
    for n, side in enumerate((1 - p, p) if split else (0, 1)):
        start = pl.multiple_of(first + 256 * side, 256)
        g_v[:256, 256 * n : 256 * n + 256] = g_own[:, pl.ds(start, 256)]
        g_v[256:, 256 * n : 256 * n + 256] = g_other[:, pl.ds(start, 256)]
    for f in range(0, 3696, 512):
        e = min(f + 512, 3696)
        out = lax.dot_general(
            h_v[:, f:e], g_v[...], (((0,), (0,)), ((), ())), preferred_element_type=f32
        )
        if split:
            outs[0][f:e] = out[:, :256].astype(bf16)
            outs[1][f:e] = out[:, 256:]
        else:
            outs[0][f:e] = out


def outer(pieces, g_own, g_other, first, split, name):
    out = [sds((3696, 256), bf16), sds((3696, 256), f32)] if split else sds((3696, 512), f32)
    return call(
        functools.partial(outer_body, first=first, split=split),
        out,
        (*pieces, g_own, g_other),
        scratch=[pltpu.VMEM((512, 3696), bf16), pltpu.VMEM((512, 512), bf16)],
        flops=512 * 1024 * 3696,
        moved=8 << 20,
        name=name,
        grant=28,
    )


def fold_body(own, other, *refs):
    *more, first, second = refs
    total = own[...] + other[...].astype(f32)
    for i, out in enumerate((first, second)):
        part = total[32 * i : 32 * i + 32]
        if more:
            part = part + more[i][...].astype(f32)
        out[...] = part.astype(bf16)


def fold(own, other, *more):
    return call(fold_body, [sds((32, own.shape[1]), bf16)] * 2, (own, other, *more))


def here_body(own, other, pure_a, pure_b, mixed_a, mixed_b, out):
    total = own[...] + other[...].astype(f32)
    for at, (one, two) in ((0, (pure_a, mixed_a)), (32, (pure_b, mixed_b))):
        part = total[at : at + 32] + one[...].astype(f32) + two[...].astype(f32)
        out[at : at + 32] = part.astype(bf16)


def merge_body(partial, recv, out):
    p = lax.axis_index("dp")
    mine = pl.ds(pl.multiple_of(256 * p, 256), 256)
    rest = pl.ds(pl.multiple_of(256 * (1 - p), 256), 256)
    out[:, mine] = (partial[:, mine] + recv[...].astype(f32)).astype(bf16)
    out[:, rest] = partial[:, rest].astype(bf16)


def per_device(stream, hidden, w_down, norm_gain, value_head, value_bias, rewards, segments):
    p = lax.axis_index("dp")
    smem = pl.BlockSpec(memory_space=pltpu.SMEM)
    vmem = pl.BlockSpec(memory_space=pltpu.VMEM)
    hbm = pl.BlockSpec(memory_space=pl.ANY)

    payload, owed = call(
        prep_body,
        (sds((144, 512), bf16), sds((8, 128), f32)),
        (stream, norm_gain[None], value_head[None], rewards, segments),
        in_specs=[hbm] * 5,
        scratch=[
            pltpu.VMEM((128, 512), bf16),
            pltpu.VMEM((1, 512), f32),
            pltpu.VMEM((1, 512), f32),
            pltpu.VMEM((1, 128), f32),
            pltpu.VMEM((1, 128), jnp.int32),
            pltpu.SemaphoreType.DMA((5,)),
        ],
        grant=56,
    )
    payload_mate = col(payload, MATE, "payload_mate")
    ready = after(hidden, payload)
    y3 = col(ready, PAIR, "y3")
    down = col(ready, ZUP, "down")
    up = col(ready, ZDOWN, "up")

    w_half = lax.dynamic_slice_in_dim(w_down, p * HIGH, LO, 0)
    got = col(after(w_half, payload_mate), MATE, "got")

    owed_other = core(owed, "owed_other")
    block = call(wide_body, sds((144, 1024), bf16), (payload, payload_mate, owed_other))
    near, sums, owed = call(
        pick_body,
        (sds((144, 1024), bf16), sds((8, 128), f32), sds((8, 128), f32)),
        (block, row(block, XONE, "block_x1")),
    )
    away = row(near, XTHREE, "block_x3")
    here = jnp.concatenate([near, away], 0)
    there = row(here, ZLO, "block_zlo")

    gates = ((y3,), (down, up), (away,))
    for i, perm in enumerate((PAIR, ZONE, ZTHREE)):
        sums = after(sums, *gates[i])
        sums = sums + col(sums, perm, f"sums{i}")
        if i == 0:
            down, up = lax.optimization_barrier((down, up, sums))[:2]
            far_b = col(up[32:], ZDOWN, "far_b")
            y12 = col(jnp.concatenate([up, down], 0), PAIR, "y12")
        if i == 1:
            far_a = col(after(down[:32], sums), ZUP, "far_a")
    y0 = col(after(jnp.concatenate([far_a, far_b], 0), sums), PAIR, "y0")
    tiny = jnp.concatenate([sums, owed], 0)
    tiny = after(tiny, far_a, far_b)
    tiny = jnp.concatenate([tiny, row(tiny, XTHREE, "tiny_x3")], 0)
    tiny_zlo = row(tiny, ZLO, "tiny_zlo")
    coefs = call(
        coefs_body,
        sds((8, 128), f32),
        (after(tiny, got), tiny_zlo, value_bias),
        in_specs=[vmem, vmem, smem],
        scratch=[pltpu.VMEM((8, 128), f32)],
    )
    got_other = core(after(got, tiny_zlo), "got_other")
    coefs_mate = col(coefs, MATE, "coefs_mate")
    g_own, g_other = call(
        grad_body,
        (sds((256, 1024), bf16), sds((256, 1024), bf16)),
        (coefs, here, there),
        moved=4 << 20,
    )

    pieces = (far_a, far_b, up, down, hidden, y0, y12, y3)
    mate_give, mate_keep = outer(pieces, after(g_own, coefs_mate), g_other, 512, True, "outer_mate")
    mate_got = core(mate_give, "mate_got")
    sent = inner(after(g_other, mate_keep), w_down, got, got_other, bf16, "inner_sent")
    own = inner(after(g_own, sent[0]), w_down, got, got_other, f32, "inner_own")
    t = [col(a, PAIR, f"t{i}") for i, a in enumerate(sent)]
    w_send = (after(mate_keep, sent[0]) + mate_got.astype(f32)).astype(bf16)
    w_recv = col(w_send, MATE, "w_recv")

    q0a, q0b = fold(own[0], after(t[0], w_send))
    from_down = col(q0a, ZUP, "from_down")
    from_up = col(q0b, ZDOWN, "from_up")
    stream_grad = call(
        own_grad_body, sds((128, 512), bf16), (after(stream, q0a), near, coefs, coefs_mate)
    )
    partial = outer(pieces, after(g_own, q0a), g_other, 0, False, "outer_own")
    q1b, q1a = fold(own[1], after(t[1], partial, from_up))
    pure_b = col(q1b, ZUP, "pure_b")
    pure_a = col(q1a, ZDOWN, "pure_a")
    q2a, q2b = fold(own[2], after(t[2], stream_grad), from_down, from_up)
    q2a, q2b, pure_a, pure_b = lax.optimization_barrier((q2a, q2b, pure_a, pure_b))
    mixed_a = col(q2a, ZUP, "mixed_a")
    mixed_b = col(q2b, ZDOWN, "mixed_b")
    part = call(
        merge_body, sds((3696, 512), bf16), (after(partial, mixed_a, mixed_b, t[3]), w_recv)
    )
    part_other = core(part, "part")
    weight_grad = (part.astype(f32) + part_other.astype(f32)).astype(bf16)
    hidden_grad = call(
        here_body,
        sds((64, 3696), bf16),
        (own[3], t[3], pure_a, pure_b, mixed_a, mixed_b),
    )
    return weight_grad, hidden_grad, stream_grad


def solution(mesh):
    in_specs = (
        P(("dp", "row"), "col"),
        P(("dp", "col"), "row"),
        P("row", "col"),
        P("col"),
        P("col"),
        P(),
        P("dp", "row"),
        P("dp", "row"),
    )
    out_specs = (P("row", "col"), P(("dp", "col"), "row"), P(("dp", "row"), "col"))
    return jax.shard_map(
        per_device, mesh=mesh, in_specs=in_specs, out_specs=out_specs, check_vma=False
    )
```

```python
import functools

import jax
import jax.numpy as jnp
from jax import lax
from jax.experimental import pallas as pl
from jax.experimental.pallas import tpu as pltpu
from jax.sharding import PartitionSpec as P

loss_scale = 2097152.0
bf16, f32 = jnp.bfloat16, jnp.float32
WIDTH, COUNT = 8192.0, 2048.0

PAIR = [(c, c ^ 1) for c in range(16)]
MATE = [(c, c ^ 3) for c in range(16)]
ZUP = [(c, (c + 4) % 16) for c in range(16)]
ZDOWN = [(c, (c + 12) % 16) for c in range(16)]
ZONE = [(c, c ^ 4) for c in range(16)]
ZTHREE = [(c, c ^ 12) for c in range(16)]
ZLO = [(r, r ^ 4) for r in range(8)]
CORE = [(0, 1), (1, 0)]
XONE = [(r, r ^ 1) for r in range(8)]
XTHREE = [(r, r ^ 3) for r in range(8)]
MIB = 1024 * 1024


def send(a, axis, perm, name):
    with jax.named_scope(name):
        return lax.ppermute(a, axis, perm)


def col(a, perm, name):
    return send(a, "col", perm, name)


def row(a, perm, name):
    return send(a, "row", perm, name)


def core(a, name):
    return send(a, "dp", CORE, name)


def after(a, *others):
    return lax.optimization_barrier((a, *others))[0]


def sds(shape, dtype):
    return jax.ShapeDtypeStruct(shape, dtype)


def call(body, out_shape, args, in_specs=None, scratch=(), flops=0, moved=0, name=None, grant=16):
    extra = {} if in_specs is None else {"in_specs": in_specs}
    with jax.named_scope(name or getattr(body, "__name__", "mid")):
      return pl.pallas_call(
        body,
        out_shape=out_shape,
        scratch_shapes=list(scratch),
        compiler_params=pltpu.CompilerParams(vmem_limit_bytes=grant * MIB),
        cost_estimate=pl.CostEstimate(flops=flops, bytes_accessed=moved, transcendentals=0),
        **extra,
    )(*args)


def place():
    r, c = lax.axis_index("row"), lax.axis_index("col")
    return r % 4, r // 4, c % 4, c // 4


def prep_body(stream, gain, head, reward, segment, out, s_v, g_v, h_v, r_v, i_v, sems):
    moves = [
        pltpu.make_async_copy(src, dst, sems.at[i])
        for i, (src, dst) in enumerate(
            ((stream, s_v), (gain, g_v), (head, h_v), (reward, r_v), (segment, i_v))
        )
    ]
    for m in moves:
        m.start()
    for m in moves:
        m.wait()

    def parts(v):
        high = v.astype(bf16).astype(f32)
        mid = (v - high).astype(bf16).astype(f32)
        return high, mid, v - high - mid

    out[0:128] = s_v[...]
    rows = parts(g_v[...] * h_v[...])
    rows += (jnp.concatenate([*parts(r_v[...]), i_v[...].astype(f32)], 1),)
    line = lax.broadcasted_iota(jnp.int32, (16, 512), 0)
    extra = jnp.zeros((16, 512), f32)
    for i, a in enumerate(rows):
        extra = jnp.where(line == i, jnp.broadcast_to(a, (16, 512)), extra)
    out[128:144] = extra.astype(bf16)


def pick_body(own, other, out, sums, owed):
    x, _, y, _ = place()

    @pl.when(lax.rem(x, 2) == y // 2)
    def _():
        out[0:128] = own[0:128]

    @pl.when(lax.rem(x, 2) != y // 2)
    def _():
        out[0:128] = other[0:128]

    mine, theirs = own[128:144].astype(f32), other[128:144].astype(f32)
    even = lax.rem(x, 2) == 0
    first = jnp.where(even, mine, theirs)
    second = jnp.where(even, theirs, mine)
    for i, a in enumerate((first[3:4], second[3:4])):
        owed[i : i + 1] = a[:, 0:128] + a[:, 128:256] + a[:, 256:384]
        owed[2 + i : 3 + i] = a[:, 384:512]
    owed[4:8] = jnp.zeros((4, 128), f32)
    out[128:144] = mine.astype(bf16)
    gw = gains_of(own)

    def total(a):
        a = sum(a[:, 128 * i : 128 * i + 128] for i in range(8))
        return jnp.sum(a.T, axis=0, keepdims=True)

    v = out[0:128].astype(f32)
    sums[0:1] = total(v * v)
    sums[1:2] = total(v * gw)
    sums[2:8] = jnp.zeros((6, 128), f32)


def gains_of(block):
    extra = block[128:144].astype(f32)
    return extra[0:1] + extra[1:2] + extra[2:3]


def coefs_body(here, there, bias, out, target):
    x, zlo, y, _ = place()

    def side(src, at):
        near, away = src[at : at + 2], src[24 + at : 26 + at]
        low, high = jnp.where(x // 2 == 0, near, away), jnp.where(x // 2 == 0, away, near)
        return jnp.concatenate([low, high], 0)

    def rows(at):
        mine, theirs = side(here, at), side(there, at)
        return jnp.where(zlo == 0, mine, theirs), jnp.where(zlo == 0, theirs, mine)

    value = jnp.concatenate([*rows(8), *rows(16)], 0)
    segment = jnp.concatenate([*rows(10), *rows(18)], 0)
    shape = value.shape
    line = lax.broadcasted_iota(jnp.int32, shape, 0) % 8
    lane = lax.broadcasted_iota(jnp.int32, shape, 1)

    def ahead(a, step):
        if step >= 128:
            return pltpu.roll(a, shape[0] - step // 128, 0)
        here = pltpu.roll(a, 128 - step, 1)
        below = pltpu.roll(here, shape[0] - 1, 0)
        return jnp.where(lane + step < 128, here, below)

    step = 1
    while step < 1024:
        inside = line * 128 + lane + step < 1024
        same = inside & (ahead(segment, step) == segment)
        value = value + jnp.where(same, ahead(value, step), 0.0)
        step *= 2
    mean = jnp.sum(value) / COUNT
    off = value - mean
    spread = jnp.sum(off * off) / COUNT
    target[...] = (off / jnp.sqrt(jnp.broadcast_to(spread, shape) + 1e-05))[:8]
    wanted, sq, lin = [], [], []
    for i in range(4):
        zl = zlo if i < 2 else 1 - zlo
        b = x // 2 if i % 2 == 0 else 1 - x // 2
        wanted.append(target[pl.ds(4 * zl + 2 * b + y // 2, 1)])
        src = (here, there)[i // 2]
        at = 24 * (i % 2)
        sq.append(src[at : at + 1])
        lin.append(src[at + 1 : at + 2])
    wanted, sq, lin = (jnp.concatenate(a, 0) for a in (wanted, sq, lin))
    rms = jnp.sqrt(sq / WIDTH + 1e-05)
    head = lin / rms
    dvalue = loss_scale * (head + bias[0] - wanted) / COUNT
    out[0:4] = dvalue / rms
    out[4:8] = head / WIDTH / rms


def columns(coefs):
    padded = jnp.concatenate([coefs, jnp.zeros((120, 128), f32)], 0).T
    lane = lax.broadcasted_iota(jnp.int32, (128, 128), 1)

    def column(at):
        return jnp.sum(jnp.where(lane == at, padded, 0.0), axis=1, keepdims=True)

    return column


def formed(block, s, l, gains):
    return (s * (gains - block.astype(f32) * l)).astype(bf16)


def own_grad_body(stream, block, coefs, coefs_mate, grad):
    x, _, y, _ = place()
    column = columns(jnp.where(lax.rem(x, 2) == y // 2, coefs[...], coefs_mate[...]))
    grad[...] = formed(stream[...], column(0), column(4), gains_of(block)[:, :512])


def grad_body(coefs, here, there, g_own, g_other):
    x, zlo, y, zhi = place()
    odd = lax.rem(y, 2)
    column = columns(coefs[...])
    gains = gains_of(here)
    for k, spots in enumerate(((192, 224), (128, 64), (0, 32), (96, 160))):
        z = lax.rem(zhi + k, 4)
        zl, b = z // 2, lax.rem(z, 2)
        at = jnp.where(zl == zlo, 0, 2) + jnp.where(b == x // 2, 0, 1)
        s_all, l_all = column(at), column(4 + at)
        s_all = jnp.where(odd == 0, s_all, jnp.concatenate([s_all[64:], s_all[:64]], 0))
        l_all = jnp.where(odd == 0, l_all, jnp.concatenate([l_all[64:], l_all[:64]], 0))
        start = jnp.where(b == x // 2, 0, 144)
        for same, src in ((True, here), (False, there)):

            @pl.when((zl == zlo) == same)
            def _(src=src, s_all=s_all, l_all=l_all, start=start, spots=spots):
                for who, out in ((0, g_own), (1, g_other)):
                    parity = odd if who == 0 else 1 - odd
                    first = pl.multiple_of(start + 64 * parity, 16)
                    rows = slice(64 * who, 64 * who + 64)
                    made = formed(src[pl.ds(first, 64)], s_all[rows], l_all[rows], gains)
                    for i, spot in enumerate(spots):
                        out[spot : spot + 32] = made[32 * i : 32 * i + 32]


LO = 1856
CHUNKS = ((0, 1024), (1024, 2048), (2048, 3072), (3072, 3696))
HIGH = 3696 - LO
SPANS = ((0, LO), (LO, 3696))
def inner_body(g, w, got, other, *refs):
    out, (w_v, m_v, sems) = refs[:4], refs[4:]
    p = lax.axis_index("dp")
    for i, (a, b) in enumerate(CHUNKS):
        pltpu.make_async_copy(w.at[a:b], w_v.at[a:b], sems.at[i]).start()

    def mate_copy(j, low, high):
        a, b = SPANS[j]
        src, off = (low, high)[j], (0, HIGH)[j]
        return pltpu.make_async_copy(src.at[a - off : b - off], m_v.at[a:b], sems.at[4 + j])

    @pl.when(p == 0)
    def _():
        for j in range(2):
            mate_copy(j, got, other).start()

    @pl.when(p == 1)
    def _():
        for j in range(2):
            mate_copy(j, other, got).start()

    left, right = g[:, :512], g[:, 512:]
    nt = (((1,), (1,)), ((), ()))
    waits = ((0,), (1,), (), ())
    for i, (a, b) in enumerate(CHUNKS):
        pltpu.make_async_copy(w.at[a:b], w_v.at[a:b], sems.at[i]).wait()
        for j in waits[i]:
            mate_copy(j, other, other).wait()
        for f in range(a, b, 512):
            e = min(f + 512, b)
            made = lax.dot_general(left, w_v[f:e], nt, preferred_element_type=f32)
            made = made + lax.dot_general(right, m_v[f:e], nt, preferred_element_type=f32)
            for n, o in enumerate(out):
                o[:, f:e] = made[64 * n : 64 * n + 64].astype(o.dtype)


def inner(g, w, got, other, dtype, name):
    hbm = pl.BlockSpec(memory_space=pl.ANY)
    return call(
        inner_body,
        [sds((64, 3696), dtype)] * 4,
        (g, w, got, other),
        in_specs=[pl.BlockSpec(memory_space=pltpu.VMEM)] + [hbm] * 3,
        scratch=[
            pltpu.VMEM((3696, 512), bf16),
            pltpu.VMEM((3696, 512), bf16),
            pltpu.SemaphoreType.DMA((6,)),
        ],
        flops=2 * 256 * 1024 * 3696,
        moved=10 << 20,
        name=name,
        grant=24,
    )


def outer_body(*refs, first, split):
    (far_a, far_b, up, down, here, y0, y12, y3), (g_own, g_other) = refs[:8], refs[8:10]
    *outs, h_v, g_v, sems = refs[10:]
    p = lax.axis_index("dp")
    moves = (
        (0, far_a, 0, 32),
        (32, far_b, 0, 32),
        (64, up, 32, 64),
        (96, down, 0, 32),
        (128, up, 0, 32),
        (160, down, 32, 64),
        (192, here, 0, 64),
        (256, y0, 0, 64),
        (320, y12, 32, 96),
        (384, y12, 0, 32),
        (416, y12, 96, 128),
        (448, y3, 0, 64),
    )
    moves = [
        pltpu.make_async_copy(src.at[a:b], h_v.at[at : at + b - a], sems.at[i])
        for i, (at, src, a, b) in enumerate(moves)
    ]
    for m in moves:
        m.start()
    for n, side in enumerate((1 - p, p) if split else (0, 1)):
        start = pl.multiple_of(first + 256 * side, 256)
        g_v[:256, 256 * n : 256 * n + 256] = g_own[:, pl.ds(start, 256)]
        g_v[256:, 256 * n : 256 * n + 256] = g_other[:, pl.ds(start, 256)]
    for m in moves:
        m.wait()
    for f in range(0, 3696, 512):
        e = min(f + 512, 3696)
        out = lax.dot_general(
            h_v[:, f:e], g_v[...], (((0,), (0,)), ((), ())), preferred_element_type=f32
        )
        if split:
            outs[0][f:e] = out[:, :256].astype(bf16)
            outs[1][f:e] = out[:, 256:]
        else:
            outs[0][f:e] = out


def outer(pieces, g_own, g_other, first, split, name):
    out = [sds((3696, 256), bf16), sds((3696, 256), f32)] if split else sds((3696, 512), f32)
    return call(
        functools.partial(outer_body, first=first, split=split),
        out,
        (*pieces, g_own, g_other),
        in_specs=[pl.BlockSpec(memory_space=pl.ANY)] * 8
        + [pl.BlockSpec(memory_space=pltpu.VMEM)] * 2,
        scratch=[
            pltpu.VMEM((512, 3696), bf16),
            pltpu.VMEM((512, 512), bf16),
            pltpu.SemaphoreType.DMA((12,)),
        ],
        flops=512 * 1024 * 3696,
        moved=8 << 20,
        name=name,
        grant=28,
    )


def fold_body(own, other, *refs):
    *more, first, second = refs
    total = own[...] + other[...].astype(f32)
    for i, out in enumerate((first, second)):
        part = total[32 * i : 32 * i + 32]
        if more:
            part = part + more[i][...].astype(f32)
        out[...] = part.astype(bf16)


def fold(own, other, *more):
    return call(fold_body, [sds((32, own.shape[1]), bf16)] * 2, (own, other, *more))


def here_body(own, other, pure_a, pure_b, mixed_a, mixed_b, out):
    total = own[...] + other[...].astype(f32)
    for at, (one, two) in ((0, (pure_a, mixed_a)), (32, (pure_b, mixed_b))):
        part = total[at : at + 32] + one[...].astype(f32) + two[...].astype(f32)
        out[at : at + 32] = part.astype(bf16)


def merge_body(partial, recv, out):
    p = lax.axis_index("dp")
    mine = pl.ds(pl.multiple_of(256 * p, 256), 256)
    rest = pl.ds(pl.multiple_of(256 * (1 - p), 256), 256)
    out[:, mine] = (partial[:, mine] + recv[...].astype(f32)).astype(bf16)
    out[:, rest] = partial[:, rest].astype(bf16)


def per_device(stream, hidden, w_down, norm_gain, value_head, value_bias, rewards, segments):
    p = lax.axis_index("dp")
    smem = pl.BlockSpec(memory_space=pltpu.SMEM)
    vmem = pl.BlockSpec(memory_space=pltpu.VMEM)
    hbm = pl.BlockSpec(memory_space=pl.ANY)

    payload = call(
        prep_body,
        sds((144, 512), bf16),
        (stream, norm_gain[None], value_head[None], rewards, segments),
        in_specs=[hbm] * 5,
        scratch=[
            pltpu.VMEM((128, 512), bf16),
            pltpu.VMEM((1, 512), f32),
            pltpu.VMEM((1, 512), f32),
            pltpu.VMEM((1, 128), f32),
            pltpu.VMEM((1, 128), jnp.int32),
            pltpu.SemaphoreType.DMA((5,)),
        ],
        grant=56,
    )
    payload_mate = col(payload, MATE, "payload_mate")
    ready = after(hidden, payload)
    y3 = col(ready, PAIR, "y3")
    down = col(ready, ZUP, "down")
    up = col(ready, ZDOWN, "up")

    w_half = lax.dynamic_slice_in_dim(w_down, p * HIGH, LO, 0)
    got = col(after(w_half, payload_mate), MATE, "got")

    block = jnp.concatenate([payload, payload_mate], 1)
    near, sums, owed = call(
        pick_body,
        (sds((144, 1024), bf16), sds((8, 128), f32), sds((8, 128), f32)),
        (block, row(block, XONE, "block_x1")),
    )
    away = row(near, XTHREE, "block_x3")
    here = jnp.concatenate([near, away], 0)
    there = row(here, ZLO, "block_zlo")
    owed_other = core(owed, "owed_other")

    gates = ((y3,), (down, up), (away,))
    for i, perm in enumerate((PAIR, ZONE, ZTHREE)):
        sums = after(sums, *gates[i])
        sums = sums + col(sums, perm, f"sums{i}")
        if i == 0:
            down, up = lax.optimization_barrier((down, up, sums))[:2]
            far_a = col(down[:32], ZUP, "far_a")
            far_b = col(up[32:], ZDOWN, "far_b")
            y12 = col(jnp.concatenate([up, down], 0), PAIR, "y12")
    y0 = col(after(jnp.concatenate([far_a, far_b], 0), sums), PAIR, "y0")
    tiny = jnp.concatenate([sums, owed, owed_other], 0)
    tiny = after(tiny, far_a, far_b)
    tiny = jnp.concatenate([tiny, row(tiny, XTHREE, "tiny_x3")], 0)
    tiny_zlo = row(tiny, ZLO, "tiny_zlo")
    coefs = call(
        coefs_body,
        sds((8, 128), f32),
        (after(tiny, got), tiny_zlo, value_bias),
        in_specs=[vmem, vmem, smem],
        scratch=[pltpu.VMEM((8, 128), f32)],
    )
    got_other = core(after(got, tiny_zlo), "got_other")
    coefs_mate = col(coefs, MATE, "coefs_mate")
    g_own, g_other = call(
        grad_body,
        (sds((256, 1024), bf16), sds((256, 1024), bf16)),
        (coefs, here, there),
        moved=4 << 20,
    )

    pieces = (far_a, far_b, up, down, hidden, y0, y12, y3)
    mate_give, mate_keep = outer(pieces, after(g_own, coefs_mate), g_other, 512, True, "outer_mate")
    mate_got = core(mate_give, "mate_got")
    sent = inner(after(g_other, mate_keep), w_down, got, got_other, bf16, "inner_sent")
    own = inner(after(g_own, sent[0]), w_down, got, got_other, f32, "inner_own")
    t = [col(a, PAIR, f"t{i}") for i, a in enumerate(sent)]
    w_send = (after(mate_keep, sent[0]) + mate_got.astype(f32)).astype(bf16)
    w_recv = col(w_send, MATE, "w_recv")

    q0a, q0b = fold(own[0], after(t[0], w_send))
    from_down = col(q0a, ZUP, "from_down")
    from_up = col(q0b, ZDOWN, "from_up")
    stream_grad = call(
        own_grad_body, sds((128, 512), bf16), (after(stream, q0a), near, coefs, coefs_mate)
    )
    partial = outer(pieces, after(g_own, q0a), g_other, 0, False, "outer_own")
    q1b, q1a = fold(own[1], after(t[1], partial, from_up))
    pure_b = col(q1b, ZUP, "pure_b")
    pure_a = col(q1a, ZDOWN, "pure_a")
    q2a, q2b = fold(own[2], after(t[2], stream_grad), from_down, from_up)
    q2a, q2b, pure_a, pure_b = lax.optimization_barrier((q2a, q2b, pure_a, pure_b))
    mixed_a = col(q2a, ZUP, "mixed_a")
    mixed_b = col(q2b, ZDOWN, "mixed_b")
    part = call(
        merge_body, sds((3696, 512), bf16), (after(partial, q2a), w_recv)
    )
    part_other = core(part, "part")
    weight_grad = (part.astype(f32) + part_other.astype(f32)).astype(bf16)
    hidden_grad = call(
        here_body,
        sds((64, 3696), bf16),
        (own[3], t[3], pure_a, pure_b, mixed_a, mixed_b),
    )
    return weight_grad, hidden_grad, stream_grad


def solution(mesh):
    in_specs = (
        P(("dp", "row"), "col"),
        P(("dp", "col"), "row"),
        P("row", "col"),
        P("col"),
        P("col"),
        P(),
        P("dp", "row"),
        P("dp", "row"),
    )
    out_specs = (P("row", "col"), P(("dp", "col"), "row"), P(("dp", "row"), "col"))
    return jax.shard_map(
        per_device, mesh=mesh, in_specs=in_specs, out_specs=out_specs, check_vma=False
    )
```

```python
import functools

import jax
import jax.numpy as jnp
from jax import lax
from jax.experimental import pallas as pl
from jax.experimental.pallas import tpu as pltpu
from jax.sharding import PartitionSpec as P

loss_scale = 2097152.0
bf16, f32 = jnp.bfloat16, jnp.float32
WIDTH, COUNT = 8192.0, 2048.0

PAIR = [(c, c ^ 1) for c in range(16)]
MATE = [(c, c ^ 3) for c in range(16)]
ZUP = [(c, (c + 4) % 16) for c in range(16)]
ZDOWN = [(c, (c + 12) % 16) for c in range(16)]
ZONE = [(c, c ^ 4) for c in range(16)]
ZTHREE = [(c, c ^ 12) for c in range(16)]
ZLO = [(r, r ^ 4) for r in range(8)]
CORE = [(0, 1), (1, 0)]
XONE = [(r, r ^ 1) for r in range(8)]
XTHREE = [(r, r ^ 3) for r in range(8)]
MIB = 1024 * 1024


def send(a, axis, perm, name):
    with jax.named_scope(name):
        return lax.ppermute(a, axis, perm)


def col(a, perm, name):
    return send(a, "col", perm, name)


def row(a, perm, name):
    return send(a, "row", perm, name)


def core(a, name):
    return send(a, "dp", CORE, name)


def after(a, *others):
    return lax.optimization_barrier((a, *others))[0]


def sds(shape, dtype):
    return jax.ShapeDtypeStruct(shape, dtype)


def call(body, out_shape, args, in_specs=None, scratch=(), flops=0, moved=0, name=None, grant=16):
    extra = {} if in_specs is None else {"in_specs": in_specs}
    with jax.named_scope(name or getattr(body, "__name__", "mid")):
      return pl.pallas_call(
        body,
        out_shape=out_shape,
        scratch_shapes=list(scratch),
        compiler_params=pltpu.CompilerParams(vmem_limit_bytes=grant * MIB),
        cost_estimate=pl.CostEstimate(flops=flops, bytes_accessed=moved, transcendentals=0),
        **extra,
    )(*args)


def place():
    r, c = lax.axis_index("row"), lax.axis_index("col")
    return r % 4, r // 4, c % 4, c // 4


def prep_body(stream, gain, head, reward, segment, out, s_v, g_v, h_v, r_v, i_v, sems):
    moves = [
        pltpu.make_async_copy(src, dst, sems.at[i])
        for i, (src, dst) in enumerate(
            ((stream, s_v), (gain, g_v), (head, h_v), (reward, r_v), (segment, i_v))
        )
    ]
    for m in moves:
        m.start()
    for m in moves:
        m.wait()

    def parts(v):
        high = v.astype(bf16).astype(f32)
        mid = (v - high).astype(bf16).astype(f32)
        return high, mid, v - high - mid

    out[0:128] = s_v[...]
    rows = parts(g_v[...] * h_v[...])
    rows += (jnp.concatenate([*parts(r_v[...]), i_v[...].astype(f32)], 1),)
    line = lax.broadcasted_iota(jnp.int32, (16, 512), 0)
    extra = jnp.zeros((16, 512), f32)
    for i, a in enumerate(rows):
        extra = jnp.where(line == i, jnp.broadcast_to(a, (16, 512)), extra)
    out[128:144] = extra.astype(bf16)


def pick_body(own, other, out, sums, owed):
    x, _, y, _ = place()

    @pl.when(lax.rem(x, 2) == y // 2)
    def _():
        out[0:128] = own[0:128]

    @pl.when(lax.rem(x, 2) != y // 2)
    def _():
        out[0:128] = other[0:128]

    mine, theirs = own[128:144].astype(f32), other[128:144].astype(f32)
    even = lax.rem(x, 2) == 0
    first = jnp.where(even, mine, theirs)
    second = jnp.where(even, theirs, mine)
    for i, a in enumerate((first[3:4], second[3:4])):
        owed[i : i + 1] = a[:, 0:128] + a[:, 128:256] + a[:, 256:384]
        owed[2 + i : 3 + i] = a[:, 384:512]
    owed[4:8] = jnp.zeros((4, 128), f32)
    out[128:144] = mine.astype(bf16)
    gw = gains_of(own)

    def total(a):
        a = sum(a[:, 128 * i : 128 * i + 128] for i in range(8))
        return jnp.sum(a.T, axis=0, keepdims=True)

    v = out[0:128].astype(f32)
    sums[0:1] = total(v * v)
    sums[1:2] = total(v * gw)
    sums[2:8] = jnp.zeros((6, 128), f32)


def gains_of(block):
    extra = block[128:144].astype(f32)
    return extra[0:1] + extra[1:2] + extra[2:3]


def coefs_body(here, there, bias, out, target):
    x, zlo, y, _ = place()

    def side(src, at):
        near, away = src[at : at + 2], src[24 + at : 26 + at]
        low, high = jnp.where(x // 2 == 0, near, away), jnp.where(x // 2 == 0, away, near)
        return jnp.concatenate([low, high], 0)

    def rows(at):
        mine, theirs = side(here, at), side(there, at)
        return jnp.where(zlo == 0, mine, theirs), jnp.where(zlo == 0, theirs, mine)

    value = jnp.concatenate([*rows(8), *rows(16)], 0)
    segment = jnp.concatenate([*rows(10), *rows(18)], 0)
    shape = value.shape
    line = lax.broadcasted_iota(jnp.int32, shape, 0) % 8
    lane = lax.broadcasted_iota(jnp.int32, shape, 1)

    def ahead(a, step):
        if step >= 128:
            return pltpu.roll(a, shape[0] - step // 128, 0)
        here = pltpu.roll(a, 128 - step, 1)
        below = pltpu.roll(here, shape[0] - 1, 0)
        return jnp.where(lane + step < 128, here, below)

    step = 1
    while step < 1024:
        inside = line * 128 + lane + step < 1024
        same = inside & (ahead(segment, step) == segment)
        value = value + jnp.where(same, ahead(value, step), 0.0)
        step *= 2
    mean = jnp.sum(value) / COUNT
    off = value - mean
    spread = jnp.sum(off * off) / COUNT
    target[...] = (off / jnp.sqrt(jnp.broadcast_to(spread, shape) + 1e-05))[:8]
    wanted, sq, lin = [], [], []
    for i in range(4):
        zl = zlo if i < 2 else 1 - zlo
        b = x // 2 if i % 2 == 0 else 1 - x // 2
        wanted.append(target[pl.ds(4 * zl + 2 * b + y // 2, 1)])
        src = (here, there)[i // 2]
        at = 24 * (i % 2)
        sq.append(src[at : at + 1])
        lin.append(src[at + 1 : at + 2])
    wanted, sq, lin = (jnp.concatenate(a, 0) for a in (wanted, sq, lin))
    rms = jnp.sqrt(sq / WIDTH + 1e-05)
    head = lin / rms
    dvalue = loss_scale * (head + bias[0] - wanted) / COUNT
    out[0:4] = dvalue / rms
    out[4:8] = head / WIDTH / rms


def columns(coefs):
    padded = jnp.concatenate([coefs, jnp.zeros((120, 128), f32)], 0).T
    lane = lax.broadcasted_iota(jnp.int32, (128, 128), 1)

    def column(at):
        return jnp.sum(jnp.where(lane == at, padded, 0.0), axis=1, keepdims=True)

    return column


def formed(block, s, l, gains):
    return (s * (gains - block.astype(f32) * l)).astype(bf16)


def own_grad_body(stream, block, coefs, coefs_mate, grad):
    x, _, y, _ = place()
    column = columns(jnp.where(lax.rem(x, 2) == y // 2, coefs[...], coefs_mate[...]))
    grad[...] = formed(stream[...], column(0), column(4), gains_of(block)[:, :512])


def grad_body(coefs, here, there, g_own, g_other):
    x, zlo, y, zhi = place()
    odd = lax.rem(y, 2)
    column = columns(coefs[...])
    gains = gains_of(here)
    for k, spots in enumerate(((192, 224), (128, 64), (0, 32), (96, 160))):
        z = lax.rem(zhi + k, 4)
        zl, b = z // 2, lax.rem(z, 2)
        at = jnp.where(zl == zlo, 0, 2) + jnp.where(b == x // 2, 0, 1)
        s_all, l_all = column(at), column(4 + at)
        s_all = jnp.where(odd == 0, s_all, jnp.concatenate([s_all[64:], s_all[:64]], 0))
        l_all = jnp.where(odd == 0, l_all, jnp.concatenate([l_all[64:], l_all[:64]], 0))
        start = jnp.where(b == x // 2, 0, 144)
        for same, src in ((True, here), (False, there)):

            @pl.when((zl == zlo) == same)
            def _(src=src, s_all=s_all, l_all=l_all, start=start, spots=spots):
                for who, out in ((0, g_own), (1, g_other)):
                    parity = odd if who == 0 else 1 - odd
                    first = pl.multiple_of(start + 64 * parity, 16)
                    rows = slice(64 * who, 64 * who + 64)
                    made = formed(src[pl.ds(first, 64)], s_all[rows], l_all[rows], gains)
                    for i, spot in enumerate(spots):
                        out[spot : spot + 32] = made[32 * i : 32 * i + 32]


LO = 1856
CHUNKS = ((0, 1024), (1024, 2048), (2048, 3072), (3072, 3696))
HIGH = 3696 - LO
SPANS = ((0, LO), (LO, 3696))
def inner_body(g, w, got, other, *refs):
    out, (w_v, m_v, sems) = refs[:4], refs[4:]
    p = lax.axis_index("dp")
    for i, (a, b) in enumerate(CHUNKS):
        pltpu.make_async_copy(w.at[a:b], w_v.at[a:b], sems.at[i]).start()

    def mate_copy(j, low, high):
        a, b = SPANS[j]
        src, off = (low, high)[j], (0, HIGH)[j]
        return pltpu.make_async_copy(src.at[a - off : b - off], m_v.at[a:b], sems.at[4 + j])

    @pl.when(p == 0)
    def _():
        for j in range(2):
            mate_copy(j, got, other).start()

    @pl.when(p == 1)
    def _():
        for j in range(2):
            mate_copy(j, other, got).start()

    left, right = g[:, :512], g[:, 512:]
    nt = (((1,), (1,)), ((), ()))
    waits = ((0,), (1,), (), ())
    for i, (a, b) in enumerate(CHUNKS):
        pltpu.make_async_copy(w.at[a:b], w_v.at[a:b], sems.at[i]).wait()
        for j in waits[i]:
            mate_copy(j, other, other).wait()
        for f in range(a, b, 512):
            e = min(f + 512, b)
            made = lax.dot_general(left, w_v[f:e], nt, preferred_element_type=f32)
            made = made + lax.dot_general(right, m_v[f:e], nt, preferred_element_type=f32)
            for n, o in enumerate(out):
                o[:, f:e] = made[64 * n : 64 * n + 64].astype(o.dtype)


def inner(g, w, got, other, dtype, name):
    hbm = pl.BlockSpec(memory_space=pl.ANY)
    return call(
        inner_body,
        [sds((64, 3696), dtype)] * 4,
        (g, w, got, other),
        in_specs=[pl.BlockSpec(memory_space=pltpu.VMEM)] + [hbm] * 3,
        scratch=[
            pltpu.VMEM((3696, 512), bf16),
            pltpu.VMEM((3696, 512), bf16),
            pltpu.SemaphoreType.DMA((6,)),
        ],
        flops=2 * 256 * 1024 * 3696,
        moved=10 << 20,
        name=name,
        grant=24,
    )


def outer_body(*refs, first, split):
    (far_a, far_b, up, down, here, y0, y12, y3), (g_own, g_other) = refs[:8], refs[8:10]
    *outs, h_v, g_v = refs[10:]
    p = lax.axis_index("dp")
    for at, src in (
        (0, far_a[...]),
        (32, far_b[...]),
        (64, up[32:64]),
        (96, down[0:32]),
        (128, up[0:32]),
        (160, down[32:64]),
        (192, here[...]),
        (256, y0[...]),
        (320, y12[0, 32:64]),
        (352, y12[1, 0:32]),
        (384, y12[0, 0:32]),
        (416, y12[1, 32:64]),
        (448, y3[...]),
    ):
        h_v[at : at + src.shape[0]] = src
    for n, side in enumerate((1 - p, p) if split else (0, 1)):
        start = pl.multiple_of(first + 256 * side, 256)
        g_v[:256, 256 * n : 256 * n + 256] = g_own[:, pl.ds(start, 256)]
        g_v[256:, 256 * n : 256 * n + 256] = g_other[:, pl.ds(start, 256)]
    for f in range(0, 3696, 512):
        e = min(f + 512, 3696)
        out = lax.dot_general(
            h_v[:, f:e], g_v[...], (((0,), (0,)), ((), ())), preferred_element_type=f32
        )
        if split:
            outs[0][f:e] = out[:, :256].astype(bf16)
            outs[1][f:e] = out[:, 256:]
        else:
            outs[0][f:e] = out


def outer(pieces, g_own, g_other, first, split, name):
    out = [sds((3696, 256), bf16), sds((3696, 256), f32)] if split else sds((3696, 512), f32)
    return call(
        functools.partial(outer_body, first=first, split=split),
        out,
        (*pieces, g_own, g_other),
        scratch=[pltpu.VMEM((512, 3696), bf16), pltpu.VMEM((512, 512), bf16)],
        flops=512 * 1024 * 3696,
        moved=8 << 20,
        name=name,
        grant=28,
    )


def fold_body(own, other, *refs):
    *more, first, second = refs
    total = own[...] + other[...].astype(f32)
    for i, out in enumerate((first, second)):
        part = total[32 * i : 32 * i + 32]
        if more:
            part = part + more[i][...].astype(f32)
        out[...] = part.astype(bf16)


def fold(own, other, *more):
    return call(fold_body, [sds((32, own.shape[1]), bf16)] * 2, (own, other, *more))


def here_body(own, other, pure_a, pure_b, mixed_a, mixed_b, out):
    total = own[...] + other[...].astype(f32)
    for at, (one, two) in ((0, (pure_a, mixed_a)), (32, (pure_b, mixed_b))):
        part = total[at : at + 32] + one[...].astype(f32) + two[...].astype(f32)
        out[at : at + 32] = part.astype(bf16)


def merge_body(partial, recv, out):
    p = lax.axis_index("dp")
    mine = pl.ds(pl.multiple_of(256 * p, 256), 256)
    rest = pl.ds(pl.multiple_of(256 * (1 - p), 256), 256)
    out[:, mine] = (partial[:, mine] + recv[...].astype(f32)).astype(bf16)
    out[:, rest] = partial[:, rest].astype(bf16)


def per_device(stream, hidden, w_down, norm_gain, value_head, value_bias, rewards, segments):
    p = lax.axis_index("dp")
    smem = pl.BlockSpec(memory_space=pltpu.SMEM)
    vmem = pl.BlockSpec(memory_space=pltpu.VMEM)
    hbm = pl.BlockSpec(memory_space=pl.ANY)

    payload = call(
        prep_body,
        sds((144, 512), bf16),
        (stream, norm_gain[None], value_head[None], rewards, segments),
        in_specs=[hbm] * 5,
        scratch=[
            pltpu.VMEM((128, 512), bf16),
            pltpu.VMEM((1, 512), f32),
            pltpu.VMEM((1, 512), f32),
            pltpu.VMEM((1, 128), f32),
            pltpu.VMEM((1, 128), jnp.int32),
            pltpu.SemaphoreType.DMA((5,)),
        ],
        grant=56,
    )
    payload_mate = col(payload, MATE, "payload_mate")
    ready = after(hidden, payload)
    y3 = col(ready, PAIR, "y3")
    down = col(ready, ZUP, "down")
    up = col(ready, ZDOWN, "up")

    w_half = lax.dynamic_slice_in_dim(w_down, p * HIGH, LO, 0)
    got = col(after(w_half, payload_mate), MATE, "got")

    block = jnp.concatenate([payload, payload_mate], 1)
    near, sums, owed = call(
        pick_body,
        (sds((144, 1024), bf16), sds((8, 128), f32), sds((8, 128), f32)),
        (block, row(block, XONE, "block_x1")),
    )
    away = row(near, XTHREE, "block_x3")
    here = jnp.concatenate([near, away], 0)
    there = row(here, ZLO, "block_zlo")
    owed_other = core(owed, "owed_other")

    gates = ((y3,), (down, up), (away,))
    for i, perm in enumerate((PAIR, ZONE, ZTHREE)):
        sums = after(sums, *gates[i])
        sums = sums + col(sums, perm, f"sums{i}")
        if i == 0:
            down, up = lax.optimization_barrier((down, up, sums))[:2]
            far_a = col(down[:32], ZUP, "far_a")
            far_b = col(up[32:], ZDOWN, "far_b")
            y12 = col(jnp.stack([up, down]), PAIR, "y12")
    y0 = col(after(jnp.concatenate([far_a, far_b], 0), sums), PAIR, "y0")
    tiny = jnp.concatenate([sums, owed, owed_other], 0)
    tiny = after(tiny, far_a, far_b)
    tiny = jnp.concatenate([tiny, row(tiny, XTHREE, "tiny_x3")], 0)
    tiny_zlo = row(tiny, ZLO, "tiny_zlo")
    coefs = call(
        coefs_body,
        sds((8, 128), f32),
        (after(tiny, got), tiny_zlo, value_bias),
        in_specs=[vmem, vmem, smem],
        scratch=[pltpu.VMEM((8, 128), f32)],
    )
    got_other = core(after(got, tiny_zlo), "got_other")
    coefs_mate = col(coefs, MATE, "coefs_mate")
    g_own, g_other = call(
        grad_body,
        (sds((256, 1024), bf16), sds((256, 1024), bf16)),
        (coefs, here, there),
        moved=4 << 20,
    )

    pieces = (far_a, far_b, up, down, hidden, y0, y12, y3)
    mate_give, mate_keep = outer(pieces, after(g_own, coefs_mate), g_other, 512, True, "outer_mate")
    mate_got = core(mate_give, "mate_got")
    sent = inner(after(g_other, mate_keep), w_down, got, got_other, bf16, "inner_sent")
    own = inner(after(g_own, sent[0]), w_down, got, got_other, f32, "inner_own")
    t = [col(a, PAIR, f"t{i}") for i, a in enumerate(sent)]
    w_send = (after(mate_keep, sent[0]) + mate_got.astype(f32)).astype(bf16)
    w_recv = col(w_send, MATE, "w_recv")

    q0a, q0b = fold(own[0], after(t[0], w_send))
    from_down = col(q0a, ZUP, "from_down")
    from_up = col(q0b, ZDOWN, "from_up")
    stream_grad = call(
        own_grad_body, sds((128, 512), bf16), (after(stream, q0a), near, coefs, coefs_mate)
    )
    partial = outer(pieces, after(g_own, q0a), g_other, 0, False, "outer_own")
    q1b, q1a = fold(own[1], after(t[1], partial, from_up))
    pure_b = col(q1b, ZUP, "pure_b")
    pure_a = col(q1a, ZDOWN, "pure_a")
    q2a, q2b = fold(own[2], after(t[2], stream_grad), from_down, from_up)
    q2a, q2b, pure_a, pure_b = lax.optimization_barrier((q2a, q2b, pure_a, pure_b))
    mixed_a = col(q2a, ZUP, "mixed_a")
    mixed_b = col(q2b, ZDOWN, "mixed_b")
    part = call(
        merge_body, sds((3696, 512), bf16), (after(partial, q2a), w_recv)
    )
    part_other = core(part, "part")
    weight_grad = (part.astype(f32) + part_other.astype(f32)).astype(bf16)
    hidden_grad = call(
        here_body,
        sds((64, 3696), bf16),
        (after(own[3], weight_grad), t[3], pure_a, pure_b, mixed_a, mixed_b),
    )
    return weight_grad, hidden_grad, stream_grad


def solution(mesh):
    in_specs = (
        P(("dp", "row"), "col"),
        P(("dp", "col"), "row"),
        P("row", "col"),
        P("col"),
        P("col"),
        P(),
        P("dp", "row"),
        P("dp", "row"),
    )
    out_specs = (P("row", "col"), P(("dp", "col"), "row"), P(("dp", "row"), "col"))
    return jax.shard_map(
        per_device, mesh=mesh, in_specs=in_specs, out_specs=out_specs, check_vma=False
    )
```

```python
import functools

import jax
import jax.numpy as jnp
from jax import lax
from jax.experimental import pallas as pl
from jax.experimental.pallas import tpu as pltpu
from jax.sharding import PartitionSpec as P

loss_scale = 2097152.0
bf16, f32 = jnp.bfloat16, jnp.float32
WIDTH, COUNT = 8192.0, 2048.0

PAIR = [(c, c ^ 1) for c in range(16)]
MATE = [(c, c ^ 3) for c in range(16)]
ZUP = [(c, (c + 4) % 16) for c in range(16)]
ZDOWN = [(c, (c + 12) % 16) for c in range(16)]
ZONE = [(c, c ^ 4) for c in range(16)]
ZTHREE = [(c, c ^ 12) for c in range(16)]
ZLO = [(r, r ^ 4) for r in range(8)]
CORE = [(0, 1), (1, 0)]
XONE = [(r, r ^ 1) for r in range(8)]
XTHREE = [(r, r ^ 3) for r in range(8)]
MIB = 1024 * 1024


def send(a, axis, perm, name):
    with jax.named_scope(name):
        return lax.ppermute(a, axis, perm)


def col(a, perm, name):
    return send(a, "col", perm, name)


def row(a, perm, name):
    return send(a, "row", perm, name)


def core(a, name):
    return send(a, "dp", CORE, name)


def after(a, *others):
    return lax.optimization_barrier((a, *others))[0]


def sds(shape, dtype):
    return jax.ShapeDtypeStruct(shape, dtype)


def call(body, out_shape, args, in_specs=None, scratch=(), flops=0, moved=0, name=None, grant=16):
    extra = {} if in_specs is None else {"in_specs": in_specs}
    with jax.named_scope(name or getattr(body, "__name__", "mid")):
      return pl.pallas_call(
        body,
        out_shape=out_shape,
        scratch_shapes=list(scratch),
        compiler_params=pltpu.CompilerParams(vmem_limit_bytes=grant * MIB),
        cost_estimate=pl.CostEstimate(flops=flops, bytes_accessed=moved, transcendentals=0),
        **extra,
    )(*args)


def place():
    r, c = lax.axis_index("row"), lax.axis_index("col")
    return r % 4, r // 4, c % 4, c // 4


def prep_body(stream, gain, head, reward, segment, out, s_v, g_v, h_v, r_v, i_v, sems):
    moves = [
        pltpu.make_async_copy(src, dst, sems.at[i])
        for i, (src, dst) in enumerate(
            ((stream, s_v), (gain, g_v), (head, h_v), (reward, r_v), (segment, i_v))
        )
    ]
    for m in moves:
        m.start()
    for m in moves:
        m.wait()

    def parts(v):
        high = v.astype(bf16).astype(f32)
        mid = (v - high).astype(bf16).astype(f32)
        return high, mid, v - high - mid

    out[0:128] = s_v[...]
    rows = parts(g_v[...] * h_v[...])
    rows += (jnp.concatenate([*parts(r_v[...]), i_v[...].astype(f32)], 1),)
    line = lax.broadcasted_iota(jnp.int32, (16, 512), 0)
    extra = jnp.zeros((16, 512), f32)
    for i, a in enumerate(rows):
        extra = jnp.where(line == i, jnp.broadcast_to(a, (16, 512)), extra)
    out[128:144] = extra.astype(bf16)


def pick_body(own, other, out, sums, owed):
    x, _, y, _ = place()

    @pl.when(lax.rem(x, 2) == y // 2)
    def _():
        out[0:128] = own[0:128]

    @pl.when(lax.rem(x, 2) != y // 2)
    def _():
        out[0:128] = other[0:128]

    mine, theirs = own[128:144].astype(f32), other[128:144].astype(f32)
    even = lax.rem(x, 2) == 0
    first = jnp.where(even, mine, theirs)
    second = jnp.where(even, theirs, mine)
    for i, a in enumerate((first[3:4], second[3:4])):
        owed[i : i + 1] = a[:, 0:128] + a[:, 128:256] + a[:, 256:384]
        owed[2 + i : 3 + i] = a[:, 384:512]
    owed[4:8] = jnp.zeros((4, 128), f32)
    out[128:144] = mine.astype(bf16)
    gw = gains_of(own)

    def total(a):
        a = sum(a[:, 128 * i : 128 * i + 128] for i in range(8))
        return jnp.sum(a.T, axis=0, keepdims=True)

    v = out[0:128].astype(f32)
    sums[0:1] = total(v * v)
    sums[1:2] = total(v * gw)
    sums[2:8] = jnp.zeros((6, 128), f32)


def gains_of(block):
    extra = block[128:144].astype(f32)
    return extra[0:1] + extra[1:2] + extra[2:3]


def coefs_body(here, there, bias, out, target):
    x, zlo, y, _ = place()

    def side(src, at):
        near, away = src[at : at + 2], src[24 + at : 26 + at]
        low, high = jnp.where(x // 2 == 0, near, away), jnp.where(x // 2 == 0, away, near)
        return jnp.concatenate([low, high], 0)

    def rows(at):
        mine, theirs = side(here, at), side(there, at)
        return jnp.where(zlo == 0, mine, theirs), jnp.where(zlo == 0, theirs, mine)

    value = jnp.concatenate([*rows(8), *rows(16)], 0)
    segment = jnp.concatenate([*rows(10), *rows(18)], 0)
    shape = value.shape
    line = lax.broadcasted_iota(jnp.int32, shape, 0) % 8
    lane = lax.broadcasted_iota(jnp.int32, shape, 1)

    def ahead(a, step):
        if step >= 128:
            return pltpu.roll(a, shape[0] - step // 128, 0)
        here = pltpu.roll(a, 128 - step, 1)
        below = pltpu.roll(here, shape[0] - 1, 0)
        return jnp.where(lane + step < 128, here, below)

    step = 1
    while step < 1024:
        inside = line * 128 + lane + step < 1024
        same = inside & (ahead(segment, step) == segment)
        value = value + jnp.where(same, ahead(value, step), 0.0)
        step *= 2
    mean = jnp.sum(value) / COUNT
    off = value - mean
    spread = jnp.sum(off * off) / COUNT
    target[...] = (off / jnp.sqrt(jnp.broadcast_to(spread, shape) + 1e-05))[:8]
    wanted, sq, lin = [], [], []
    for i in range(4):
        zl = zlo if i < 2 else 1 - zlo
        b = x // 2 if i % 2 == 0 else 1 - x // 2
        wanted.append(target[pl.ds(4 * zl + 2 * b + y // 2, 1)])
        src = (here, there)[i // 2]
        at = 24 * (i % 2)
        sq.append(src[at : at + 1])
        lin.append(src[at + 1 : at + 2])
    wanted, sq, lin = (jnp.concatenate(a, 0) for a in (wanted, sq, lin))
    rms = jnp.sqrt(sq / WIDTH + 1e-05)
    head = lin / rms
    dvalue = loss_scale * (head + bias[0] - wanted) / COUNT
    out[0:4] = dvalue / rms
    out[4:8] = head / WIDTH / rms


def columns(coefs):
    padded = jnp.concatenate([coefs, jnp.zeros((120, 128), f32)], 0).T
    lane = lax.broadcasted_iota(jnp.int32, (128, 128), 1)

    def column(at):
        return jnp.sum(jnp.where(lane == at, padded, 0.0), axis=1, keepdims=True)

    return column


def formed(block, s, l, gains):
    return (s * (gains - block.astype(f32) * l)).astype(bf16)


def own_grad_body(stream, block, coefs, coefs_mate, grad):
    x, _, y, _ = place()
    column = columns(jnp.where(lax.rem(x, 2) == y // 2, coefs[...], coefs_mate[...]))
    grad[...] = formed(stream[...], column(0), column(4), gains_of(block)[:, :512])


def grad_body(coefs, here, there, g_own, g_other):
    x, zlo, y, zhi = place()
    odd = lax.rem(y, 2)
    column = columns(coefs[...])
    gains = gains_of(here)
    for k, spots in enumerate(((192, 224), (128, 64), (0, 32), (96, 160))):
        z = lax.rem(zhi + k, 4)
        zl, b = z // 2, lax.rem(z, 2)
        at = jnp.where(zl == zlo, 0, 2) + jnp.where(b == x // 2, 0, 1)
        s_all, l_all = column(at), column(4 + at)
        s_all = jnp.where(odd == 0, s_all, jnp.concatenate([s_all[64:], s_all[:64]], 0))
        l_all = jnp.where(odd == 0, l_all, jnp.concatenate([l_all[64:], l_all[:64]], 0))
        start = jnp.where(b == x // 2, 0, 144)
        for same, src in ((True, here), (False, there)):

            @pl.when((zl == zlo) == same)
            def _(src=src, s_all=s_all, l_all=l_all, start=start, spots=spots):
                for who, out in ((0, g_own), (1, g_other)):
                    parity = odd if who == 0 else 1 - odd
                    first = pl.multiple_of(start + 64 * parity, 16)
                    rows = slice(64 * who, 64 * who + 64)
                    made = formed(src[pl.ds(first, 64)], s_all[rows], l_all[rows], gains)
                    for i, spot in enumerate(spots):
                        out[spot : spot + 32] = made[32 * i : 32 * i + 32]


LO = 1856
CHUNKS = ((0, 1024), (1024, 2048), (2048, 3072), (3072, 3696))
HIGH = 3696 - LO
SPANS = ((0, LO), (LO, 3696))
def inner_body(g, w, got, other, *refs):
    out, (w_v, m_v, sems) = refs[:4], refs[4:]
    p = lax.axis_index("dp")
    for i, (a, b) in enumerate(CHUNKS):
        pltpu.make_async_copy(w.at[a:b], w_v.at[a:b], sems.at[i]).start()

    def mate_copy(j, low, high):
        a, b = SPANS[j]
        src, off = (low, high)[j], (0, HIGH)[j]
        return pltpu.make_async_copy(src.at[a - off : b - off], m_v.at[a:b], sems.at[4 + j])

    @pl.when(p == 0)
    def _():
        for j in range(2):
            mate_copy(j, got, other).start()

    @pl.when(p == 1)
    def _():
        for j in range(2):
            mate_copy(j, other, got).start()

    left, right = g[:, :512], g[:, 512:]
    nt = (((1,), (1,)), ((), ()))
    waits = ((0,), (1,), (), ())
    for i, (a, b) in enumerate(CHUNKS):
        pltpu.make_async_copy(w.at[a:b], w_v.at[a:b], sems.at[i]).wait()
        for j in waits[i]:
            mate_copy(j, other, other).wait()
        for f in range(a, b, 512):
            e = min(f + 512, b)
            made = lax.dot_general(left, w_v[f:e], nt, preferred_element_type=f32)
            made = made + lax.dot_general(right, m_v[f:e], nt, preferred_element_type=f32)
            for n, o in enumerate(out):
                o[:, f:e] = made[64 * n : 64 * n + 64].astype(o.dtype)


def inner(g, w, got, other, dtype, name):
    hbm = pl.BlockSpec(memory_space=pl.ANY)
    return call(
        inner_body,
        [sds((64, 3696), dtype)] * 4,
        (g, w, got, other),
        in_specs=[pl.BlockSpec(memory_space=pltpu.VMEM)] + [hbm] * 3,
        scratch=[
            pltpu.VMEM((3696, 512), bf16),
            pltpu.VMEM((3696, 512), bf16),
            pltpu.SemaphoreType.DMA((6,)),
        ],
        flops=2 * 256 * 1024 * 3696,
        moved=10 << 20,
        name=name,
        grant=24,
    )


def outer_body(*refs, first, split):
    (far_a, far_b, up, down, here, y0, y12, y3), (g_own, g_other) = refs[:8], refs[8:10]
    *outs, h_v, g_v = refs[10:]
    p = lax.axis_index("dp")
    for at, src in (
        (0, far_a[...]),
        (32, far_b[...]),
        (64, up[32:64]),
        (96, down[0:32]),
        (128, up[0:32]),
        (160, down[32:64]),
        (192, here[...]),
        (256, y0[...]),
        (320, y12[0, 32:64]),
        (352, y12[1, 0:32]),
        (384, y12[0, 0:32]),
        (416, y12[1, 32:64]),
        (448, y3[...]),
    ):
        h_v[at : at + src.shape[0]] = src
    for n, side in enumerate((1 - p, p) if split else (0, 1)):
        start = pl.multiple_of(first + 256 * side, 256)
        g_v[:256, 256 * n : 256 * n + 256] = g_own[:, pl.ds(start, 256)]
        g_v[256:, 256 * n : 256 * n + 256] = g_other[:, pl.ds(start, 256)]
    for f in range(0, 3696, 512):
        e = min(f + 512, 3696)
        out = lax.dot_general(
            h_v[:, f:e], g_v[...], (((0,), (0,)), ((), ())), preferred_element_type=f32
        )
        if split:
            outs[0][f:e] = out[:, :256].astype(bf16)
            outs[1][f:e] = out[:, 256:]
        else:
            outs[0][f:e] = out


def outer(pieces, g_own, g_other, first, split, name):
    out = [sds((3696, 256), bf16), sds((3696, 256), f32)] if split else sds((3696, 512), f32)
    return call(
        functools.partial(outer_body, first=first, split=split),
        out,
        (*pieces, g_own, g_other),
        scratch=[pltpu.VMEM((512, 3696), bf16), pltpu.VMEM((512, 512), bf16)],
        flops=512 * 1024 * 3696,
        moved=8 << 20,
        name=name,
        grant=28,
    )


def fold_body(own, other, *refs):
    *more, first, second = refs
    total = own[...] + other[...].astype(f32)
    for i, out in enumerate((first, second)):
        part = total[32 * i : 32 * i + 32]
        if more:
            part = part + more[i][...].astype(f32)
        out[...] = part.astype(bf16)


def fold(own, other, *more):
    return call(fold_body, [sds((32, own.shape[1]), bf16)] * 2, (own, other, *more))


def here_body(own, other, pure_a, pure_b, mixed_a, mixed_b, out):
    total = own[...] + other[...].astype(f32)
    for at, (one, two) in ((0, (pure_a, mixed_a)), (32, (pure_b, mixed_b))):
        part = total[at : at + 32] + one[...].astype(f32) + two[...].astype(f32)
        out[at : at + 32] = part.astype(bf16)


def merge_body(partial, recv, out):
    p = lax.axis_index("dp")
    mine = pl.ds(pl.multiple_of(256 * p, 256), 256)
    rest = pl.ds(pl.multiple_of(256 * (1 - p), 256), 256)
    out[:, mine] = (partial[:, mine] + recv[...].astype(f32)).astype(bf16)
    out[:, rest] = partial[:, rest].astype(bf16)


def per_device(stream, hidden, w_down, norm_gain, value_head, value_bias, rewards, segments):
    p = lax.axis_index("dp")
    smem = pl.BlockSpec(memory_space=pltpu.SMEM)
    vmem = pl.BlockSpec(memory_space=pltpu.VMEM)
    hbm = pl.BlockSpec(memory_space=pl.ANY)

    payload = call(
        prep_body,
        sds((144, 512), bf16),
        (stream, norm_gain[None], value_head[None], rewards, segments),
        in_specs=[hbm] * 5,
        scratch=[
            pltpu.VMEM((128, 512), bf16),
            pltpu.VMEM((1, 512), f32),
            pltpu.VMEM((1, 512), f32),
            pltpu.VMEM((1, 128), f32),
            pltpu.VMEM((1, 128), jnp.int32),
            pltpu.SemaphoreType.DMA((5,)),
        ],
        grant=56,
    )
    payload_mate = col(payload, MATE, "payload_mate")
    ready = after(hidden, payload)
    y3 = col(ready, PAIR, "y3")
    down = col(hidden, ZUP, "down")
    up = col(hidden, ZDOWN, "up")

    w_half = lax.dynamic_slice_in_dim(w_down, p * HIGH, LO, 0)
    got = col(after(w_half, payload_mate), MATE, "got")

    block = jnp.concatenate([payload, payload_mate], 1)
    near, sums, owed = call(
        pick_body,
        (sds((144, 1024), bf16), sds((8, 128), f32), sds((8, 128), f32)),
        (block, row(block, XONE, "block_x1")),
    )
    away = row(near, XTHREE, "block_x3")
    here = jnp.concatenate([near, away], 0)
    there = row(here, ZLO, "block_zlo")
    owed_other = core(owed, "owed_other")

    gates = ((y3,), (down, up), (away,))
    for i, perm in enumerate((PAIR, ZONE, ZTHREE)):
        sums = after(sums, *gates[i])
        sums = sums + col(sums, perm, f"sums{i}")
        if i == 0:
            down, up = lax.optimization_barrier((down, up, sums))[:2]
            far_a = col(down[:32], ZUP, "far_a")
            far_b = col(up[32:], ZDOWN, "far_b")
            y12 = col(jnp.stack([up, down]), PAIR, "y12")
    y0 = col(after(jnp.concatenate([far_a, far_b], 0), sums), PAIR, "y0")
    tiny = jnp.concatenate([sums, owed, owed_other], 0)
    tiny = after(tiny, far_a, far_b)
    tiny = jnp.concatenate([tiny, row(tiny, XTHREE, "tiny_x3")], 0)
    tiny_zlo = row(tiny, ZLO, "tiny_zlo")
    coefs = call(
        coefs_body,
        sds((8, 128), f32),
        (after(tiny, got), tiny_zlo, value_bias),
        in_specs=[vmem, vmem, smem],
        scratch=[pltpu.VMEM((8, 128), f32)],
    )
    got_other = core(after(got, tiny_zlo), "got_other")
    coefs_mate = col(coefs, MATE, "coefs_mate")
    g_own, g_other = call(
        grad_body,
        (sds((256, 1024), bf16), sds((256, 1024), bf16)),
        (coefs, here, there),
        moved=4 << 20,
    )

    pieces = (far_a, far_b, up, down, hidden, y0, y12, y3)
    mate_give, mate_keep = outer(pieces, after(g_own, coefs_mate), g_other, 512, True, "outer_mate")
    mate_got = core(mate_give, "mate_got")
    sent = inner(after(g_other, mate_keep), w_down, got, got_other, bf16, "inner_sent")
    own = inner(after(g_own, sent[0]), w_down, got, got_other, f32, "inner_own")
    t = [col(a, PAIR, f"t{i}") for i, a in enumerate(sent)]
    w_send = (after(mate_keep, sent[0]) + mate_got.astype(f32)).astype(bf16)
    w_recv = col(w_send, MATE, "w_recv")

    q0a, q0b = fold(own[0], after(t[0], w_send))
    from_down = col(q0a, ZUP, "from_down")
    from_up = col(q0b, ZDOWN, "from_up")
    stream_grad = call(
        own_grad_body, sds((128, 512), bf16), (after(stream, q0a), near, coefs, coefs_mate)
    )
    partial = outer(pieces, after(g_own, q0a), g_other, 0, False, "outer_own")
    q1b, q1a = fold(own[1], after(t[1], partial, from_up))
    pure_b = col(q1b, ZUP, "pure_b")
    pure_a = col(q1a, ZDOWN, "pure_a")
    q2a, q2b = fold(own[2], after(t[2], stream_grad), from_down, from_up)
    q2a, q2b, pure_a, pure_b = lax.optimization_barrier((q2a, q2b, pure_a, pure_b))
    mixed_a = col(q2a, ZUP, "mixed_a")
    mixed_b = col(q2b, ZDOWN, "mixed_b")
    part = call(
        merge_body, sds((3696, 512), bf16), (after(partial, q2a), w_recv)
    )
    part_other = core(part, "part")
    weight_grad = (part.astype(f32) + part_other.astype(f32)).astype(bf16)
    hidden_grad = call(
        here_body,
        sds((64, 3696), bf16),
        (after(own[3], weight_grad), t[3], pure_a, pure_b, mixed_a, mixed_b),
    )
    return weight_grad, hidden_grad, stream_grad


def solution(mesh):
    in_specs = (
        P(("dp", "row"), "col"),
        P(("dp", "col"), "row"),
        P("row", "col"),
        P("col"),
        P("col"),
        P(),
        P("dp", "row"),
        P("dp", "row"),
    )
    out_specs = (P("row", "col"), P(("dp", "col"), "row"), P(("dp", "row"), "col"))
    return jax.shard_map(
        per_device, mesh=mesh, in_specs=in_specs, out_specs=out_specs, check_vma=False
    )
```

```python
import functools

import jax
import jax.numpy as jnp
from jax import lax
from jax.experimental import pallas as pl
from jax.experimental.pallas import tpu as pltpu
from jax.sharding import PartitionSpec as P

loss_scale = 2097152.0
bf16, f32 = jnp.bfloat16, jnp.float32
WIDTH, COUNT = 8192.0, 2048.0

PAIR = [(c, c ^ 1) for c in range(16)]
MATE = [(c, c ^ 3) for c in range(16)]
ZUP = [(c, (c + 4) % 16) for c in range(16)]
ZDOWN = [(c, (c + 12) % 16) for c in range(16)]
ZONE = [(c, c ^ 4) for c in range(16)]
ZTHREE = [(c, c ^ 12) for c in range(16)]
ZLO = [(r, r ^ 4) for r in range(8)]
CORE = [(0, 1), (1, 0)]
XONE = [(r, r ^ 1) for r in range(8)]
XTHREE = [(r, r ^ 3) for r in range(8)]
MIB = 1024 * 1024


def send(a, axis, perm, name):
    with jax.named_scope(name):
        return lax.ppermute(a, axis, perm)


def col(a, perm, name):
    return send(a, "col", perm, name)


def row(a, perm, name):
    return send(a, "row", perm, name)


def core(a, name):
    return send(a, "dp", CORE, name)


def after(a, *others):
    return lax.optimization_barrier((a, *others))[0]


def sds(shape, dtype):
    return jax.ShapeDtypeStruct(shape, dtype)


def call(body, out_shape, args, in_specs=None, scratch=(), flops=0, moved=0, name=None, grant=16):
    extra = {} if in_specs is None else {"in_specs": in_specs}
    with jax.named_scope(name or getattr(body, "__name__", "mid")):
      return pl.pallas_call(
        body,
        out_shape=out_shape,
        scratch_shapes=list(scratch),
        compiler_params=pltpu.CompilerParams(vmem_limit_bytes=grant * MIB),
        cost_estimate=pl.CostEstimate(flops=flops, bytes_accessed=moved, transcendentals=0),
        **extra,
    )(*args)


def place():
    r, c = lax.axis_index("row"), lax.axis_index("col")
    return r % 4, r // 4, c % 4, c // 4


def prep_body(stream, gain, head, reward, segment, out, s_v, g_v, h_v, r_v, i_v, sems):
    moves = [
        pltpu.make_async_copy(src, dst, sems.at[i])
        for i, (src, dst) in enumerate(
            ((stream, s_v), (gain, g_v), (head, h_v), (reward, r_v), (segment, i_v))
        )
    ]
    for m in moves:
        m.start()
    for m in moves:
        m.wait()

    def parts(v):
        high = v.astype(bf16).astype(f32)
        mid = (v - high).astype(bf16).astype(f32)
        return high, mid, v - high - mid

    out[0:128] = s_v[...]
    rows = parts(g_v[...] * h_v[...])
    rows += (jnp.concatenate([*parts(r_v[...]), i_v[...].astype(f32)], 1),)
    line = lax.broadcasted_iota(jnp.int32, (16, 512), 0)
    extra = jnp.zeros((16, 512), f32)
    for i, a in enumerate(rows):
        extra = jnp.where(line == i, jnp.broadcast_to(a, (16, 512)), extra)
    out[128:144] = extra.astype(bf16)


def pick_body(own, other, out, sums, owed):
    x, _, y, _ = place()

    @pl.when(lax.rem(x, 2) == y // 2)
    def _():
        out[0:128] = own[0:128]

    @pl.when(lax.rem(x, 2) != y // 2)
    def _():
        out[0:128] = other[0:128]

    mine, theirs = own[128:144].astype(f32), other[128:144].astype(f32)
    even = lax.rem(x, 2) == 0
    first = jnp.where(even, mine, theirs)
    second = jnp.where(even, theirs, mine)
    for i, a in enumerate((first[3:4], second[3:4])):
        owed[i : i + 1] = a[:, 0:128] + a[:, 128:256] + a[:, 256:384]
        owed[2 + i : 3 + i] = a[:, 384:512]
    owed[4:8] = jnp.zeros((4, 128), f32)
    out[128:144] = mine.astype(bf16)
    gw = gains_of(own)

    def total(a):
        a = sum(a[:, 128 * i : 128 * i + 128] for i in range(8))
        return jnp.sum(a.T, axis=0, keepdims=True)

    v = out[0:128].astype(f32)
    sums[0:1] = total(v * v)
    sums[1:2] = total(v * gw)
    sums[2:8] = jnp.zeros((6, 128), f32)


def gains_of(block):
    extra = block[128:144].astype(f32)
    return extra[0:1] + extra[1:2] + extra[2:3]


def coefs_body(here, there, bias, out, target):
    x, zlo, y, _ = place()

    def side(src, at):
        near, away = src[at : at + 2], src[24 + at : 26 + at]
        low, high = jnp.where(x // 2 == 0, near, away), jnp.where(x // 2 == 0, away, near)
        return jnp.concatenate([low, high], 0)

    def rows(at):
        mine, theirs = side(here, at), side(there, at)
        return jnp.where(zlo == 0, mine, theirs), jnp.where(zlo == 0, theirs, mine)

    value = jnp.concatenate([*rows(8), *rows(16)], 0)
    segment = jnp.concatenate([*rows(10), *rows(18)], 0)
    shape = value.shape
    line = lax.broadcasted_iota(jnp.int32, shape, 0) % 8
    lane = lax.broadcasted_iota(jnp.int32, shape, 1)

    def ahead(a, step):
        if step >= 128:
            return pltpu.roll(a, shape[0] - step // 128, 0)
        here = pltpu.roll(a, 128 - step, 1)
        below = pltpu.roll(here, shape[0] - 1, 0)
        return jnp.where(lane + step < 128, here, below)

    step = 1
    while step < 1024:
        inside = line * 128 + lane + step < 1024
        same = inside & (ahead(segment, step) == segment)
        value = value + jnp.where(same, ahead(value, step), 0.0)
        step *= 2
    mean = jnp.sum(value) / COUNT
    off = value - mean
    spread = jnp.sum(off * off) / COUNT
    target[...] = (off / jnp.sqrt(jnp.broadcast_to(spread, shape) + 1e-05))[:8]
    wanted, sq, lin = [], [], []
    for i in range(4):
        zl = zlo if i < 2 else 1 - zlo
        b = x // 2 if i % 2 == 0 else 1 - x // 2
        wanted.append(target[pl.ds(4 * zl + 2 * b + y // 2, 1)])
        src = (here, there)[i // 2]
        at = 24 * (i % 2)
        sq.append(src[at : at + 1])
        lin.append(src[at + 1 : at + 2])
    wanted, sq, lin = (jnp.concatenate(a, 0) for a in (wanted, sq, lin))
    rms = jnp.sqrt(sq / WIDTH + 1e-05)
    head = lin / rms
    dvalue = loss_scale * (head + bias[0] - wanted) / COUNT
    out[0:4] = dvalue / rms
    out[4:8] = head / WIDTH / rms


def columns(coefs):
    padded = jnp.concatenate([coefs, jnp.zeros((120, 128), f32)], 0).T
    lane = lax.broadcasted_iota(jnp.int32, (128, 128), 1)

    def column(at):
        return jnp.sum(jnp.where(lane == at, padded, 0.0), axis=1, keepdims=True)

    return column


def formed(block, s, l, gains):
    return (s * (gains - block.astype(f32) * l)).astype(bf16)


def own_grad_body(stream, block, coefs, coefs_mate, grad):
    x, _, y, _ = place()
    column = columns(jnp.where(lax.rem(x, 2) == y // 2, coefs[...], coefs_mate[...]))
    grad[...] = formed(stream[...], column(0), column(4), gains_of(block)[:, :512])


def grad_body(coefs, here, there, g_own, g_other):
    x, zlo, y, zhi = place()
    odd = lax.rem(y, 2)
    column = columns(coefs[...])
    gains = gains_of(here)
    for k, spots in enumerate(((192, 224), (128, 64), (0, 32), (96, 160))):
        z = lax.rem(zhi + k, 4)
        zl, b = z // 2, lax.rem(z, 2)
        at = jnp.where(zl == zlo, 0, 2) + jnp.where(b == x // 2, 0, 1)
        s_all, l_all = column(at), column(4 + at)
        s_all = jnp.where(odd == 0, s_all, jnp.concatenate([s_all[64:], s_all[:64]], 0))
        l_all = jnp.where(odd == 0, l_all, jnp.concatenate([l_all[64:], l_all[:64]], 0))
        start = jnp.where(b == x // 2, 0, 144)
        for same, src in ((True, here), (False, there)):

            @pl.when((zl == zlo) == same)
            def _(src=src, s_all=s_all, l_all=l_all, start=start, spots=spots):
                for who, out in ((0, g_own), (1, g_other)):
                    parity = odd if who == 0 else 1 - odd
                    first = pl.multiple_of(start + 64 * parity, 16)
                    rows = slice(64 * who, 64 * who + 64)
                    made = formed(src[pl.ds(first, 64)], s_all[rows], l_all[rows], gains)
                    for i, spot in enumerate(spots):
                        out[spot : spot + 32] = made[32 * i : 32 * i + 32]


LO = 1856
CHUNKS = ((0, 1024), (1024, 2048), (2048, 3072), (3072, 3696))
HIGH = 3696 - LO
SPANS = ((0, LO), (LO, 3696))
def inner_body(g, w, got, other, *refs):
    out, (w_v, m_v, sems) = refs[:4], refs[4:]
    p = lax.axis_index("dp")
    for i, (a, b) in enumerate(CHUNKS):
        pltpu.make_async_copy(w.at[a:b], w_v.at[a:b], sems.at[i]).start()

    def mate_copy(j, low, high):
        a, b = SPANS[j]
        src, off = (low, high)[j], (0, HIGH)[j]
        return pltpu.make_async_copy(src.at[a - off : b - off], m_v.at[a:b], sems.at[4 + j])

    @pl.when(p == 0)
    def _():
        for j in range(2):
            mate_copy(j, got, other).start()

    @pl.when(p == 1)
    def _():
        for j in range(2):
            mate_copy(j, other, got).start()

    left, right = g[:, :512], g[:, 512:]
    nt = (((1,), (1,)), ((), ()))
    waits = ((0,), (1,), (), ())
    for i, (a, b) in enumerate(CHUNKS):
        pltpu.make_async_copy(w.at[a:b], w_v.at[a:b], sems.at[i]).wait()
        for j in waits[i]:
            mate_copy(j, other, other).wait()
        for f in range(a, b, 512):
            e = min(f + 512, b)
            made = lax.dot_general(left, w_v[f:e], nt, preferred_element_type=f32)
            made = made + lax.dot_general(right, m_v[f:e], nt, preferred_element_type=f32)
            for n, o in enumerate(out):
                o[:, f:e] = made[64 * n : 64 * n + 64].astype(o.dtype)


def inner(g, w, got, other, dtype, name):
    hbm = pl.BlockSpec(memory_space=pl.ANY)
    return call(
        inner_body,
        [sds((64, 3696), dtype)] * 4,
        (g, w, got, other),
        in_specs=[pl.BlockSpec(memory_space=pltpu.VMEM)] + [hbm] * 3,
        scratch=[
            pltpu.VMEM((3696, 512), bf16),
            pltpu.VMEM((3696, 512), bf16),
            pltpu.SemaphoreType.DMA((6,)),
        ],
        flops=2 * 256 * 1024 * 3696,
        moved=10 << 20,
        name=name,
        grant=24,
    )


def outer_body(*refs, first, split):
    (far_a, far_b, up, down, here, y0, y12, y3), (g_own, g_other) = refs[:8], refs[8:10]
    *outs, h_v, g_v = refs[10:]
    p = lax.axis_index("dp")
    for at, src in (
        (0, far_a[...]),
        (32, far_b[...]),
        (64, up[32:64]),
        (96, down[0:32]),
        (128, up[0:32]),
        (160, down[32:64]),
        (192, here[...]),
        (256, y0[...]),
        (320, y12[0, 32:64]),
        (352, y12[1, 0:32]),
        (384, y12[0, 0:32]),
        (416, y12[1, 32:64]),
        (448, y3[...]),
    ):
        h_v[at : at + src.shape[0]] = src
    for n, side in enumerate((1 - p, p) if split else (0, 1)):
        start = pl.multiple_of(first + 256 * side, 256)
        g_v[:256, 256 * n : 256 * n + 256] = g_own[:, pl.ds(start, 256)]
        g_v[256:, 256 * n : 256 * n + 256] = g_other[:, pl.ds(start, 256)]
    for f in range(0, 3696, 512):
        e = min(f + 512, 3696)
        out = lax.dot_general(
            h_v[:, f:e], g_v[...], (((0,), (0,)), ((), ())), preferred_element_type=f32
        )
        if split:
            outs[0][f:e] = out[:, :256].astype(bf16)
            outs[1][f:e] = out[:, 256:]
        else:
            outs[0][f:e] = out


def outer(pieces, g_own, g_other, first, split, name):
    out = [sds((3696, 256), bf16), sds((3696, 256), f32)] if split else sds((3696, 512), f32)
    return call(
        functools.partial(outer_body, first=first, split=split),
        out,
        (*pieces, g_own, g_other),
        scratch=[pltpu.VMEM((512, 3696), bf16), pltpu.VMEM((512, 512), bf16)],
        flops=512 * 1024 * 3696,
        moved=8 << 20,
        name=name,
        grant=28,
    )


def fold_body(own, other, *refs):
    *more, first, second = refs
    total = own[...] + other[...].astype(f32)
    for i, out in enumerate((first, second)):
        part = total[32 * i : 32 * i + 32]
        if more:
            part = part + more[i][...].astype(f32)
        out[...] = part.astype(bf16)


def fold(own, other, *more):
    return call(fold_body, [sds((32, own.shape[1]), bf16)] * 2, (own, other, *more))


def here_body(own, other, pure_a, pure_b, mixed_a, mixed_b, out):
    total = own[...] + other[...].astype(f32)
    for at, (one, two) in ((0, (pure_a, mixed_a)), (32, (pure_b, mixed_b))):
        part = total[at : at + 32] + one[...].astype(f32) + two[...].astype(f32)
        out[at : at + 32] = part.astype(bf16)


def merge_body(partial, recv, out):
    p = lax.axis_index("dp")
    mine = pl.ds(pl.multiple_of(256 * p, 256), 256)
    rest = pl.ds(pl.multiple_of(256 * (1 - p), 256), 256)
    out[:, mine] = (partial[:, mine] + recv[...].astype(f32)).astype(bf16)
    out[:, rest] = partial[:, rest].astype(bf16)


def per_device(stream, hidden, w_down, norm_gain, value_head, value_bias, rewards, segments):
    p = lax.axis_index("dp")
    smem = pl.BlockSpec(memory_space=pltpu.SMEM)
    vmem = pl.BlockSpec(memory_space=pltpu.VMEM)
    hbm = pl.BlockSpec(memory_space=pl.ANY)

    payload = call(
        prep_body,
        sds((144, 512), bf16),
        (stream, norm_gain[None], value_head[None], rewards, segments),
        in_specs=[hbm] * 5,
        scratch=[
            pltpu.VMEM((128, 512), bf16),
            pltpu.VMEM((1, 512), f32),
            pltpu.VMEM((1, 512), f32),
            pltpu.VMEM((1, 128), f32),
            pltpu.VMEM((1, 128), jnp.int32),
            pltpu.SemaphoreType.DMA((5,)),
        ],
        grant=56,
    )
    payload_mate = col(payload, MATE, "payload_mate")
    y3 = col(after(hidden, payload_mate), PAIR, "y3")
    down = col(hidden, ZUP, "down")
    up = col(hidden, ZDOWN, "up")

    w_half = lax.dynamic_slice_in_dim(w_down, p * HIGH, LO, 0)
    got = col(after(w_half, payload_mate), MATE, "got")

    block = jnp.concatenate([payload, payload_mate], 1)
    near, sums, owed = call(
        pick_body,
        (sds((144, 1024), bf16), sds((8, 128), f32), sds((8, 128), f32)),
        (block, row(block, XONE, "block_x1")),
    )
    away = row(near, XTHREE, "block_x3")
    here = jnp.concatenate([near, away], 0)
    there = row(here, ZLO, "block_zlo")
    owed_other = core(owed, "owed_other")

    gates = ((y3,), (down, up), (away,))
    for i, perm in enumerate((PAIR, ZONE, ZTHREE)):
        sums = after(sums, *gates[i])
        sums = sums + col(sums, perm, f"sums{i}")
        if i == 0:
            down, up = lax.optimization_barrier((down, up, sums))[:2]
            far_a = col(down[:32], ZUP, "far_a")
            far_b = col(up[32:], ZDOWN, "far_b")
            y12 = col(jnp.stack([up, down]), PAIR, "y12")
    y0 = col(after(jnp.concatenate([far_a, far_b], 0), sums), PAIR, "y0")
    tiny = jnp.concatenate([sums, owed, owed_other], 0)
    tiny = after(tiny, far_a, far_b)
    tiny = jnp.concatenate([tiny, row(tiny, XTHREE, "tiny_x3")], 0)
    tiny_zlo = row(tiny, ZLO, "tiny_zlo")
    coefs = call(
        coefs_body,
        sds((8, 128), f32),
        (after(tiny, got), tiny_zlo, value_bias),
        in_specs=[vmem, vmem, smem],
        scratch=[pltpu.VMEM((8, 128), f32)],
    )
    got_other = core(after(got, tiny_zlo), "got_other")
    coefs_mate = col(coefs, MATE, "coefs_mate")
    g_own, g_other = call(
        grad_body,
        (sds((256, 1024), bf16), sds((256, 1024), bf16)),
        (coefs, here, there),
        moved=4 << 20,
    )

    pieces = (far_a, far_b, up, down, hidden, y0, y12, y3)
    mate_give, mate_keep = outer(pieces, after(g_own, coefs_mate), g_other, 512, True, "outer_mate")
    mate_got = core(mate_give, "mate_got")
    sent = inner(after(g_other, mate_keep), w_down, got, got_other, bf16, "inner_sent")
    own = inner(after(g_own, sent[0]), w_down, got, got_other, f32, "inner_own")
    t = [col(a, PAIR, f"t{i}") for i, a in enumerate(sent)]
    w_send = (after(mate_keep, sent[0]) + mate_got.astype(f32)).astype(bf16)
    w_recv = col(w_send, MATE, "w_recv")

    q0a, q0b = fold(own[0], after(t[0], w_send))
    from_down = col(q0a, ZUP, "from_down")
    from_up = col(q0b, ZDOWN, "from_up")
    stream_grad = call(
        own_grad_body, sds((128, 512), bf16), (after(stream, q0a), near, coefs, coefs_mate)
    )
    partial = outer(pieces, after(g_own, q0a), g_other, 0, False, "outer_own")
    q1b, q1a = fold(own[1], after(t[1], partial, from_up))
    pure_b = col(q1b, ZUP, "pure_b")
    pure_a = col(q1a, ZDOWN, "pure_a")
    q2a, q2b = fold(own[2], after(t[2], stream_grad), from_down, from_up)
    q2a, q2b, pure_a, pure_b = lax.optimization_barrier((q2a, q2b, pure_a, pure_b))
    mixed_a = col(q2a, ZUP, "mixed_a")
    mixed_b = col(q2b, ZDOWN, "mixed_b")
    part = call(
        merge_body, sds((3696, 512), bf16), (after(partial, q2a), w_recv)
    )
    part_other = core(part, "part")
    weight_grad = (part.astype(f32) + part_other.astype(f32)).astype(bf16)
    hidden_grad = call(
        here_body,
        sds((64, 3696), bf16),
        (after(own[3], weight_grad), t[3], pure_a, pure_b, mixed_a, mixed_b),
    )
    return weight_grad, hidden_grad, stream_grad


def solution(mesh):
    in_specs = (
        P(("dp", "row"), "col"),
        P(("dp", "col"), "row"),
        P("row", "col"),
        P("col"),
        P("col"),
        P(),
        P("dp", "row"),
        P("dp", "row"),
    )
    out_specs = (P("row", "col"), P(("dp", "col"), "row"), P(("dp", "row"), "col"))
    return jax.shard_map(
        per_device, mesh=mesh, in_specs=in_specs, out_specs=out_specs, check_vma=False
    )
```

```python
import functools

import jax
import jax.numpy as jnp
from jax import lax
from jax.experimental import pallas as pl
from jax.experimental.pallas import tpu as pltpu
from jax.sharding import PartitionSpec as P

loss_scale = 2097152.0
bf16, f32 = jnp.bfloat16, jnp.float32
WIDTH, COUNT = 8192.0, 2048.0

PAIR = [(c, c ^ 1) for c in range(16)]
MATE = [(c, c ^ 3) for c in range(16)]
ZUP = [(c, (c + 4) % 16) for c in range(16)]
ZDOWN = [(c, (c + 12) % 16) for c in range(16)]
ZONE = [(c, c ^ 4) for c in range(16)]
ZTHREE = [(c, c ^ 12) for c in range(16)]
ZLO = [(r, r ^ 4) for r in range(8)]
CORE = [(0, 1), (1, 0)]
XONE = [(r, r ^ 1) for r in range(8)]
XTHREE = [(r, r ^ 3) for r in range(8)]
MIB = 1024 * 1024


def send(a, axis, perm, name):
    with jax.named_scope(name):
        return lax.ppermute(a, axis, perm)


def col(a, perm, name):
    return send(a, "col", perm, name)


def row(a, perm, name):
    return send(a, "row", perm, name)


def core(a, name):
    return send(a, "dp", CORE, name)


def after(a, *others):
    return lax.optimization_barrier((a, *others))[0]


def sds(shape, dtype):
    return jax.ShapeDtypeStruct(shape, dtype)


def call(body, out_shape, args, in_specs=None, scratch=(), flops=0, moved=0, name=None, grant=16):
    extra = {} if in_specs is None else {"in_specs": in_specs}
    with jax.named_scope(name or getattr(body, "__name__", "mid")):
      return pl.pallas_call(
        body,
        out_shape=out_shape,
        scratch_shapes=list(scratch),
        compiler_params=pltpu.CompilerParams(vmem_limit_bytes=grant * MIB),
        cost_estimate=pl.CostEstimate(flops=flops, bytes_accessed=moved, transcendentals=0),
        **extra,
    )(*args)


def place():
    r, c = lax.axis_index("row"), lax.axis_index("col")
    return r % 4, r // 4, c % 4, c // 4


def prep_body(stream, gain, head, reward, segment, out, s_v, g_v, h_v, r_v, i_v, sems):
    moves = [
        pltpu.make_async_copy(src, dst, sems.at[i])
        for i, (src, dst) in enumerate(
            ((stream, s_v), (gain, g_v), (head, h_v), (reward, r_v), (segment, i_v))
        )
    ]
    for m in moves:
        m.start()
    for m in moves:
        m.wait()

    def parts(v):
        high = v.astype(bf16).astype(f32)
        mid = (v - high).astype(bf16).astype(f32)
        return high, mid, v - high - mid

    out[0:128] = s_v[...]
    rows = parts(g_v[...] * h_v[...])
    rows += (jnp.concatenate([*parts(r_v[...]), i_v[...].astype(f32)], 1),)
    line = lax.broadcasted_iota(jnp.int32, (16, 512), 0)
    extra = jnp.zeros((16, 512), f32)
    for i, a in enumerate(rows):
        extra = jnp.where(line == i, jnp.broadcast_to(a, (16, 512)), extra)
    out[128:144] = extra.astype(bf16)


def pick_body(own, other, out, sums, owed):
    x, _, y, _ = place()

    @pl.when(lax.rem(x, 2) == y // 2)
    def _():
        out[0:128] = own[0:128]

    @pl.when(lax.rem(x, 2) != y // 2)
    def _():
        out[0:128] = other[0:128]

    mine, theirs = own[128:144].astype(f32), other[128:144].astype(f32)
    even = lax.rem(x, 2) == 0
    first = jnp.where(even, mine, theirs)
    second = jnp.where(even, theirs, mine)
    for i, a in enumerate((first[3:4], second[3:4])):
        owed[i : i + 1] = a[:, 0:128] + a[:, 128:256] + a[:, 256:384]
        owed[2 + i : 3 + i] = a[:, 384:512]
    owed[4:8] = jnp.zeros((4, 128), f32)
    out[128:144] = mine.astype(bf16)
    gw = gains_of(own)

    def total(a):
        a = sum(a[:, 128 * i : 128 * i + 128] for i in range(8))
        return jnp.sum(a.T, axis=0, keepdims=True)

    v = out[0:128].astype(f32)
    sums[0:1] = total(v * v)
    sums[1:2] = total(v * gw)
    sums[2:8] = jnp.zeros((6, 128), f32)


def gains_of(block):
    extra = block[128:144].astype(f32)
    return extra[0:1] + extra[1:2] + extra[2:3]


def coefs_body(here, there, bias, out, target):
    x, zlo, y, _ = place()

    def side(src, at):
        near, away = src[at : at + 2], src[24 + at : 26 + at]
        low, high = jnp.where(x // 2 == 0, near, away), jnp.where(x // 2 == 0, away, near)
        return jnp.concatenate([low, high], 0)

    def rows(at):
        mine, theirs = side(here, at), side(there, at)
        return jnp.where(zlo == 0, mine, theirs), jnp.where(zlo == 0, theirs, mine)

    value = jnp.concatenate([*rows(8), *rows(16)], 0)
    segment = jnp.concatenate([*rows(10), *rows(18)], 0)
    shape = value.shape
    line = lax.broadcasted_iota(jnp.int32, shape, 0) % 8
    lane = lax.broadcasted_iota(jnp.int32, shape, 1)

    def ahead(a, step):
        if step >= 128:
            return pltpu.roll(a, shape[0] - step // 128, 0)
        here = pltpu.roll(a, 128 - step, 1)
        below = pltpu.roll(here, shape[0] - 1, 0)
        return jnp.where(lane + step < 128, here, below)

    step = 1
    while step < 1024:
        inside = line * 128 + lane + step < 1024
        same = inside & (ahead(segment, step) == segment)
        value = value + jnp.where(same, ahead(value, step), 0.0)
        step *= 2
    mean = jnp.sum(value) / COUNT
    off = value - mean
    spread = jnp.sum(off * off) / COUNT
    target[...] = (off / jnp.sqrt(jnp.broadcast_to(spread, shape) + 1e-05))[:8]
    wanted, sq, lin = [], [], []
    for i in range(4):
        zl = zlo if i < 2 else 1 - zlo
        b = x // 2 if i % 2 == 0 else 1 - x // 2
        wanted.append(target[pl.ds(4 * zl + 2 * b + y // 2, 1)])
        src = (here, there)[i // 2]
        at = 24 * (i % 2)
        sq.append(src[at : at + 1])
        lin.append(src[at + 1 : at + 2])
    wanted, sq, lin = (jnp.concatenate(a, 0) for a in (wanted, sq, lin))
    rms = jnp.sqrt(sq / WIDTH + 1e-05)
    head = lin / rms
    dvalue = loss_scale * (head + bias[0] - wanted) / COUNT
    out[0:4] = dvalue / rms
    out[4:8] = head / WIDTH / rms


def columns(coefs):
    padded = jnp.concatenate([coefs, jnp.zeros((120, 128), f32)], 0).T
    lane = lax.broadcasted_iota(jnp.int32, (128, 128), 1)

    def column(at):
        return jnp.sum(jnp.where(lane == at, padded, 0.0), axis=1, keepdims=True)

    return column


def formed(block, s, l, gains):
    return (s * (gains - block.astype(f32) * l)).astype(bf16)


def own_grad_body(stream, block, coefs, coefs_mate, grad):
    x, _, y, _ = place()
    column = columns(jnp.where(lax.rem(x, 2) == y // 2, coefs[...], coefs_mate[...]))
    grad[...] = formed(stream[...], column(0), column(4), gains_of(block)[:, :512])


def grad_body(coefs, here, there, g_own, g_other):
    x, zlo, y, zhi = place()
    odd = lax.rem(y, 2)
    column = columns(coefs[...])
    gains = gains_of(here)
    for k, spots in enumerate(((192, 224), (128, 64), (0, 32), (96, 160))):
        z = lax.rem(zhi + k, 4)
        zl, b = z // 2, lax.rem(z, 2)
        at = jnp.where(zl == zlo, 0, 2) + jnp.where(b == x // 2, 0, 1)
        s_all, l_all = column(at), column(4 + at)
        s_all = jnp.where(odd == 0, s_all, jnp.concatenate([s_all[64:], s_all[:64]], 0))
        l_all = jnp.where(odd == 0, l_all, jnp.concatenate([l_all[64:], l_all[:64]], 0))
        start = jnp.where(b == x // 2, 0, 144)
        for same, src in ((True, here), (False, there)):

            @pl.when((zl == zlo) == same)
            def _(src=src, s_all=s_all, l_all=l_all, start=start, spots=spots):
                for who, out in ((0, g_own), (1, g_other)):
                    parity = odd if who == 0 else 1 - odd
                    first = pl.multiple_of(start + 64 * parity, 16)
                    rows = slice(64 * who, 64 * who + 64)
                    made = formed(src[pl.ds(first, 64)], s_all[rows], l_all[rows], gains)
                    for i, spot in enumerate(spots):
                        out[spot : spot + 32] = made[32 * i : 32 * i + 32]


LO = 1856
CHUNKS = ((0, 512), (512, 1536), (1536, 2560), (2560, 3696))
HIGH = 3696 - LO
SPANS = ((0, 512), (512, LO), (LO, 2560), (2560, 3696))
def inner_body(g, w, got, other, *refs):
    out, (w_v, m_v, sems) = refs[:4], refs[4:]
    p = lax.axis_index("dp")
    for i, (a, b) in enumerate(CHUNKS):
        pltpu.make_async_copy(w.at[a:b], w_v.at[a:b], sems.at[i]).start()

    def mate_copy(j, low, high):
        a, b = SPANS[j]
        src, off = (low, low, high, high)[j], (0, 0, HIGH, HIGH)[j]
        return pltpu.make_async_copy(src.at[a - off : b - off], m_v.at[a:b], sems.at[4 + j])

    @pl.when(p == 0)
    def _():
        for j in range(4):
            mate_copy(j, got, other).start()

    @pl.when(p == 1)
    def _():
        for j in range(4):
            mate_copy(j, other, got).start()

    left, right = g[:, :512], g[:, 512:]
    nt = (((1,), (1,)), ((), ()))
    waits = ((0,), (1,), (2,), (3,))
    for i, (a, b) in enumerate(CHUNKS):
        pltpu.make_async_copy(w.at[a:b], w_v.at[a:b], sems.at[i]).wait()
        for j in waits[i]:
            mate_copy(j, other, other).wait()
        for f in range(a, b, 512):
            e = min(f + 512, b)
            made = lax.dot_general(left, w_v[f:e], nt, preferred_element_type=f32)
            made = made + lax.dot_general(right, m_v[f:e], nt, preferred_element_type=f32)
            for n, o in enumerate(out):
                o[:, f:e] = made[64 * n : 64 * n + 64].astype(o.dtype)


def inner(g, w, got, other, dtype, name):
    hbm = pl.BlockSpec(memory_space=pl.ANY)
    return call(
        inner_body,
        [sds((64, 3696), dtype)] * 4,
        (g, w, got, other),
        in_specs=[pl.BlockSpec(memory_space=pltpu.VMEM)] + [hbm] * 3,
        scratch=[
            pltpu.VMEM((3696, 512), bf16),
            pltpu.VMEM((3696, 512), bf16),
            pltpu.SemaphoreType.DMA((8,)),
        ],
        flops=2 * 256 * 1024 * 3696,
        moved=10 << 20,
        name=name,
        grant=24,
    )


def outer_body(*refs, first, split):
    (far_a, far_b, up, down, here, y0, y12, y3), (g_own, g_other) = refs[:8], refs[8:10]
    *outs, h_v, g_v = refs[10:]
    p = lax.axis_index("dp")
    for at, src in (
        (0, far_a[...]),
        (32, far_b[...]),
        (64, up[32:64]),
        (96, down[0:32]),
        (128, up[0:32]),
        (160, down[32:64]),
        (192, here[...]),
        (256, y0[...]),
        (320, y12[0, 32:64]),
        (352, y12[1, 0:32]),
        (384, y12[0, 0:32]),
        (416, y12[1, 32:64]),
        (448, y3[...]),
    ):
        h_v[at : at + src.shape[0]] = src
    for n, side in enumerate((1 - p, p) if split else (0, 1)):
        start = pl.multiple_of(first + 256 * side, 256)
        g_v[:256, 256 * n : 256 * n + 256] = g_own[:, pl.ds(start, 256)]
        g_v[256:, 256 * n : 256 * n + 256] = g_other[:, pl.ds(start, 256)]
    for f in range(0, 3696, 512):
        e = min(f + 512, 3696)
        out = lax.dot_general(
            h_v[:, f:e], g_v[...], (((0,), (0,)), ((), ())), preferred_element_type=f32
        )
        if split:
            outs[0][f:e] = out[:, :256].astype(bf16)
            outs[1][f:e] = out[:, 256:]
        else:
            outs[0][f:e] = out


def outer(pieces, g_own, g_other, first, split, name):
    out = [sds((3696, 256), bf16), sds((3696, 256), f32)] if split else sds((3696, 512), f32)
    return call(
        functools.partial(outer_body, first=first, split=split),
        out,
        (*pieces, g_own, g_other),
        scratch=[pltpu.VMEM((512, 3696), bf16), pltpu.VMEM((512, 512), bf16)],
        flops=512 * 1024 * 3696,
        moved=8 << 20,
        name=name,
        grant=28,
    )


def fold_body(own, other, *refs):
    *more, first, second = refs
    total = own[...] + other[...].astype(f32)
    for i, out in enumerate((first, second)):
        part = total[32 * i : 32 * i + 32]
        if more:
            part = part + more[i][...].astype(f32)
        out[...] = part.astype(bf16)


def fold(own, other, *more):
    return call(fold_body, [sds((32, own.shape[1]), bf16)] * 2, (own, other, *more))


def here_body(own, other, pure_a, pure_b, mixed_a, mixed_b, out):
    total = own[...] + other[...].astype(f32)
    for at, (one, two) in ((0, (pure_a, mixed_a)), (32, (pure_b, mixed_b))):
        part = total[at : at + 32] + one[...].astype(f32) + two[...].astype(f32)
        out[at : at + 32] = part.astype(bf16)


def merge_body(partial, recv, out):
    p = lax.axis_index("dp")
    mine = pl.ds(pl.multiple_of(256 * p, 256), 256)
    rest = pl.ds(pl.multiple_of(256 * (1 - p), 256), 256)
    out[:, mine] = (partial[:, mine] + recv[...].astype(f32)).astype(bf16)
    out[:, rest] = partial[:, rest].astype(bf16)


def per_device(stream, hidden, w_down, norm_gain, value_head, value_bias, rewards, segments):
    p = lax.axis_index("dp")
    smem = pl.BlockSpec(memory_space=pltpu.SMEM)
    vmem = pl.BlockSpec(memory_space=pltpu.VMEM)
    hbm = pl.BlockSpec(memory_space=pl.ANY)

    payload = call(
        prep_body,
        sds((144, 512), bf16),
        (stream, norm_gain[None], value_head[None], rewards, segments),
        in_specs=[hbm] * 5,
        scratch=[
            pltpu.VMEM((128, 512), bf16),
            pltpu.VMEM((1, 512), f32),
            pltpu.VMEM((1, 512), f32),
            pltpu.VMEM((1, 128), f32),
            pltpu.VMEM((1, 128), jnp.int32),
            pltpu.SemaphoreType.DMA((5,)),
        ],
        grant=56,
    )
    payload_mate = col(payload, MATE, "payload_mate")
    ready = after(hidden, payload)
    y3 = col(ready, PAIR, "y3")
    down = col(ready, ZUP, "down")
    up = col(ready, ZDOWN, "up")

    w_half = lax.dynamic_slice_in_dim(w_down, p * HIGH, LO, 0)
    got = col(after(w_half, payload_mate), MATE, "got")

    block = jnp.concatenate([payload, payload_mate], 1)
    near, sums, owed = call(
        pick_body,
        (sds((144, 1024), bf16), sds((8, 128), f32), sds((8, 128), f32)),
        (block, row(block, XONE, "block_x1")),
    )
    away = row(near, XTHREE, "block_x3")
    here = jnp.concatenate([near, away], 0)
    there = row(here, ZLO, "block_zlo")
    owed_other = core(owed, "owed_other")

    gates = ((y3,), (down, up), (away,))
    for i, perm in enumerate((PAIR, ZONE, ZTHREE)):
        sums = after(sums, *gates[i])
        sums = sums + col(sums, perm, f"sums{i}")
        if i == 0:
            down, up = lax.optimization_barrier((down, up, sums))[:2]
            far_a = col(down[:32], ZUP, "far_a")
            far_b = col(up[32:], ZDOWN, "far_b")
            y12 = col(jnp.stack([up, down]), PAIR, "y12")
    y0 = col(after(jnp.concatenate([far_a, far_b], 0), sums), PAIR, "y0")
    tiny = jnp.concatenate([sums, owed, owed_other], 0)
    tiny = after(tiny, far_a, far_b)
    tiny = jnp.concatenate([tiny, row(tiny, XTHREE, "tiny_x3")], 0)
    tiny_zlo = row(tiny, ZLO, "tiny_zlo")
    coefs = call(
        coefs_body,
        sds((8, 128), f32),
        (after(tiny, got), tiny_zlo, value_bias),
        in_specs=[vmem, vmem, smem],
        scratch=[pltpu.VMEM((8, 128), f32)],
    )
    got_other = core(after(got, tiny_zlo), "got_other")
    coefs_mate = col(coefs, MATE, "coefs_mate")
    g_own, g_other = call(
        grad_body,
        (sds((256, 1024), bf16), sds((256, 1024), bf16)),
        (coefs, here, there),
        moved=4 << 20,
    )

    pieces = (far_a, far_b, up, down, hidden, y0, y12, y3)
    mate_give, mate_keep = outer(pieces, after(g_own, coefs_mate), g_other, 512, True, "outer_mate")
    mate_got = core(mate_give, "mate_got")
    sent = inner(after(g_other, mate_keep), w_down, got, got_other, bf16, "inner_sent")
    own = inner(after(g_own, sent[0]), w_down, got, got_other, f32, "inner_own")
    t = [col(a, PAIR, f"t{i}") for i, a in enumerate(sent)]
    w_send = (after(mate_keep, sent[0]) + mate_got.astype(f32)).astype(bf16)
    w_recv = col(w_send, MATE, "w_recv")

    q0a, q0b = fold(own[0], after(t[0], w_send))
    from_down = col(q0a, ZUP, "from_down")
    from_up = col(q0b, ZDOWN, "from_up")
    stream_grad = call(
        own_grad_body, sds((128, 512), bf16), (after(stream, q0a), near, coefs, coefs_mate)
    )
    partial = outer(pieces, after(g_own, q0a), g_other, 0, False, "outer_own")
    q1b, q1a = fold(own[1], after(t[1], partial, from_up))
    pure_b = col(q1b, ZUP, "pure_b")
    pure_a = col(q1a, ZDOWN, "pure_a")
    q2a, q2b = fold(own[2], after(t[2], stream_grad), from_down, from_up)
    q2a, q2b, pure_a, pure_b = lax.optimization_barrier((q2a, q2b, pure_a, pure_b))
    mixed_a = col(q2a, ZUP, "mixed_a")
    mixed_b = col(q2b, ZDOWN, "mixed_b")
    part = call(
        merge_body, sds((3696, 512), bf16), (after(partial, q2a), w_recv)
    )
    part_other = core(part, "part")
    weight_grad = (part.astype(f32) + part_other.astype(f32)).astype(bf16)
    hidden_grad = call(
        here_body,
        sds((64, 3696), bf16),
        (after(own[3], weight_grad), t[3], pure_a, pure_b, mixed_a, mixed_b),
    )
    return weight_grad, hidden_grad, stream_grad


def solution(mesh):
    in_specs = (
        P(("dp", "row"), "col"),
        P(("dp", "col"), "row"),
        P("row", "col"),
        P("col"),
        P("col"),
        P(),
        P("dp", "row"),
        P("dp", "row"),
    )
    out_specs = (P("row", "col"), P(("dp", "col"), "row"), P(("dp", "row"), "col"))
    return jax.shard_map(
        per_device, mesh=mesh, in_specs=in_specs, out_specs=out_specs, check_vma=False
    )
```
